32 devices in a mesh: shard: 8 (over z, x), ctx: 2 (over y), tp: 2 (over core).
Axes of the slice: x: 2, y: 2, z: 4, core: 2. Of those that a mesh axis runs over, the one named last changes fastest.
Arguments:
- inputs: bfloat16 [16384, 1024], P(('shard', 'ctx')), may hold values from -6 to 6
- cotangent: bfloat16 [16384, 1024], P(('shard', 'ctx')), may hold values from -8 to 8
- w_qkv: float32 [3, 1024, 1024], P(None, 'shard', 'tp'), may hold values from -0.25 to 0.25
- m_qkv: float32 [3, 1024, 1024], P(None, 'shard', 'tp'), may hold values from -80 to 80
- v_qkv: float32 [3, 1024, 1024], P(None, 'shard', 'tp'), may hold values from 491.52 to 6553.6
- w_dense: float32 [1024, 1024], P('tp', 'shard'), may hold values from -0.75 to 0.75
- m_dense: float32 [1024, 1024], P('tp', 'shard'), may hold values from -28 to 28
- v_dense: float32 [1024, 1024], P('tp', 'shard'), may hold values from 49.152 to 655.36
- w_fc1: float32 [1024, 4096], P('shard', 'tp'), may hold values from -0.1875 to 0.1875
- m_fc1: float32 [1024, 4096], P('shard', 'tp'), may hold values from -28 to 28
- v_fc1: float32 [1024, 4096], P('shard', 'tp'), may hold values from 49.152 to 655.36
- w_fc2: float32 [4096, 1024], P('tp', 'shard'), may hold values from -0.09375 to 0.09375
- m_fc2: float32 [4096, 1024], P('tp', 'shard'), may hold values from -56 to 56
- v_fc2: float32 [4096, 1024], P('tp', 'shard'), may hold values from 196.608 to 2621.44
- vectors: float32 [13, 1024], P(None, 'shard'), may hold values from -0.9 to 1.6
- m_vectors: float32 [13, 1024], P(None, 'shard'), may hold values from -146.32365 to 146.32365
- v_vectors: float32 [13, 1024], P(None, 'shard'), may hold values from 49.152 to 78643.2
Outputs:
- outputs: bfloat16 [16384, 1024], P(('shard', 'ctx'))
- input_grad: float32 [16384, 1024], P(('shard', 'ctx'))
- first_qkv: float32 [3, 1024, 1024], P(None, 'shard', 'tp')
- second_qkv: float32 [3, 1024, 1024], P(None, 'shard', 'tp')
- new_qkv: float32 [3, 1024, 1024], P(None, 'shard', 'tp')
- first_dense: float32 [1024, 1024], P('tp', 'shard')
- second_dense: float32 [1024, 1024], P('tp', 'shard')
- new_dense: float32 [1024, 1024], P('tp', 'shard')
- first_fc1: float32 [1024, 4096], P('shard', 'tp')
- second_fc1: float32 [1024, 4096], P('shard', 'tp')
- new_fc1: float32 [1024, 4096], P('shard', 'tp')
- first_fc2: float32 [4096, 1024], P('tp', 'shard')
- second_fc2: float32 [4096, 1024], P('tp', 'shard')
- new_fc2: float32 [4096, 1024], P('tp', 'shard')
- first_vectors: float32 [13, 1024], P(None, 'shard')
- second_vectors: float32 [13, 1024], P(None, 'shard')
- new_vectors: float32 [13, 1024], P(None, 'shard')
The draws below stay inside these ranges and needn't reach their ends.
All inputs are finite; a program needn't handle non-finite values.
Results may differ from the reference program's by a relative error of at most 0.0045.
The reference program's roundings to bfloat16 on the way count: a program that leaves them out, or rounds other values in their place, can miss the bound.
Values may be sent and summed in bfloat16 or wider, within the bound.
No kernel may reach another device: no remote copies, remote signals or barrier semaphores. Data moves between devices by JAX's collectives and lax.ppermute only.
A program may use at most 192 MiB of HBM per device.

```python
import math
import jax
import jax.numpy as jnp
from jax import lax

D = 1024
HEADS = 16
HD = 64
ROT = 16
FF = 4096
STEP = 10
SEQ_LEN = 2048
TOKENS = 16384
NVEC = 13
BLOCK = 512
N_SHARD = 8


def row_factors():
    fc1_rows = FF // D
    return jnp.concatenate([jnp.full((3,), 2.0, jnp.float32), jnp.full((1,), 1.0, jnp.float32), jnp.full((fc1_rows,), 0.1, jnp.float32), jnp.full((1,), 1.0, jnp.float32), jnp.array([12.0, 12.0, 0.4, 0.4], jnp.float32)])


def draw_vectors(key, part):
    key = jax.random.fold_in(key, 11)
    fc1_rows = FF // D
    noise = jnp.clip(jax.random.normal(key, (NVEC, D), jnp.float32), -3.0, 3.0)
    gain_rows = jnp.zeros((NVEC,), jnp.float32).at[5 + fc1_rows].set(1.0).at[7 + fc1_rows].set(1.0)
    scale = 0.3 - 0.1 * gain_rows
    return gain_rows[:, None] + scale[:, None] * noise


def draw_m_vectors(key, part):
    key = jax.random.fold_in(key, 12)
    noise = jnp.clip(jax.random.normal(key, (NVEC, D), jnp.float32), -3.0, 3.0)
    return noise * 0.11 * jnp.sqrt(row_factors() * TOKENS)[:, None]


def draw_v_vectors(key, part):
    key = jax.random.fold_in(key, 13)
    level = jax.random.uniform(key, (NVEC, D), jnp.float32)
    return (row_factors() * TOKENS)[:, None] * 0.03 * jnp.exp(level * jnp.log(0.4 / 0.03))


def raised(values, rng, source, target, blocks, factor):
    owner, partner = [(jnp.arange(values.shape[position]) // (values.shape[position] // blocks)).reshape([-1 if axis == position else 1 for axis in range(values.ndim)]) for position in (source, target)]
    chosen = jax.random.permutation(rng, blocks)[partner]
    strong = (owner == chosen) | (owner == (partner + blocks // 2) % blocks)
    return jnp.where(strong, factor * values, values)


def level_of(key, shape, cuts, low, top_value):
    level, own = 1.0, jax.random.fold_in(key, 6)
    for axis_at, blocks in cuts:
        steps = jnp.exp(jax.random.uniform(jax.random.fold_in(own, axis_at), (blocks,), jnp.float32, low / len(cuts), top_value / len(cuts)))
        level = level * jnp.repeat(steps, shape[axis_at] // blocks).reshape([-1 if axis == axis_at else 1 for axis in range(len(shape))])
    return level


def scatter_about(rng, extent, scale, reach, split=(), kind=jnp.bfloat16):
    values = scale * jax.random.normal(rng, extent, jnp.float32)
    if split:
        values = values * level_of(rng, extent, split, -0.22, 0.18)
    return jnp.clip(values, -reach, reach).astype(kind)


def heavy_noise(own_key, dims, scale, most, cuts, heavy, held_as=jnp.bfloat16):
    values = scale * jax.random.normal(own_key, dims, jnp.float32)
    if cuts:
        values = values * level_of(own_key, dims, cuts, -0.22, 0.18)
    return jnp.clip(raised(values, jax.random.fold_in(own_key, 3), *heavy), -most, most).astype(held_as)


def setup_inputs(seed: int = 0) -> dict:
    seeds = jax.random.split(jax.random.key(seed), 18)
    return {
        "inputs": scatter_about(seeds[0], (TOKENS, D), 1.0, 6.0, ((0, 16),)),
        "cotangent": heavy_noise(seeds[1], (TOKENS, D), 1.0, 8.0, ((0, 16),), (0, 1, 16, 2.0)),
        "w_qkv": scatter_about(seeds[2], (3, D, D), (D // 2) ** -0.5, 0.25, ((1, 8), (2, 2)), jnp.float32),
        "m_qkv": scatter_about(seeds[3], (3, D, D), (0.11 * TOKENS ** 0.5), 80.0, ((1, 8), (2, 2)), jnp.float32),
        "v_qkv": jnp.clip(jnp.exp(math.log(6553.6) - 2.5902672 * jax.random.uniform(seeds[4], (3, D, D), jnp.float32) ** level_of(seeds[4], (3, D, D), ((1, 8), (2, 2)), -0.2, 0.2)), 491.52, 6553.6),
        "w_dense": scatter_about(seeds[5], (D, D), (D // 16) ** -0.5, 0.75, ((0, 2), (1, 8)), jnp.float32),
        "m_dense": scatter_about(seeds[6], (D, D), (0.035 * TOKENS ** 0.5), 28.0, ((0, 2), (1, 8)), jnp.float32),
        "v_dense": jnp.clip(jnp.exp(math.log(655.36) - 2.5902671 * jax.random.uniform(seeds[7], (D, D), jnp.float32) ** level_of(seeds[7], (D, D), ((0, 2), (1, 8)), -0.2, 0.2)), 49.152, 655.36),
        "w_fc1": scatter_about(seeds[8], (D, FF), D ** -0.5, 0.1875, ((0, 8), (1, 2)), jnp.float32),
        "m_fc1": scatter_about(seeds[9], (D, FF), (0.035 * TOKENS ** 0.5), 28.0, ((0, 8), (1, 2)), jnp.float32),
        "v_fc1": jnp.clip(jnp.exp(math.log(655.36) - 2.5902671 * jax.random.uniform(seeds[10], (D, FF), jnp.float32) ** level_of(seeds[10], (D, FF), ((0, 8), (1, 2)), -0.2, 0.2)), 49.152, 655.36),
        "w_fc2": scatter_about(seeds[11], (FF, D), FF ** -0.5, 0.09375, ((0, 2), (1, 8)), jnp.float32),
        "m_fc2": scatter_about(seeds[12], (FF, D), (0.07 * TOKENS ** 0.5), 56.0, ((0, 2), (1, 8)), jnp.float32),
        "v_fc2": jnp.clip(jnp.exp(math.log(2621.44) - 2.5902671 * jax.random.uniform(seeds[13], (FF, D), jnp.float32) ** level_of(seeds[13], (FF, D), ((0, 2), (1, 8)), -0.2, 0.2)), 196.608, 2621.44),
        "vectors": draw_vectors(jax.random.fold_in(seeds[17], 71), 0),
        "m_vectors": draw_m_vectors(jax.random.fold_in(seeds[17], 71), 0),
        "v_vectors": draw_v_vectors(jax.random.fold_in(seeds[17], 71), 0),
    }


norm_eps = 1e-05
rope_base = 10000.0
masked_score = -1e+30
beta_one = 0.9
beta_two = 0.95
adam_eps = 1e-08
rate_matrix = 0.05
rate_vector = 0.5
weight_decay = 0.01
highest = lax.Precision.HIGHEST

@jax.custom_vjp
def low(v):
    return lax.optimization_barrier(v.astype(jnp.bfloat16)).astype(jnp.float32)

@jax.custom_vjp
def low_back(v):
    return v

def low_keep(v):
    return (low(v), None)

def low_pass(kept, grad):
    return (grad,)

def back_keep(v):
    return (v, None)

def back_low(kept, grad):
    return (low(grad),)
low.defvjp(low_keep, low_pass)
low_back.defvjp(back_keep, back_low)

def both_ways(value):
    return low(low_back(value))

def layer_norm(value, gain, shift):
    centre = value - lax.optimization_barrier(jnp.mean(value, axis=-1, keepdims=True))
    spread = lax.optimization_barrier(jnp.mean(centre * centre, axis=-1, keepdims=True))
    return centre * lax.rsqrt(spread + norm_eps) * gain + shift

def rope_tables(length):
    half = ROT // 2
    frequency = rope_base ** (-(jnp.arange(half, dtype=jnp.float32) * 2.0) / ROT)
    angle = jnp.arange(length, dtype=jnp.float32)[:, None] * frequency[None, :]
    return (jnp.cos(angle), jnp.sin(angle))

def rotate(value, cosine, sine):
    half = cosine.shape[1]
    first = value[..., :half]
    second = value[..., half:2 * half]
    cos_part = cosine[:, None, :]
    sin_part = sine[:, None, :]
    return jnp.concatenate([first * cos_part - second * sin_part, second * cos_part + first * sin_part, value[..., 2 * half:]], axis=-1)

def layer(params, tokens):
    w_qkv, w_dense, w_fc1, w_fc2, vectors = [low(weight) for weight in params]
    fc1_rows = FF // D
    bias_qkv = vectors[0:3]
    bias_dense = vectors[3]
    bias_fc1 = vectors[4:4 + fc1_rows].reshape(FF)
    bias_fc2 = vectors[4 + fc1_rows]
    gain_one = vectors[5 + fc1_rows]
    shift_one = vectors[6 + fc1_rows]
    gain_two = vectors[7 + fc1_rows]
    shift_two = vectors[8 + fc1_rows]
    normed_one = low(layer_norm(tokens, gain_one, shift_one))
    normed_two = low(layer_norm(tokens, gain_two, shift_two))
    projected = both_ways(jnp.einsum('td,kde->tke', normed_one, w_qkv, precision=highest) + bias_qkv[None])
    heads = projected.reshape(SEQ_LEN, 3, HEADS, HD)
    cosine, sine = rope_tables(SEQ_LEN)
    query_rot = low(rotate(heads[:, 0], cosine, sine))
    key_rot = low(rotate(heads[:, 1], cosine, sine))
    value = heads[:, 2]
    scale = HD ** (-0.5)

    def attend_block(start):
        query_block = lax.dynamic_slice_in_dim(query_rot, start, BLOCK, 0)
        raw = jnp.einsum('qhd,khd->hqk', query_block, key_rot, precision=highest)
        scores = low_back(raw * scale)
        rows = start + jnp.arange(BLOCK, dtype=jnp.int32)
        columns = jnp.arange(SEQ_LEN, dtype=jnp.int32)
        scores = jnp.where(columns[None, None, :] <= rows[None, :, None], scores, masked_score)
        top = lax.optimization_barrier(jnp.max(scores, axis=-1, keepdims=True))
        exponent = jnp.exp(scores - top)
        shares = low(exponent / lax.optimization_barrier(jnp.sum(exponent, axis=-1, keepdims=True)))
        return jnp.einsum('hqk,khd->qhd', shares, value, precision=highest)
    starts = jnp.arange(SEQ_LEN // BLOCK, dtype=jnp.int32) * BLOCK
    attended = both_ways(lax.map(jax.checkpoint(attend_block), starts).reshape(SEQ_LEN, D))
    hidden = low_back(jnp.dot(normed_two, w_fc1, precision=highest) + bias_fc1)
    activated = low(jax.nn.gelu(hidden, approximate=False))
    attn_out = jnp.dot(attended, w_dense, precision=highest) + bias_dense
    mlp_out = jnp.dot(activated, w_fc2, precision=highest) + bias_fc2
    return tokens + attn_out + mlp_out

def adam(weight, first, second, gradient, rate, decay):
    first_new = beta_one * first + (1.0 - beta_one) * gradient
    second_new = beta_two * second + (1.0 - beta_two) * gradient * gradient
    scaled = first_new / (1.0 - beta_one ** STEP) / (jnp.sqrt(second_new / (1.0 - beta_two ** STEP)) + adam_eps)
    return (first_new, second_new, weight - rate * (scaled + decay * weight))

def reference(inputs, cotangent, w_qkv, m_qkv, v_qkv, w_dense, m_dense, v_dense, w_fc1, m_fc1, v_fc1, w_fc2, m_fc2, v_fc2, vectors, m_vectors, v_vectors):
    params = (w_qkv, w_dense, w_fc1, w_fc2, vectors)
    seq_inputs = inputs.astype(jnp.float32).reshape(N_SHARD, SEQ_LEN, D)
    seq_back = cotangent.astype(jnp.float32).reshape(N_SHARD, SEQ_LEN, D)

    def per_sequence(totals, pair):
        tokens, back = pair
        result, pullback = jax.vjp(layer, params, tokens)
        param_grads, token_grad = pullback(back)
        totals = jax.tree.map(lambda accum, addend: accum + addend, totals, param_grads)
        return (totals, (result.astype(jnp.bfloat16), token_grad))
    zeros = jax.tree.map(jnp.zeros_like, params)
    grads, (outputs, token_grads) = lax.scan(per_sequence, zeros, (seq_inputs, seq_back))
    results = [outputs.reshape(TOKENS, D), token_grads.reshape(TOKENS, D)]
    states = ((m_qkv, v_qkv, rate_matrix, weight_decay), (m_dense, v_dense, rate_matrix, weight_decay), (m_fc1, v_fc1, rate_matrix, weight_decay), (m_fc2, v_fc2, rate_matrix, weight_decay), (m_vectors, v_vectors, rate_vector, 0.0))
    for weight, gradient, state in zip(params, grads, states):
        results.extend(adam(weight, state[0], state[1], gradient, state[2], state[3]))
    return tuple(results)
```

```python
import functools

import jax
import jax.numpy as jnp
from jax import lax
from jax.experimental import pallas as pl
from jax.experimental.pallas import tpu as pltpu
from jax.sharding import PartitionSpec as P

D = 1024
HD = 64
ROT = 16
FF = 4096
STEP = 10

norm_eps = 1e-05
rope_base = 10000.0
masked_score = -1e30
beta_one = 0.9
beta_two = 0.95
adam_eps = 1e-08
rate_matrix = 0.05
rate_vector = 0.5
weight_decay = 0.01

BQ = 512
BK = 512
UNIT_BLOCK = 256
VMEM = 56 * 1024 * 1024

bf16 = jnp.bfloat16
f32 = jnp.float32


def dot(a, b, contract):
    return lax.dot_general(a, b, (contract, ((), ())), preferred_element_type=f32)


NN = ((1,), (0,))
NT = ((1,), (1,))
TN = ((0,), (0,))


def swap(value, axis, mask):
    return lax.ppermute(value, axis, [(i, i ^ mask) for i in range(lax.axis_size(axis))])


def pick(value, index, axis):
    return lax.dynamic_index_in_dim(value, index, axis, keepdims=False)


def assemble(own, got, index, widths):
    _, rows, cols = own.shape

    def kernel(index_ref, own_ref, got_ref, *outs):
        for which, ref in enumerate((own_ref, got_ref)):
            for r in range(4):
                slot = index_ref[0] ^ ((r << 1) | which)
                start = 0
                for out, width in zip(outs, widths):
                    out[slot] = ref[r, :, start : start + width]
                    start += width

    vmem = pl.BlockSpec(memory_space=pltpu.VMEM)
    return pl.pallas_call(
        kernel,
        in_specs=[pl.BlockSpec(memory_space=pltpu.SMEM), vmem, vmem],
        out_specs=[vmem] * len(widths),
        out_shape=[jax.ShapeDtypeStruct((8, rows, width), bf16) for width in widths],
        compiler_params=pltpu.CompilerParams(vmem_limit_bytes=VMEM),
    )(index, own, got)


def turn(value, cosine, sine_up, sine_down, sign):
    up = pltpu.roll(value, value.shape[1] - ROT // 2, 1)
    down = pltpu.roll(value, ROT // 2, 1)
    return value * cosine + sign * (up * sine_up + down * sine_down)


def attend_kernel(
    ctx_ref, heads_ref, back_ref, cos_ref, up_ref, down_ref, heads_out, back_out,
    q_s, k_s, v_s, g_s, kt_s, vt_s, e_s, dp_s, dk_s, dv_s, dq_s, o_s, ot_s, dqt_s,
):
    step = pl.program_id(0)
    half = back_ref.shape[0] // 2
    lanes = back_ref.shape[1]
    ctx = ctx_ref[0]
    scale = HD ** (-0.5)

    @pl.when(step == 0)
    def _():
        dk_s[...] = jnp.zeros_like(dk_s)
        dv_s[...] = jnp.zeros_like(dv_s)
        for first, which in ((0, ctx), (half, 1 - ctx)):
            for at in range(0, half, BK):
                block = which * (half // BK) + at // BK
                rows = pl.ds(pl.multiple_of(block * BK, BK), BK)
                tables = (cos_ref[rows], up_ref[rows], down_ref[rows])
                here = slice(first + at, first + at + BK)
                query = turn(heads_ref[here, :lanes].astype(f32), *tables, 1.0).astype(bf16)
                q_s[rows] = (query.astype(f32) * scale).astype(bf16)
                key = turn(heads_ref[here, lanes : 2 * lanes].astype(f32), *tables, 1.0).astype(bf16)
                k_s[rows] = key
                kt_s[block] = key.astype(f32).T.astype(bf16)
                value = heads_ref[here, 2 * lanes :]
                v_s[rows] = value
                vt_s[block] = value.astype(f32).T.astype(bf16)
                g_s[rows] = back_ref[here]

    rows = pl.ds(pl.multiple_of(step * BQ, BQ), BQ)
    low_lanes = lax.broadcasted_iota(jnp.int32, (BQ, lanes), 1) < HD

    def both(value):
        value = value.astype(f32)
        return jnp.concatenate(
            [jnp.where(low_lanes, value, 0.0), jnp.where(low_lanes, 0.0, value)], axis=0
        ).astype(bf16)

    q_both = both(q_s[rows])
    g_both = both(g_s[rows])

    def keys_at(block):
        return pl.ds(pl.multiple_of(block * BK, BK), BK)

    def score(block):
        return dot(k_s[keys_at(block)], q_both, NT)

    key_row = lax.broadcasted_iota(jnp.int32, (BK, BQ), 0)
    query_col = lax.broadcasted_iota(jnp.int32, (BK, BQ), 1)
    keep = key_row <= query_col
    diagonal = score(step)
    diagonal = jnp.where(jnp.concatenate([keep, keep], axis=1), diagonal, masked_score)
    e_s[step] = diagonal
    top = jnp.max(diagonal, axis=0, keepdims=True)

    def first_pass(block, top):
        value = score(block)
        e_s[block] = value
        return jnp.maximum(top, jnp.max(value, axis=0, keepdims=True))

    top = lax.fori_loop(0, step, first_pass, top)

    def second_pass(block, carry):
        total, inner = carry
        exponent = jnp.exp(e_s[block] - top)
        d_shares = dot(v_s[keys_at(block)], g_both, NT)
        e_s[block] = exponent
        dp_s[block] = d_shares
        total = total + jnp.sum(exponent, axis=0, keepdims=True)
        inner = inner + jnp.sum(exponent * d_shares, axis=0, keepdims=True)
        return total, inner

    zero = jnp.zeros((1, 2 * BQ), f32)
    total, inner = lax.fori_loop(0, step + 1, second_pass, (zero, zero))
    inverse = 1.0 / total
    inner = inner * inverse
    ot_s[...] = jnp.zeros_like(ot_s)
    dqt_s[...] = jnp.zeros_like(dqt_s)

    def third_pass(block, carry):
        shares = e_s[block] * inverse
        low = shares.astype(bf16)
        d_scores = (shares * (dp_s[block] - inner)).astype(bf16)
        at = keys_at(block)
        dv_s[at] += dot(low, g_both, NN)
        dk_s[at] += dot(d_scores, q_both, NN)
        ot_s[...] += dot(vt_s[block], low, NN)
        dqt_s[...] += dot(kt_s[block], d_scores, NN)
        return carry

    lax.fori_loop(0, step + 1, third_pass, 0)

    def joined(ref):
        return jnp.concatenate([ref[:HD, :BQ], ref[HD:, BQ:]], axis=0).T

    o_s[rows] = joined(ot_s).astype(bf16)
    d_query = joined(dqt_s) * scale
    dq_s[rows] = turn(d_query, cos_ref[rows], up_ref[rows], down_ref[rows], -1.0).astype(bf16)

    @pl.when(step == pl.num_programs(0) - 1)
    def _():
        for first, which in ((0, ctx), (half, 1 - ctx)):
            for at in range(0, half, BK):
                here = slice(first + at, first + at + BK)
                rows = pl.ds(pl.multiple_of(which * half + at, BK), BK)
                tables = (cos_ref[rows], up_ref[rows], down_ref[rows])
                heads_out[here, :lanes] = dq_s[rows]
                heads_out[here, lanes : 2 * lanes] = turn(dk_s[rows], *tables, -1.0).astype(bf16)
                heads_out[here, 2 * lanes :] = dv_s[rows].astype(bf16)
                back_out[here] = o_s[rows]


def attend(ctx, heads, back, tables, pair):
    length = heads.shape[0]
    lanes = 2 * HD
    blocks = length // BK
    table = pl.BlockSpec((length, lanes), lambda i: (0, 0))
    return pl.pallas_call(
        attend_kernel,
        grid=(length // BQ,),
        in_specs=[
            pl.BlockSpec(memory_space=pltpu.SMEM),
            pl.BlockSpec((length, 3 * lanes), lambda i: (0, pair)),
            pl.BlockSpec((length, lanes), lambda i: (0, pair)),
            table,
            table,
            table,
        ],
        out_specs=[pl.BlockSpec((length, 3 * lanes), lambda i: (0, 0)), table],
        out_shape=[
            jax.ShapeDtypeStruct((length, 3 * lanes), bf16),
            jax.ShapeDtypeStruct((length, lanes), bf16),
        ],
        scratch_shapes=[pltpu.VMEM((length, lanes), bf16)] * 4
        + [pltpu.VMEM((blocks, lanes, BK), bf16)] * 2
        + [pltpu.VMEM((blocks, BK, 2 * BQ), f32)] * 2
        + [pltpu.VMEM((length, lanes), f32)] * 2
        + [pltpu.VMEM((length, lanes), bf16)] * 2
        + [pltpu.VMEM((lanes, 2 * BQ), f32)] * 2,
        compiler_params=pltpu.CompilerParams(vmem_limit_bytes=VMEM),
    )(ctx, heads, back, *tables)


def mlp_kernel(normed_ref, back_ref, up_ref, down_ref, bias_ref, act_ref, dh_ref, sum_ref):
    rows = normed_ref.shape[0]
    step = min(256, rows)
    total = jnp.zeros((1, up_ref.shape[1]), f32)
    for at in range(0, rows, step):
        here = slice(at, at + step)
        hidden = dot(normed_ref[here], up_ref[...], NN) + bias_ref[...]
        d_act = dot(back_ref[here], down_ref[...], NN)
        share = 0.5 * (1.0 + lax.erf(hidden * (0.5**0.5)))
        density = jnp.exp(-0.5 * hidden * hidden) * 0.3989422804014327
        act_ref[here] = (hidden * share).astype(bf16)
        d_hidden = (d_act * (share + hidden * density)).astype(bf16)
        dh_ref[here] = d_hidden
        total = total + jnp.sum(d_hidden.astype(f32), axis=0, keepdims=True)
    sum_ref[...] = total


def mlp(normed, back, up, down, bias):
    rows, width = normed.shape
    units = up.shape[1]
    whole = pl.BlockSpec((rows, width), lambda j: (0, 0))
    columns = pl.BlockSpec((width, UNIT_BLOCK), lambda j: (0, j))
    out = pl.BlockSpec((rows, UNIT_BLOCK), lambda j: (0, j))
    line = pl.BlockSpec((1, UNIT_BLOCK), lambda j: (0, j))
    return pl.pallas_call(
        mlp_kernel,
        grid=(units // UNIT_BLOCK,),
        in_specs=[whole, whole, columns, columns, line],
        out_specs=[out, out, line],
        out_shape=[
            jax.ShapeDtypeStruct((rows, units), bf16),
            jax.ShapeDtypeStruct((rows, units), bf16),
            jax.ShapeDtypeStruct((1, units), f32),
        ],
        compiler_params=pltpu.CompilerParams(vmem_limit_bytes=VMEM),
    )(normed, back, up, down, bias)


def grads_kernel(column_ref, first_ref, one_ref, second_ref, two_ref, kept_ref, sent_ref):
    value = jnp.concatenate(
        [dot(first_ref[...], one_ref[...], TN), dot(second_ref[...], two_ref[...], TN)], axis=1
    )
    rows = value.shape[0] // 2
    top, bottom = value[:rows], value[rows:]
    here = column_ref[0] == 0
    kept_ref[0] = jnp.where(here, top, bottom)
    sent_ref[0] = jnp.where(here, bottom, top).astype(bf16)


def grads(column, first, one, second, two):
    length, width = first.shape
    rows = width // 8
    cols = one.shape[1] + two.shape[1]
    left = pl.BlockSpec((length, 2 * rows), lambda i: (0, i))
    out = pl.BlockSpec((1, rows, cols), lambda i: (i, 0, 0))
    return pl.pallas_call(
        grads_kernel,
        grid=(4,),
        in_specs=[
            pl.BlockSpec(memory_space=pltpu.SMEM),
            left,
            pl.BlockSpec(one.shape, lambda i: (0, 0)),
            left,
            pl.BlockSpec(two.shape, lambda i: (0, 0)),
        ],
        out_specs=[out, out],
        out_shape=[
            jax.ShapeDtypeStruct((4, rows, cols), f32),
            jax.ShapeDtypeStruct((4, rows, cols), bf16),
        ],
        compiler_params=pltpu.CompilerParams(vmem_limit_bytes=VMEM),
    )(column, first, one, second, two)


def combine(line, kept, crossed):
    def kernel(line_ref, kept_ref, crossed_ref, own_ref, *outs):
        for r, out in zip((0, 2, 3, 1), (own_ref,) + outs):
            at = line_ref[0] ^ r
            out[...] = (kept_ref[at] + crossed_ref[at].astype(f32)).astype(out.dtype)

    vmem = pl.BlockSpec(memory_space=pltpu.VMEM)
    shape = kept.shape[1:]
    return pl.pallas_call(
        kernel,
        in_specs=[pl.BlockSpec(memory_space=pltpu.SMEM), vmem, vmem],
        out_specs=[vmem] * 4,
        out_shape=[jax.ShapeDtypeStruct(shape, f32)] + [jax.ShapeDtypeStruct(shape, bf16)] * 3,
        compiler_params=pltpu.CompilerParams(vmem_limit_bytes=VMEM),
    )(line, kept, crossed)


def finish_kernel(
    tp_ref, dh_a, dh_b, o_a, o_b, act_a, act_b, du_a, du_b, tok_ref,
    wh, wd, f1_a, f1_b, f2_a, f2_b, gain_ref, send_ref, keep_ref, norm_ref, line_ref,
):
    cut = dh_a.shape[1]
    lanes = o_a.shape[1]

    @pl.when(pl.program_id(0) == 0)
    def _():
        norm_ref[...] = jnp.zeros_like(norm_ref)
        line_ref[...] = jnp.zeros_like(line_ref)

    out = (
        dot(act_a[...], f2_a[...], NT)
        + dot(act_b[...], f2_b[...], NT)
        + dot(o_a[...], wd[:, :lanes], NT)
        + dot(o_b[...], wd[:, lanes:], NT)
    )
    one = dot(dh_a[...], wh[:, :cut], NT) + dot(dh_b[...], wh[:, cut:], NT)
    two = dot(du_a[...], f1_a[...], NT) + dot(du_b[...], f1_b[...], NT)
    tokens = tok_ref[...].astype(f32)
    centre = tokens - jnp.mean(tokens, axis=-1, keepdims=True)
    unit = centre * lax.rsqrt(jnp.mean(centre * centre, axis=-1, keepdims=True) + norm_eps)
    grad = one * gain_ref[0:1] + two * gain_ref[1:2]

    @pl.when(pl.program_id(0) < pl.num_programs(0) // 2)
    def _():
        send_ref[0] = out
        send_ref[1] = grad

    @pl.when(pl.program_id(0) >= pl.num_programs(0) // 2)
    def _():
        keep_ref[0] = out
        keep_ref[1] = grad

    for at, value in enumerate((one * unit, one, two * unit, two)):
        norm_ref[at : at + 1] += jnp.sum(value, axis=0, keepdims=True)
    line_ref[0:1, :cut] += jnp.sum(dh_a[...].astype(f32), axis=0, keepdims=True)
    line_ref[0:1, cut:] += jnp.sum(dh_b[...].astype(f32), axis=0, keepdims=True)


def finish(tp, rowwise, weights, gains, theirs):
    length, width = rowwise[-1].shape
    block = 256
    heads = weights[0].shape[1]
    steps = length // (2 * block)
    half = steps // 2
    start = steps if theirs else 0

    def row(i, tp_ref):
        side = jnp.where(i < half, 1 - tp_ref[0], tp_ref[0])
        return start + side * half + lax.rem(i, half)

    def by_rows(value):
        return pl.BlockSpec((block, value.shape[1]), lambda i, ref: (row(i, ref), 0))

    def fixed(shape):
        return pl.BlockSpec(shape, lambda i, ref: (0, 0))

    return pl.pallas_call(
        finish_kernel,
        grid_spec=pltpu.PrefetchScalarGridSpec(
            num_scalar_prefetch=1,
            grid=(steps,),
            in_specs=[by_rows(value) for value in rowwise]
            + [fixed(value.shape) for value in weights]
            + [fixed(gains.shape)],
            out_specs=[
                pl.BlockSpec((2, block, width), lambda i, ref: (0, jnp.minimum(i, half - 1), 0)),
                pl.BlockSpec((2, block, width), lambda i, ref: (0, jnp.maximum(i - half, 0), 0)),
                fixed((4, width)),
                fixed((1, heads)),
            ],
        ),
        out_shape=[
            jax.ShapeDtypeStruct((2, half * block, width), f32),
            jax.ShapeDtypeStruct((2, half * block, width), f32),
            jax.ShapeDtypeStruct((4, width), f32),
            jax.ShapeDtypeStruct((1, heads), f32),
        ],
        compiler_params=pltpu.CompilerParams(vmem_limit_bytes=VMEM),
    )(tp, *rowwise, *weights, gains)


def after(value, *others):
    return lax.optimization_barrier((value,) + others)[0]


def gather_chunk(payload, index, widths):
    line = [swap(payload, "shard", r << 1) for r in (2, 3, 1)]
    own = jnp.stack([payload, line[2], line[0], line[1]])
    got = swap(own, "shard", 1)
    full = assemble(own, got, index, widths)
    return own, got, [value.reshape(-1, value.shape[2]) for value in full]


def adam(weight, first, second, gradient, rate, decay):
    first_new = beta_one * first + (1.0 - beta_one) * gradient
    second_new = beta_two * second + (1.0 - beta_two) * gradient * gradient
    scaled = (
        first_new
        / (1.0 - beta_one**STEP)
        / (jnp.sqrt(second_new / (1.0 - beta_two**STEP)) + adam_eps)
    )
    return (first_new, second_new, weight - rate * (scaled + decay * weight))


def adam_store(weight, first, second, gradient, outs, at):
    for ref, value in zip(outs, adam(weight[at], first[at], second[at], gradient, rate_matrix, weight_decay)):
        ref[at] = value


def adam_heads_kernel(ctx_ref, *refs):
    sums, (wq, mq, vq, wd, md, vd), outs = refs[:-12], refs[-12:-6], refs[-6:]
    pairs = len(sums) // 2
    lanes = 2 * HD
    first = ctx_ref[0] == 0
    for pair in range(pairs):
        mine, other = sums[2 * pair : 2 * pair + 2]
        for plane in range(4):
            cols = slice(plane * lanes, (plane + 1) * lanes)
            left, right = mine[:, cols], other[:, cols]
            for group, total in enumerate((jnp.where(first, left, right), jnp.where(first, right, left))):
                start = (group * pairs + pair) * lanes
                place = slice(start, start + lanes)
                if plane < 3:
                    adam_store(wq, mq, vq, total, outs[:3], (plane, slice(None), place))
                else:
                    adam_store(wd, md, vd, total.T, outs[3:], (place, slice(None)))


def adam_fc_kernel(ctx_ref, *refs):
    sums, (w1, m1, v1, w2, m2, v2), outs = refs[:-12], refs[-12:-6], refs[-6:]
    chunks = len(sums) // 2
    cut = w1.shape[1] // (2 * chunks)
    tile = 128
    first = ctx_ref[0] == 0
    for chunk in range(chunks):
        mine, other = sums[2 * chunk : 2 * chunk + 2]
        for at in range(0, 2 * cut, tile):
            left, right = mine[:, at : at + tile], other[:, at : at + tile]
            for group, total in enumerate((jnp.where(first, left, right), jnp.where(first, right, left))):
                start = (group * chunks + chunk) * cut + at % cut
                place = slice(start, start + tile)
                if at < cut:
                    adam_store(w1, m1, v1, total, outs[:3], (slice(None), place))
                else:
                    adam_store(w2, m2, v2, total.T, outs[3:], (place, slice(None)))


def adam_matrices(kernel, ctx, sums, states):
    vmem = pl.BlockSpec(memory_space=pltpu.VMEM)
    return pl.pallas_call(
        kernel,
        in_specs=[pl.BlockSpec(memory_space=pltpu.SMEM)] + [vmem] * (len(sums) + 6),
        out_specs=[vmem] * 6,
        out_shape=[jax.ShapeDtypeStruct(value.shape, f32) for value in states],
        compiler_params=pltpu.CompilerParams(vmem_limit_bytes=VMEM),
    )(ctx, *sums, *states)


def rope_tables(length, lanes):
    half = ROT // 2
    frequency = rope_base ** (-(jnp.arange(half, dtype=f32) * 2.0) / ROT)
    angle = jnp.arange(length, dtype=f32)[:, None] * frequency[None, :]
    cosine, sine = jnp.cos(angle), jnp.sin(angle)
    rest = HD - ROT
    one, none, zero = jnp.ones((length, rest), f32), jnp.zeros((length, rest), f32), jnp.zeros_like(sine)
    tables = (
        jnp.concatenate([cosine, cosine, one], axis=1),
        jnp.concatenate([-sine, zero, none], axis=1),
        jnp.concatenate([zero, sine, none], axis=1),
    )
    return [jnp.tile(table, (1, lanes // HD)) for table in tables]


def body(
    inputs, cotangent, w_qkv, m_qkv, v_qkv, w_dense, m_dense, v_dense,
    w_fc1, m_fc1, v_fc1, w_fc2, m_fc2, v_fc2, vectors, m_vectors, v_vectors,
):
    shard = lax.axis_index("shard")
    ctx = lax.axis_index("ctx")
    tp = lax.axis_index("tp")
    shards = lax.axis_size("shard")
    tok_count, width = inputs.shape
    rows = w_qkv.shape[1]
    head_cols = w_qkv.shape[2]
    units = w_fc1.shape[1]
    lanes = 2 * HD
    pairs, chunks = head_cols // (2 * lanes), 2
    own_heads, own_units = head_cols // 2, units // 2
    cut = own_units // chunks
    fc1_rows = FF // D
    count = vectors.shape[0]
    custom = shards == 8
    ctx_ref = ctx.reshape(1).astype(jnp.int32)
    shard_ref = shard.reshape(1).astype(jnp.int32)

    tp_ref = tp.reshape(1).astype(jnp.int32)
    column_ref, line_ref = shard_ref % 2, shard_ref // 2

    def gather(payload, widths):
        if custom:
            return gather_chunk(payload, shard_ref, widths)
        full = lax.all_gather(payload, "shard", axis=0, tiled=True)
        cuts = [sum(widths[:at]) for at in range(len(widths) + 1)]
        return full, full, [full[:, a:b] for a, b in zip(cuts, cuts[1:])]

    def local_grads(one, two):
        if custom:
            return grads(column_ref, normed_one if one.shape[1] == 3 * lanes else normed_two, one, all_back, two)
        first = normed_one if one.shape[1] == 3 * lanes else normed_two
        both = jnp.concatenate([dot(first, one, TN), dot(all_back, two, TN)], axis=1).astype(bf16)
        return both, both

    def step_across(kept, sent):
        if custom:
            crossed = swap(sent, "shard", 1)
            return combine(line_ref, kept, crossed)
        total = lax.psum_scatter(sent, "shard", scatter_dimension=0, tiled=True).astype(f32)
        return [total]

    def step_along(parts):
        total = parts[0]
        for r, part in zip((2, 3, 1), parts[1:]):
            total = total + swap(part, "shard", r << 1).astype(f32)
        return total, swap(total, "ctx", 1)

    with jax.named_scope("tokens"):
        part = tok_count // 2
        fetched = []

        def partner(value):
            direct = swap(pick(value.reshape(2, part, width), tp, 0), "ctx", 1)
            other = swap(direct, "tp", 1)
            fetched.append(other)
            return jnp.concatenate(
                [
                    value,
                    jnp.where(tp == 0, direct, other),
                    jnp.where(tp == 0, other, direct),
                ],
                axis=0,
            )

        all_tokens = partner(inputs)
        all_back = partner(cotangent)

    with jax.named_scope("gather_params"):
        low_qkv = pick(w_qkv.reshape(3, rows, 2, pairs, lanes), ctx, 2).astype(bf16)
        low_qkv = jnp.transpose(low_qkv, (1, 2, 0, 3)).reshape(rows, pairs * 3 * lanes)
        low_dense = pick(w_dense.reshape(2, own_heads, rows), ctx, 0).astype(bf16).T
        low_fc1 = pick(w_fc1.reshape(rows, 2, own_units), ctx, 1).astype(bf16)
        low_fc2 = pick(w_fc2.reshape(2, own_units, rows), ctx, 0).astype(bf16).T
        low_vectors = jnp.pad(vectors.astype(bf16).T, ((0, 0), (0, 128 - count)))
        payload = jnp.concatenate([low_qkv, low_dense, low_vectors], axis=1)
        _, got, (full_qkv, full_dense, full_vectors) = gather(
            payload, (pairs * 3 * lanes, pairs * lanes, 128)
        )
        full_fc1, full_fc2, lines, arrived = [], [], [], []
        gates = [got] + fetched
        for chunk in range(chunks):
            cols = slice(chunk * cut, (chunk + 1) * cut)
            payload = after(jnp.concatenate([low_fc1[:, cols], low_fc2[:, cols]], axis=1), *gates)
            own, got, (up, down) = gather(payload, (cut, cut))
            full_fc1.append(up)
            full_fc2.append(down)
            lines.append(own)
            arrived.append(got)
            gates = [own]

    vec_rows = full_vectors[:, :count].T.astype(f32)
    bias_qkv = lax.dynamic_slice_in_dim(vec_rows[0:3], tp * head_cols + ctx * own_heads, own_heads, 1)
    bias_qkv = jnp.swapaxes(bias_qkv.reshape(3, pairs, lanes), 0, 1).reshape(1, -1)
    bias_dense = vec_rows[3]
    bias_fc1 = lax.dynamic_slice_in_dim(
        vec_rows[4 : 4 + fc1_rows].reshape(1, -1), tp * units + ctx * own_units, own_units, 1
    )
    bias_fc2 = vec_rows[4 + fc1_rows]
    gain_one = vec_rows[5 + fc1_rows]
    shift_one = vec_rows[6 + fc1_rows]
    gain_two = vec_rows[7 + fc1_rows]
    shift_two = vec_rows[8 + fc1_rows]

    with jax.named_scope("norm"):
        tokens = all_tokens.astype(f32)
        centre = tokens - jnp.mean(tokens, axis=-1, keepdims=True)
        inverse = lax.rsqrt(jnp.mean(centre * centre, axis=-1, keepdims=True) + norm_eps)
        unit = centre * inverse
        normed_one = (unit * gain_one + shift_one).astype(bf16)
        normed_two = (unit * gain_two + shift_two).astype(bf16)

    tables = rope_tables(2 * tok_count, lanes)
    with jax.named_scope("project"):
        heads = (dot(normed_one, full_qkv, NN) + bias_qkv).astype(bf16)
        heads_back = dot(all_back, full_dense, NN).astype(bf16)

    def run_mlp(chunk, *gates):
        with jax.named_scope("mlp"):
            return mlp(
                normed_two, all_back, full_fc1[chunk], after(full_fc2[chunk], *gates),
                bias_fc1[:, chunk * cut : (chunk + 1) * cut],
            )

    def run_heads(pair, *gates):
        with jax.named_scope("attend"):
            return attend(ctx_ref, heads, after(heads_back, *gates), tables, pair)

    def run_finish(theirs, *gates):
        with jax.named_scope("finish"):
            rowwise = [d_heads[0], d_heads[1], attended[0], attended[1]]
            rowwise += [act[0], act[1], d_hidden[0], d_hidden[1], all_tokens]
            weights = [full_qkv, full_dense] + full_fc1 + full_fc2
            gains = after(jnp.stack([gain_one, gain_two]), *gates)
            sent, kept, norm_sums, head_line = finish(tp_ref, rowwise, weights, gains, theirs)
            return kept + swap(sent, "tp", 1), norm_sums, head_line, sent

    d_heads, attended, act, d_hidden, lines_fc1 = [], [], [], [], []

    def keep_heads(results):
        d_heads.append(results[0])
        attended.append(results[1])

    def keep_mlp(results):
        act.append(results[0])
        d_hidden.append(results[1])
        lines_fc1.append(results[2])

    keep_heads(run_heads(0, lines[0]))
    with jax.named_scope("grad_heads"):
        kept_a, sent_a = local_grads(d_heads[0], attended[0])
    keep_mlp(run_mlp(0, sent_a, lines[1]))
    with jax.named_scope("grad_fc"):
        kept_0, sent_0 = local_grads(d_hidden[0], act[0])
    with jax.named_scope("sum_heads"):
        parts_a = step_across(kept_a, sent_a)
    keep_mlp(run_mlp(1, sent_0, *parts_a))
    with jax.named_scope("grad_fc"):
        kept_1, sent_1 = local_grads(d_hidden[1], act[1])
    with jax.named_scope("sum_fc"):
        parts_0 = step_across(kept_0, sent_0)
    with jax.named_scope("sum_heads"):
        sums_a = step_along(parts_a)
    keep_heads(run_heads(1, sent_1, *parts_0, sums_a[0]))
    with jax.named_scope("sum_fc"):
        parts_1 = step_across(kept_1, sent_1)
        sums_0 = step_along(parts_0)
    theirs_sum, norm_theirs, line_theirs, sent_tp = run_finish(True, *parts_1)
    with jax.named_scope("grad_heads"):
        kept_b, sent_b = local_grads(d_heads[1], after(attended[1], sent_tp, sums_0[0]))
    with jax.named_scope("finish"):
        low_theirs = theirs_sum.astype(bf16)
    mine_sum, norm_mine, line_mine, _ = run_finish(False, low_theirs, sent_b)
    with jax.named_scope("sum_heads"):
        parts_b = step_across(kept_b, sent_b)
    with jax.named_scope("sum_fc"):
        sums_1 = step_along(parts_1)
    with jax.named_scope("sum_heads"):
        sums_b = step_along(parts_b)

    with jax.named_scope("finish"):
        norm_rows = norm_theirs + norm_mine
        head_line = line_theirs + line_mine
        total = mine_sum + swap(low_theirs, "ctx", 1).astype(f32)
        out_sum, d_unit = total[0], total[1]

        def shared(value):
            other = swap(value, "tp", 1)
            return jnp.concatenate(
                [jnp.where(tp == 0, value, other), jnp.where(tp == 0, other, value)], axis=0
            )

        own_tokens = pick(inputs.reshape(2, part, width), tp, 0).astype(f32)
        own_back = pick(cotangent.reshape(2, part, width), tp, 0).astype(f32)
        outputs = shared((own_tokens + out_sum + bias_dense + bias_fc2).astype(bf16))
        centre = own_tokens - jnp.mean(own_tokens, axis=-1, keepdims=True)
        inverse = lax.rsqrt(jnp.mean(centre * centre, axis=-1, keepdims=True) + norm_eps)
        unit = centre * inverse
        mean_d = jnp.mean(d_unit, axis=-1, keepdims=True)
        mean_du = jnp.mean(d_unit * unit, axis=-1, keepdims=True)
        input_grad = shared(own_back + inverse * (d_unit - mean_d - unit * mean_du))

    with jax.named_scope("vector_grads"):
        bias_back = jnp.sum(own_back, axis=0)[None]
        head_rows = jnp.swapaxes(head_line.reshape(pairs, 3, lanes), 0, 1).reshape(3, own_heads)
        placed_heads = lax.dynamic_update_slice_in_dim(
            jnp.zeros((3, width), f32), head_rows, tp * head_cols + ctx * own_heads, 1
        )
        placed_fc1 = lax.dynamic_update_slice_in_dim(
            jnp.zeros((1, FF), f32),
            jnp.concatenate(lines_fc1, axis=1),
            tp * units + ctx * own_units,
            1,
        ).reshape(fc1_rows, width)
        vector_grads = jnp.concatenate(
            [placed_heads, bias_back, placed_fc1, bias_back, norm_rows], axis=0
        )
        if custom:
            for axis, mask in (("tp", 1), ("shard", 1), ("shard", 2), ("ctx", 1), ("shard", 4)):
                vector_grads = vector_grads + swap(vector_grads, axis, mask)
        else:
            vector_grads = lax.psum(vector_grads, ("shard", "ctx", "tp"))
        owned_vectors = lax.dynamic_slice_in_dim(vector_grads, shard * rows, rows, 1)

    results = [outputs, input_grad]
    heads_states = (w_qkv, m_qkv, v_qkv, w_dense, m_dense, v_dense)
    fc_states = (w_fc1, m_fc1, v_fc1, w_fc2, m_fc2, v_fc2)
    head_sums = [*sums_a, *sums_b]
    fc_sums = [*sums_0, *sums_1]
    with jax.named_scope("adam"):
        if custom:
            fc_results = adam_matrices(adam_fc_kernel, ctx_ref, fc_sums, fc_states)
            results += adam_matrices(adam_heads_kernel, ctx_ref, head_sums, heads_states)
            results += fc_results
        else:

            def by_ctx(sums):
                mine, other = jnp.stack(sums[0::2]), jnp.stack(sums[1::2])
                return jnp.stack([jnp.where(ctx == 0, mine, other), jnp.where(ctx == 0, other, mine)])

            owned = by_ctx(head_sums).reshape(2, pairs, rows, 4, lanes)
            owned = jnp.transpose(owned, (3, 2, 0, 1, 4)).reshape(4, rows, head_cols)
            owned_fc = by_ctx(fc_sums).reshape(2, chunks, rows, 2, cut)
            owned_fc = jnp.transpose(owned_fc, (3, 2, 0, 1, 4)).reshape(2, rows, units)
            for gradient, entry in (
                (owned[:3], heads_states[:3]),
                (owned[3].T, heads_states[3:]),
                (owned_fc[0], fc_states[:3]),
                (owned_fc[1].T, fc_states[3:]),
            ):
                results += adam(*entry, gradient, rate_matrix, weight_decay)
        results += adam(vectors, m_vectors, v_vectors, owned_vectors, rate_vector, 0.0)
    return tuple(results)


def solution(mesh):
    tokens = P(("shard", "ctx"), None)
    layouts = [P(None, "shard", "tp"), P("tp", "shard"), P("shard", "tp"), P("tp", "shard"), P(None, "shard")]
    params = tuple(layout for layout in layouts for _ in range(3))
    return jax.shard_map(
        body,
        mesh=mesh,
        in_specs=(tokens, tokens) + params,
        out_specs=(tokens, tokens) + params,
        check_vma=False,
    )
```

```python
import math

import jax
import jax.numpy as jnp
from jax import lax
from jax.experimental import pallas as pl
from jax.experimental.pallas import tpu as pltpu
from jax.sharding import PartitionSpec as P

D = 1024
HD = 64
ROT = 16
FF = 4096
STEP = 10

norm_eps = 1e-05
rope_base = 10000.0
masked_score = -1e30
beta_one = 0.9
beta_two = 0.95
adam_eps = 1e-08
rate_matrix = 0.05
rate_vector = 0.5
weight_decay = 0.01

BQ = 512
BK = 512
UNIT_BLOCK = 256
VMEM = 56 * 1024 * 1024

bf16 = jnp.bfloat16
f32 = jnp.float32


def dot(a, b, contract):
    return lax.dot_general(a, b, (contract, ((), ())), preferred_element_type=f32)


NN = ((1,), (0,))
NT = ((1,), (1,))
TN = ((0,), (0,))


def cost(flops, moved):
    return pl.CostEstimate(flops=int(flops), bytes_accessed=int(moved), transcendentals=0)


def swap(value, axis, mask):
    return lax.ppermute(value, axis, [(i, i ^ mask) for i in range(lax.axis_size(axis))])


def pick(value, index, axis):
    return lax.dynamic_index_in_dim(value, index, axis, keepdims=False)


def assemble(own, got, index, widths):
    _, rows, cols = own.shape

    def kernel(index_ref, own_ref, got_ref, *outs):
        for which, ref in enumerate((own_ref, got_ref)):
            for r in range(4):
                slot = index_ref[0] ^ ((r << 1) | which)
                start = 0
                for out, width in zip(outs, widths):
                    out[slot] = ref[r, :, start : start + width]
                    start += width

    vmem = pl.BlockSpec(memory_space=pltpu.VMEM)
    return pl.pallas_call(
        kernel,
        in_specs=[pl.BlockSpec(memory_space=pltpu.SMEM), vmem, vmem],
        out_specs=[vmem] * len(widths),
        out_shape=[jax.ShapeDtypeStruct((8, rows, width), bf16) for width in widths],
        cost_estimate=cost(0, 32 * rows * cols),
        compiler_params=pltpu.CompilerParams(vmem_limit_bytes=VMEM),
    )(index, own, got)


def turn(value, cosine, sine_up, sine_down, sign):
    up = pltpu.roll(value, value.shape[1] - ROT // 2, 1)
    down = pltpu.roll(value, ROT // 2, 1)
    return value * cosine + sign * (up * sine_up + down * sine_down)


def attend_kernel(
    ctx_ref, heads_ref, back_ref, cos_ref, up_ref, down_ref, heads_out, back_out,
    q_s, k_s, v_s, g_s, kt_s, vt_s, e_s, dp_s, dk_s, dv_s, dq_s, o_s, ot_s, dqt_s,
):
    step = pl.program_id(0)
    half = back_ref.shape[0] // 2
    lanes = back_ref.shape[1]
    ctx = ctx_ref[0]
    scale = HD ** (-0.5)

    @pl.when(step == 0)
    def _():
        dk_s[...] = jnp.zeros_like(dk_s)
        dv_s[...] = jnp.zeros_like(dv_s)
        for first, which in ((0, ctx), (half, 1 - ctx)):
            for at in range(0, half, BK):
                block = which * (half // BK) + at // BK
                rows = pl.ds(pl.multiple_of(block * BK, BK), BK)
                tables = (cos_ref[rows], up_ref[rows], down_ref[rows])
                here = slice(first + at, first + at + BK)
                query = turn(heads_ref[here, :lanes].astype(f32), *tables, 1.0).astype(bf16)
                q_s[rows] = (query.astype(f32) * scale).astype(bf16)
                key = turn(heads_ref[here, lanes : 2 * lanes].astype(f32), *tables, 1.0).astype(bf16)
                k_s[rows] = key
                kt_s[block] = key.astype(f32).T.astype(bf16)
                value = heads_ref[here, 2 * lanes :]
                v_s[rows] = value
                vt_s[block] = value.astype(f32).T.astype(bf16)
                g_s[rows] = back_ref[here]

    rows = pl.ds(pl.multiple_of(step * BQ, BQ), BQ)
    low_lanes = lax.broadcasted_iota(jnp.int32, (BQ, lanes), 1) < HD

    def both(value):
        value = value.astype(f32)
        return jnp.concatenate(
            [jnp.where(low_lanes, value, 0.0), jnp.where(low_lanes, 0.0, value)], axis=0
        ).astype(bf16)

    q_both = both(q_s[rows])
    g_both = both(g_s[rows])

    def keys_at(block):
        return pl.ds(pl.multiple_of(block * BK, BK), BK)

    def score(block):
        return dot(k_s[keys_at(block)], q_both, NT)

    key_row = lax.broadcasted_iota(jnp.int32, (BK, BQ), 0)
    query_col = lax.broadcasted_iota(jnp.int32, (BK, BQ), 1)
    keep = key_row <= query_col
    diagonal = score(step)
    diagonal = jnp.where(jnp.concatenate([keep, keep], axis=1), diagonal, masked_score)
    e_s[step] = diagonal
    top = jnp.max(diagonal, axis=0, keepdims=True)

    def first_pass(block, top):
        value = score(block)
        e_s[block] = value
        return jnp.maximum(top, jnp.max(value, axis=0, keepdims=True))

    top = lax.fori_loop(0, step, first_pass, top)

    def second_pass(block, carry):
        total, inner = carry
        exponent = jnp.exp(e_s[block] - top)
        d_shares = dot(v_s[keys_at(block)], g_both, NT)
        e_s[block] = exponent
        dp_s[block] = d_shares
        total = total + jnp.sum(exponent, axis=0, keepdims=True)
        inner = inner + jnp.sum(exponent * d_shares, axis=0, keepdims=True)
        return total, inner

    zero = jnp.zeros((1, 2 * BQ), f32)
    total, inner = lax.fori_loop(0, step + 1, second_pass, (zero, zero))
    inverse = 1.0 / total
    inner = inner * inverse
    ot_s[...] = jnp.zeros_like(ot_s)
    dqt_s[...] = jnp.zeros_like(dqt_s)

    def third_pass(block, carry):
        shares = e_s[block] * inverse
        low = shares.astype(bf16)
        d_scores = (shares * (dp_s[block] - inner)).astype(bf16)
        at = keys_at(block)
        dv_s[at] += dot(low, g_both, NN)
        dk_s[at] += dot(d_scores, q_both, NN)
        ot_s[...] += dot(vt_s[block], low, NN)
        dqt_s[...] += dot(kt_s[block], d_scores, NN)
        return carry

    lax.fori_loop(0, step + 1, third_pass, 0)

    def joined(ref):
        return jnp.concatenate([ref[:HD, :BQ], ref[HD:, BQ:]], axis=0).T

    o_s[rows] = joined(ot_s).astype(bf16)
    d_query = joined(dqt_s) * scale
    dq_s[rows] = turn(d_query, cos_ref[rows], up_ref[rows], down_ref[rows], -1.0).astype(bf16)

    @pl.when(step == pl.num_programs(0) - 1)
    def _():
        for first, which in ((0, ctx), (half, 1 - ctx)):
            for at in range(0, half, BK):
                here = slice(first + at, first + at + BK)
                rows = pl.ds(pl.multiple_of(which * half + at, BK), BK)
                tables = (cos_ref[rows], up_ref[rows], down_ref[rows])
                heads_out[here, :lanes] = dq_s[rows]
                heads_out[here, lanes : 2 * lanes] = turn(dk_s[rows], *tables, -1.0).astype(bf16)
                heads_out[here, 2 * lanes :] = dv_s[rows].astype(bf16)
                back_out[here] = o_s[rows]


def attend(ctx, heads, back, tables, pair):
    length = heads.shape[0]
    lanes = 2 * HD
    blocks = length // BK
    table = pl.BlockSpec((length, lanes), lambda i: (0, 0))
    return pl.pallas_call(
        attend_kernel,
        grid=(length // BQ,),
        in_specs=[
            pl.BlockSpec(memory_space=pltpu.SMEM),
            pl.BlockSpec((length, 3 * lanes), lambda i: (0, pair)),
            pl.BlockSpec((length, lanes), lambda i: (0, pair)),
            table,
            table,
            table,
        ],
        out_specs=[pl.BlockSpec((length, 3 * lanes), lambda i: (0, 0)), table],
        out_shape=[
            jax.ShapeDtypeStruct((length, 3 * lanes), bf16),
            jax.ShapeDtypeStruct((length, lanes), bf16),
        ],
        scratch_shapes=[pltpu.VMEM((length, lanes), bf16)] * 4
        + [pltpu.VMEM((blocks, lanes, BK), bf16)] * 2
        + [pltpu.VMEM((blocks, BK, 2 * BQ), f32)] * 2
        + [pltpu.VMEM((length, lanes), f32)] * 2
        + [pltpu.VMEM((length, lanes), bf16)] * 2
        + [pltpu.VMEM((lanes, 2 * BQ), f32)] * 2,
        cost_estimate=cost(6 * 4 * length * length * lanes * 2, 16 * length * lanes),
        compiler_params=pltpu.CompilerParams(vmem_limit_bytes=VMEM),
    )(ctx, heads, back, *tables)


def mlp_kernel(normed_ref, back_ref, up_ref, down_ref, bias_ref, act_ref, dh_ref, sum_ref):
    rows = normed_ref.shape[0]
    step = min(256, rows)
    total = jnp.zeros((1, up_ref.shape[1]), f32)
    for at in range(0, rows, step):
        here = slice(at, at + step)
        hidden = dot(normed_ref[here], up_ref[...], NN) + bias_ref[...]
        d_act = dot(back_ref[here], down_ref[...], NN)
        share = 0.5 * (1.0 + lax.erf(hidden * (0.5**0.5)))
        density = jnp.exp(-0.5 * hidden * hidden) * 0.3989422804014327
        act_ref[here] = (hidden * share).astype(bf16)
        d_hidden = (d_act * (share + hidden * density)).astype(bf16)
        dh_ref[here] = d_hidden
        total = total + jnp.sum(d_hidden.astype(f32), axis=0, keepdims=True)
    sum_ref[...] = total


def mlp(normed, back, up, down, bias):
    rows, width = normed.shape
    units = up.shape[1]
    whole = pl.BlockSpec((rows, width), lambda j: (0, 0))
    columns = pl.BlockSpec((width, UNIT_BLOCK), lambda j: (0, j))
    out = pl.BlockSpec((rows, UNIT_BLOCK), lambda j: (0, j))
    line = pl.BlockSpec((1, UNIT_BLOCK), lambda j: (0, j))
    return pl.pallas_call(
        mlp_kernel,
        grid=(units // UNIT_BLOCK,),
        in_specs=[whole, whole, columns, columns, line],
        out_specs=[out, out, line],
        out_shape=[
            jax.ShapeDtypeStruct((rows, units), bf16),
            jax.ShapeDtypeStruct((rows, units), bf16),
            jax.ShapeDtypeStruct((1, units), f32),
        ],
        cost_estimate=cost(12 * rows * width * units, 8 * rows * width),
        compiler_params=pltpu.CompilerParams(vmem_limit_bytes=VMEM),
    )(normed, back, up, down, bias)


def grads_kernel(column_ref, first_ref, second_ref, *refs):
    rights, (kept_ref, sent_ref) = refs[:-2], refs[-2:]
    parts = [dot((first_ref, second_ref)[at % 2][...], ref[...], TN) for at, ref in enumerate(rights)]
    value = jnp.concatenate(parts, axis=1)
    rows = value.shape[0] // 2
    top, bottom = value[:rows], value[rows:]
    here = column_ref[0] == 0
    kept_ref[0] = jnp.where(here, top, bottom)
    sent_ref[0] = jnp.where(here, bottom, top).astype(bf16)


def grads(column, first, second, rights):
    length, width = first.shape
    rows = width // 8
    cols = sum(right.shape[1] for right in rights)
    left = pl.BlockSpec((length, 2 * rows), lambda i: (0, i))
    out = pl.BlockSpec((1, rows, cols), lambda i: (i, 0, 0))
    return pl.pallas_call(
        grads_kernel,
        grid=(4,),
        in_specs=[pl.BlockSpec(memory_space=pltpu.SMEM), left, left]
        + [pl.BlockSpec(right.shape, lambda i: (0, 0)) for right in rights],
        out_specs=[out, out],
        out_shape=[
            jax.ShapeDtypeStruct((4, rows, cols), f32),
            jax.ShapeDtypeStruct((4, rows, cols), bf16),
        ],
        cost_estimate=cost(0, 6 * width * cols),
        compiler_params=pltpu.CompilerParams(vmem_limit_bytes=VMEM),
    )(column, first, second, *rights)


def combine(line, kept, crossed):
    def kernel(line_ref, kept_ref, crossed_ref, own_ref, *outs):
        for r, out in zip((0, 2, 3, 1), (own_ref,) + outs):
            at = line_ref[0] ^ r
            out[...] = (kept_ref[at] + crossed_ref[at].astype(f32)).astype(out.dtype)

    vmem = pl.BlockSpec(memory_space=pltpu.VMEM)
    shape = kept.shape[1:]
    return pl.pallas_call(
        kernel,
        in_specs=[pl.BlockSpec(memory_space=pltpu.SMEM), vmem, vmem],
        out_specs=[vmem] * 4,
        out_shape=[jax.ShapeDtypeStruct(shape, f32)] + [jax.ShapeDtypeStruct(shape, bf16)] * 3,
        cost_estimate=cost(0, 12 * math.prod(kept.shape)),
        compiler_params=pltpu.CompilerParams(vmem_limit_bytes=VMEM),
    )(line, kept, crossed)


def finish_kernel(
    tp_ref, dh_a, dh_b, o_a, o_b, act_a, act_b, du_a, du_b, tok_ref,
    wh, wd, f1_a, f1_b, f2_a, f2_b, gain_ref, out_ref, norm_ref, line_ref,
):
    cut = dh_a.shape[1]
    lanes = o_a.shape[1]

    @pl.when(pl.program_id(0) == 0)
    def _():
        norm_ref[...] = jnp.zeros_like(norm_ref)
        line_ref[...] = jnp.zeros_like(line_ref)

    out_ref[0] = (
        dot(act_a[...], f2_a[...], NT)
        + dot(act_b[...], f2_b[...], NT)
        + dot(o_a[...], wd[:, :lanes], NT)
        + dot(o_b[...], wd[:, lanes:], NT)
    ).astype(out_ref.dtype)
    one = dot(dh_a[...], wh[:, :cut], NT) + dot(dh_b[...], wh[:, cut:], NT)
    two = dot(du_a[...], f1_a[...], NT) + dot(du_b[...], f1_b[...], NT)
    out_ref[1] = (one * gain_ref[0:1] + two * gain_ref[1:2]).astype(out_ref.dtype)
    tokens = tok_ref[...].astype(f32)
    centre = tokens - jnp.mean(tokens, axis=-1, keepdims=True)
    unit = centre * lax.rsqrt(jnp.mean(centre * centre, axis=-1, keepdims=True) + norm_eps)
    for at, value in enumerate((one * unit, one, two * unit, two)):
        norm_ref[at : at + 1] += jnp.sum(value, axis=0, keepdims=True)
    line_ref[0:1, :cut] += jnp.sum(dh_a[...].astype(f32), axis=0, keepdims=True)
    line_ref[0:1, cut:] += jnp.sum(dh_b[...].astype(f32), axis=0, keepdims=True)


def finish(tp, rowwise, weights, gains, theirs, keep):
    length, width = rowwise[-1].shape
    block = min(256, length // 8)
    heads = weights[0].shape[1]
    steps = length // (4 * block)
    start = 2 * steps if theirs else 0
    kind = f32 if keep else bf16

    def row(i, tp_ref):
        side = tp_ref[0] if keep else 1 - tp_ref[0]
        return start + side * steps + i

    def by_rows(value):
        return pl.BlockSpec((block, value.shape[1]), lambda i, ref: (row(i, ref), 0))

    def fixed(shape):
        return pl.BlockSpec(shape, lambda i, ref: (0, 0))

    out = pl.BlockSpec((2, block, width), lambda i, ref: (0, i, 0))
    return pl.pallas_call(
        finish_kernel,
        grid_spec=pltpu.PrefetchScalarGridSpec(
            num_scalar_prefetch=1,
            grid=(steps,),
            in_specs=[by_rows(value) for value in rowwise]
            + [fixed(value.shape) for value in weights]
            + [fixed(gains.shape)],
            out_specs=[out, fixed((4, width)), fixed((1, heads))],
        ),
        out_shape=[
            jax.ShapeDtypeStruct((2, steps * block, width), kind),
            jax.ShapeDtypeStruct((4, width), f32),
            jax.ShapeDtypeStruct((1, heads), f32),
        ],
        cost_estimate=cost((6 if keep else 0) * length * width * sum(w.shape[1] for w in weights), 4 * length * width),
        compiler_params=pltpu.CompilerParams(vmem_limit_bytes=VMEM),
    )(tp, *rowwise, *weights, gains)


def share_kernel(tp_ref, own_a, other_a, own_b, other_b, out_a, out_b):
    own = pl.program_id(0) // (pl.num_programs(0) // 2) == tp_ref[0]

    @pl.when(own)
    def _():
        out_a[...] = own_a[...]
        out_b[...] = own_b[...]

    @pl.when(jnp.logical_not(own))
    def _():
        out_a[...] = other_a[...]
        out_b[...] = other_b[...]


def share(tp, own, other):
    half, width = own[0].shape
    block = min(128, half)
    steps = half // block

    def at_own(i, ref):
        return (jnp.clip(i - ref[0] * steps, 0, steps - 1), 0)

    def at_other(i, ref):
        return (jnp.clip(i - (1 - ref[0]) * steps, 0, steps - 1), 0)

    own_spec, other_spec = pl.BlockSpec((block, width), at_own), pl.BlockSpec((block, width), at_other)
    out = pl.BlockSpec((block, width), lambda i, ref: (i, 0))
    return pl.pallas_call(
        share_kernel,
        grid_spec=pltpu.PrefetchScalarGridSpec(
            num_scalar_prefetch=1,
            grid=(2 * steps,),
            in_specs=[own_spec, other_spec, own_spec, other_spec],
            out_specs=[out, out],
        ),
        out_shape=[jax.ShapeDtypeStruct((2 * half, width), value.dtype) for value in own],
        cost_estimate=cost(0, 12 * half * width),
    )(tp, own[0], other[0], own[1], other[1])


def after(value, *others):
    return lax.optimization_barrier((value,) + others)[0] if others else value


def gather_chunk(payload, index, widths):
    line = [swap(payload, "shard", r << 1) for r in (2, 3, 1)]

    def cross(*gates):
        own = jnp.stack([after(payload, *gates), line[2], line[0], line[1]])
        got = swap(own, "shard", 1)

        def build(*gates):
            full = assemble(after(own, *gates), got, index, widths)
            return [value.reshape(-1, value.shape[2]) for value in full]

        return own, build

    return cross


def adam(weight, first, second, gradient, rate, decay):
    first_new = beta_one * first + (1.0 - beta_one) * gradient
    second_new = beta_two * second + (1.0 - beta_two) * gradient * gradient
    scaled = (
        first_new
        / (1.0 - beta_one**STEP)
        / (jnp.sqrt(second_new / (1.0 - beta_two**STEP)) + adam_eps)
    )
    return (first_new, second_new, weight - rate * (scaled + decay * weight))


def adam_store(weight, first, second, gradient, outs, at):
    for ref, value in zip(outs, adam(weight[at], first[at], second[at], gradient, rate_matrix, weight_decay)):
        ref[at] = value


def adam_heads_kernel(ctx_ref, *refs):
    sums, (wq, mq, vq, wd, md, vd), outs = refs[:-12], refs[-12:-6], refs[-6:]
    mine, other = sums
    lanes = 2 * HD
    pairs = mine.shape[1] // (4 * lanes)
    first = ctx_ref[0] == 0
    for pair in range(pairs):
        for plane in range(4):
            cols = slice((4 * pair + plane) * lanes, (4 * pair + plane + 1) * lanes)
            left, right = mine[:, cols].astype(f32), other[:, cols].astype(f32)
            for group, total in enumerate((jnp.where(first, left, right), jnp.where(first, right, left))):
                start = (group * pairs + pair) * lanes
                place = slice(start, start + lanes)
                if plane < 3:
                    adam_store(wq, mq, vq, total, outs[:3], (plane, slice(None), place))
                else:
                    adam_store(wd, md, vd, total.T, outs[3:], (place, slice(None)))


def adam_fc_kernel(ctx_ref, *refs):
    sums, (w1, m1, v1, w2, m2, v2), outs = refs[:-12], refs[-12:-6], refs[-6:]
    chunks = len(sums) // 2
    cut = w1.shape[1] // (2 * chunks)
    tile = 128
    first = ctx_ref[0] == 0
    for chunk in range(chunks):
        mine, other = sums[2 * chunk : 2 * chunk + 2]
        for at in range(0, 2 * cut, tile):
            left, right = mine[:, at : at + tile].astype(f32), other[:, at : at + tile].astype(f32)
            for group, total in enumerate((jnp.where(first, left, right), jnp.where(first, right, left))):
                start = (group * chunks + chunk) * cut + at % cut
                place = slice(start, start + tile)
                if at < cut:
                    adam_store(w1, m1, v1, total, outs[:3], (slice(None), place))
                else:
                    adam_store(w2, m2, v2, total.T, outs[3:], (place, slice(None)))


def adam_matrices(kernel, ctx, sums, states):
    vmem = pl.BlockSpec(memory_space=pltpu.VMEM)
    return pl.pallas_call(
        kernel,
        in_specs=[pl.BlockSpec(memory_space=pltpu.SMEM)] + [vmem] * (len(sums) + 6),
        out_specs=[vmem] * 6,
        out_shape=[jax.ShapeDtypeStruct(value.shape, f32) for value in states],
        cost_estimate=cost(0, 28 * sum(math.prod(v.shape) for v in states)),
        compiler_params=pltpu.CompilerParams(vmem_limit_bytes=VMEM),
    )(ctx, *sums, *states)


def rope_tables(length, lanes):
    half = ROT // 2
    lane = jnp.arange(lanes, dtype=jnp.int32) % HD
    frequency = rope_base ** (-((lane % half).astype(f32) * 2.0) / ROT)
    angle = jnp.arange(length, dtype=f32)[:, None] * frequency[None, :]
    cosine, sine = jnp.cos(angle), jnp.sin(angle)
    return [
        jnp.where(lane < ROT, cosine, 1.0),
        jnp.where(lane < half, -sine, 0.0),
        jnp.where((lane >= half) & (lane < ROT), sine, 0.0),
    ]


def body(
    inputs, cotangent, w_qkv, m_qkv, v_qkv, w_dense, m_dense, v_dense,
    w_fc1, m_fc1, v_fc1, w_fc2, m_fc2, v_fc2, vectors, m_vectors, v_vectors,
):
    shard = lax.axis_index("shard")
    ctx = lax.axis_index("ctx")
    tp = lax.axis_index("tp")
    shards = lax.axis_size("shard")
    tok_count, width = inputs.shape
    rows = w_qkv.shape[1]
    head_cols = w_qkv.shape[2]
    units = w_fc1.shape[1]
    lanes = 2 * HD
    pairs, chunks = head_cols // (2 * lanes), 2
    own_heads, own_units = head_cols // 2, units // 2
    cut = own_units // chunks
    fc1_rows = FF // D
    count = vectors.shape[0]
    custom = shards == 8
    ctx_ref = ctx.reshape(1).astype(jnp.int32)
    shard_ref = shard.reshape(1).astype(jnp.int32)

    tp_ref = tp.reshape(1).astype(jnp.int32)
    column_ref, line_ref = shard_ref % 2, shard_ref // 2

    def gather(payload, widths):
        if custom:
            return gather_chunk(payload, shard_ref, widths)
        full = lax.all_gather(payload, "shard", axis=0, tiled=True)
        cuts = [sum(widths[:at]) for at in range(len(widths) + 1)]
        return lambda *gates: (full, lambda *gates: [full[:, a:b] for a, b in zip(cuts, cuts[1:])])

    def local_grads(first, rights):
        if custom:
            return grads(column_ref, first, all_back, rights)
        parts = [dot((first, all_back)[at % 2], right, TN) for at, right in enumerate(rights)]
        both = jnp.concatenate(parts, axis=1).astype(bf16)
        return both, both

    def step_across(kept, sent):
        if custom:
            crossed = swap(sent, "shard", 1)
            return combine(line_ref, kept, crossed)
        total = lax.psum_scatter(sent, "shard", scatter_dimension=0, tiled=True).astype(f32)
        return [total]

    def step_along(parts):
        total = parts[0]
        for r, part in zip((2, 3, 1), parts[1:]):
            total = total + swap(part, "shard", r << 1).astype(f32)
        return total

    def exchange_owned(totals, *gates):
        low = after(jnp.concatenate([value.astype(bf16) for value in totals], axis=1), *gates)
        other = swap(low, "ctx", 1)
        cols = totals[0].shape[1]
        return [
            (low[:, at * cols : (at + 1) * cols], other[:, at * cols : (at + 1) * cols])
            for at in range(len(totals))
        ]

    with jax.named_scope("tokens"):
        part = tok_count // 2
        halves = [pick(value.reshape(2, part, width), tp, 0) for value in (inputs, cotangent)]
        direct = [swap(halves[0], "ctx", 1)]
        direct.append(swap(after(halves[1], direct[0]), "ctx", 1))
        shared_rows = [swap(value, "tp", 1) for value in direct]

        def whole_sequence(value, at):
            mine, other = direct[at], shared_rows[at]
            return jnp.concatenate(
                [value, jnp.where(tp == 0, mine, other), jnp.where(tp == 0, other, mine)], axis=0
            )

        all_tokens = whole_sequence(inputs, 0)
        all_back = whole_sequence(cotangent, 1)

    with jax.named_scope("gather_params"):
        low_qkv = pick(w_qkv.reshape(3, rows, 2, pairs, lanes), ctx, 2).astype(bf16)
        low_qkv = jnp.transpose(low_qkv, (1, 2, 0, 3)).reshape(rows, pairs * 3 * lanes)
        low_dense = pick(w_dense.reshape(2, own_heads, rows), ctx, 0).astype(bf16).T
        low_fc1 = pick(w_fc1.reshape(rows, 2, own_units), ctx, 1).astype(bf16)
        low_fc2 = pick(w_fc2.reshape(2, own_units, rows), ctx, 0).astype(bf16).T
        low_vectors = jnp.pad(vectors.astype(bf16).T, ((0, 0), (0, 128 - count)))
        payload = jnp.concatenate([low_qkv, low_dense, low_vectors], axis=1)
        own, build = gather(payload, (pairs * 3 * lanes, pairs * lanes, 128))()
        full_qkv, full_dense, full_vectors = build()
        payloads = [
            jnp.concatenate([low_fc1[:, c * cut : (c + 1) * cut], low_fc2[:, c * cut : (c + 1) * cut]], axis=1)
            for c in range(chunks)
        ]
        cross_0 = gather(after(payloads[0], own), (cut, cut))

    vec_rows = full_vectors[:, :count].T.astype(f32)
    bias_qkv = lax.dynamic_slice_in_dim(vec_rows[0:3], tp * head_cols + ctx * own_heads, own_heads, 1)
    bias_qkv = jnp.swapaxes(bias_qkv.reshape(3, pairs, lanes), 0, 1).reshape(1, -1)
    bias_dense = vec_rows[3]
    bias_fc1 = lax.dynamic_slice_in_dim(
        vec_rows[4 : 4 + fc1_rows].reshape(1, -1), tp * units + ctx * own_units, own_units, 1
    )
    bias_fc2 = vec_rows[4 + fc1_rows]
    gain_one = vec_rows[5 + fc1_rows]
    shift_one = vec_rows[6 + fc1_rows]
    gain_two = vec_rows[7 + fc1_rows]
    shift_two = vec_rows[8 + fc1_rows]

    with jax.named_scope("norm"):
        tokens = all_tokens.astype(f32)
        centre = tokens - jnp.mean(tokens, axis=-1, keepdims=True)
        inverse = lax.rsqrt(jnp.mean(centre * centre, axis=-1, keepdims=True) + norm_eps)
        unit = centre * inverse
        normed_one = (unit * gain_one + shift_one).astype(bf16)
        normed_two = (unit * gain_two + shift_two).astype(bf16)

    tables = rope_tables(2 * tok_count, lanes)
    with jax.named_scope("project"):
        heads = (dot(normed_one, full_qkv, NN) + bias_qkv).astype(bf16)
        heads_back = dot(all_back, full_dense, NN).astype(bf16)

    def run_mlp(chunk, build, *gates):
        with jax.named_scope("mlp"):
            up, down = build(*gates)
            full_fc1.append(up)
            full_fc2.append(down)
            return mlp(
                normed_two, all_back, up, down,
                bias_fc1[:, chunk * cut : (chunk + 1) * cut],
            )

    def run_heads(pair, *gates):
        with jax.named_scope("attend"):
            return attend(ctx_ref, heads, after(heads_back, *gates), tables, pair)

    norm_sums, head_lines = [], []

    def run_finish(theirs, keep, *gates):
        with jax.named_scope("finish"):
            rowwise = [d_heads[0], d_heads[1], attended[0], attended[1]]
            rowwise += [act[0], act[1], d_hidden[0], d_hidden[1], all_tokens]
            weights = [full_qkv, full_dense] + full_fc1 + full_fc2
            gains = after(jnp.stack([gain_one, gain_two]), *gates)
            out, norm_sum, head_line = finish(tp_ref, rowwise, weights, gains, theirs, keep)
            norm_sums.append(norm_sum)
            head_lines.append(head_line)
            return out

    d_heads, attended, act, d_hidden, lines_fc1 = [], [], [], [], []
    full_fc1, full_fc2 = [], []

    def keep_heads(results):
        d_heads.append(results[0])
        attended.append(results[1])

    def keep_mlp(results):
        act.append(results[0])
        d_hidden.append(results[1])
        lines_fc1.append(results[2])

    keep_heads(run_heads(0))
    with jax.named_scope("gather_params"):
        own_0, build_0 = cross_0(attended[0])
        cross_1 = gather(after(payloads[1], own_0), (cut, cut))
    keep_heads(run_heads(1, own_0))
    with jax.named_scope("gather_params"):
        own_1, build_1 = cross_1(attended[1])
    keep_mlp(run_mlp(0, build_0, own_1))
    with jax.named_scope("grad_fc"):
        kept_0, sent_0 = local_grads(normed_two, [d_hidden[0], act[0]])
    with jax.named_scope("grad_heads"):
        kept_h, sent_h = local_grads(
            normed_one, [d_heads[0], attended[0], d_heads[1], after(attended[1], sent_0)]
        )
    keep_mlp(run_mlp(1, build_1, sent_h))
    with jax.named_scope("sum_fc"):
        parts_0 = step_across(after(kept_0, act[1]), sent_0)
    theirs_sent = run_finish(True, False, *parts_0)
    with jax.named_scope("finish"):
        theirs_got = swap(theirs_sent, "tp", 1)
    theirs_kept = run_finish(True, True, theirs_sent)
    with jax.named_scope("sum_fc"):
        total_0 = step_along([after(parts_0[0], theirs_kept)] + list(parts_0[1:]))
    with jax.named_scope("sum_heads"):
        parts_h = step_across(after(kept_h, total_0), sent_h)
    with jax.named_scope("finish"):
        theirs_kept = after(theirs_kept, *parts_h)
        low_theirs = [(theirs_kept[at] + theirs_got[at].astype(f32)).astype(bf16) for at in range(2)]
        from_ctx = [swap(value, "ctx", 1) for value in low_theirs]
    with jax.named_scope("grad_fc"):
        kept_1, sent_1 = local_grads(normed_two, [d_hidden[1], after(act[1], *low_theirs)])
    with jax.named_scope("sum_heads"):
        mine_sent = run_finish(False, False, sent_1)
        total_h = step_along([after(parts_h[0], mine_sent)] + list(parts_h[1:]))
    with jax.named_scope("finish"):
        mine_got = swap(mine_sent, "tp", 1)
    with jax.named_scope("sum_fc"):
        parts_1 = step_across(after(kept_1, mine_sent, from_ctx[0], total_h), sent_1)
    mine_kept = run_finish(False, True, mine_sent, *parts_1)
    with jax.named_scope("sum_fc"):
        sums_0, sums_h = exchange_owned([total_0, total_h], mine_kept)
        total_1 = step_along([after(parts_1[0], mine_kept)] + list(parts_1[1:]))
        (sums_1,) = exchange_owned([total_1])
    heads_states = (w_qkv, m_qkv, v_qkv, w_dense, m_dense, v_dense)
    fc_states = (w_fc1, m_fc1, v_fc1, w_fc2, m_fc2, v_fc2)

    with jax.named_scope("finish"):
        norm_rows = sum(norm_sums)
        head_line = sum(head_lines)
        out_sum, d_unit = [
            mine_kept[at] + mine_got[at].astype(f32) + from_ctx[at].astype(f32) for at in range(2)
        ]

        own_tokens, own_back = [after(half, attended[0]).astype(f32) for half in halves]
        outputs = (own_tokens + out_sum + bias_dense + bias_fc2).astype(bf16)
        centre = own_tokens - jnp.mean(own_tokens, axis=-1, keepdims=True)
        inverse = lax.rsqrt(jnp.mean(centre * centre, axis=-1, keepdims=True) + norm_eps)
        unit = centre * inverse
        mean_d = jnp.mean(d_unit, axis=-1, keepdims=True)
        mean_du = jnp.mean(d_unit * unit, axis=-1, keepdims=True)
        input_grad = own_back + inverse * (d_unit - mean_d - unit * mean_du)
        halves = [outputs, input_grad]
        outputs, input_grad = share(tp_ref, halves, [swap(value, "tp", 1) for value in halves])

    with jax.named_scope("vector_grads"):
        bias_back = jnp.sum(own_back, axis=0)[None]
        head_rows = jnp.swapaxes(head_line.reshape(pairs, 3, lanes), 0, 1).reshape(3, own_heads)
        placed_heads = lax.dynamic_update_slice_in_dim(
            jnp.zeros((3, width), f32), head_rows, tp * head_cols + ctx * own_heads, 1
        )
        placed_fc1 = lax.dynamic_update_slice_in_dim(
            jnp.zeros((1, FF), f32),
            jnp.concatenate(lines_fc1, axis=1),
            tp * units + ctx * own_units,
            1,
        ).reshape(fc1_rows, width)
        vector_grads = jnp.concatenate(
            [placed_heads, bias_back, placed_fc1, bias_back, norm_rows], axis=0
        )
        vector_grads = after(vector_grads, total_1)
        if custom:
            for axis, masks in (("tp", (1,)), ("shard", (1,)), ("shard", (4, 6, 2)), ("ctx", (1,))):
                vector_grads = vector_grads + sum(swap(vector_grads, axis, mask) for mask in masks)
        else:
            vector_grads = lax.psum(vector_grads, ("shard", "ctx", "tp"))
        owned_vectors = lax.dynamic_slice_in_dim(vector_grads, shard * rows, rows, 1)

    results = [outputs, input_grad]
    head_sums = list(sums_h)
    fc_sums = [*sums_0, *sums_1]
    with jax.named_scope("adam"):
        if custom:
            heads_results = adam_matrices(adam_heads_kernel, ctx_ref, head_sums, heads_states)
            fc_results = adam_matrices(adam_fc_kernel, ctx_ref, fc_sums, fc_states)
            results += list(heads_results) + list(fc_results)
        else:

            def by_ctx(sums):
                mine, other = jnp.stack(sums[0::2]).astype(f32), jnp.stack(sums[1::2]).astype(f32)
                return jnp.stack([jnp.where(ctx == 0, mine, other), jnp.where(ctx == 0, other, mine)])

            owned = by_ctx(head_sums).reshape(2, rows, pairs, 4, lanes)
            owned = jnp.transpose(owned, (3, 1, 0, 2, 4)).reshape(4, rows, head_cols)
            owned_fc = by_ctx(fc_sums).reshape(2, chunks, rows, 2, cut)
            owned_fc = jnp.transpose(owned_fc, (3, 2, 0, 1, 4)).reshape(2, rows, units)
            for gradient, entry in (
                (owned[:3], heads_states[:3]),
                (owned[3].T, heads_states[3:]),
                (owned_fc[0], fc_states[:3]),
                (owned_fc[1].T, fc_states[3:]),
            ):
                results += adam(*entry, gradient, rate_matrix, weight_decay)
        results += adam(vectors, m_vectors, v_vectors, owned_vectors, rate_vector, 0.0)
    return tuple(results)


def solution(mesh):
    tokens = P(("shard", "ctx"), None)
    layouts = [P(None, "shard", "tp"), P("tp", "shard"), P("shard", "tp"), P("tp", "shard"), P(None, "shard")]
    params = tuple(layout for layout in layouts for _ in range(3))
    return jax.shard_map(
        body,
        mesh=mesh,
        in_specs=(tokens, tokens) + params,
        out_specs=(tokens, tokens) + params,
        check_vma=False,
    )
```

```python
import math

import jax
import jax.numpy as jnp
from jax import lax
from jax.experimental import pallas as pl
from jax.experimental.pallas import tpu as pltpu
from jax.sharding import PartitionSpec as P

D = 1024
HD = 64
ROT = 16
FF = 4096
STEP = 10

norm_eps = 1e-05
rope_base = 10000.0
masked_score = -1e30
beta_one = 0.9
beta_two = 0.95
adam_eps = 1e-08
rate_matrix = 0.05
rate_vector = 0.5
weight_decay = 0.01

BQ = 512
BK = 512
UNIT_BLOCK = 256
VMEM = 56 * 1024 * 1024

bf16 = jnp.bfloat16
f32 = jnp.float32


def dot(a, b, contract):
    return lax.dot_general(a, b, (contract, ((), ())), preferred_element_type=f32)


NN = ((1,), (0,))
NT = ((1,), (1,))
TN = ((0,), (0,))


def cost(flops, moved):
    return pl.CostEstimate(flops=int(flops), bytes_accessed=int(moved), transcendentals=0)


def swap(value, axis, mask):
    return lax.ppermute(value, axis, [(i, i ^ mask) for i in range(lax.axis_size(axis))])


def pick(value, index, axis):
    return lax.dynamic_index_in_dim(value, index, axis, keepdims=False)


def assemble(own, got, index, widths):
    _, rows, cols = own.shape

    def kernel(index_ref, own_ref, got_ref, *outs):
        for which, ref in enumerate((own_ref, got_ref)):
            for r in range(4):
                slot = index_ref[0] ^ ((r << 1) | which)
                start = 0
                for out, width in zip(outs, widths):
                    out[slot] = ref[r, :, start : start + width]
                    start += width

    vmem = pl.BlockSpec(memory_space=pltpu.VMEM)
    return pl.pallas_call(
        kernel,
        in_specs=[pl.BlockSpec(memory_space=pltpu.SMEM), vmem, vmem],
        out_specs=[vmem] * len(widths),
        out_shape=[jax.ShapeDtypeStruct((8, rows, width), bf16) for width in widths],
        cost_estimate=cost(0, 32 * rows * cols),
        compiler_params=pltpu.CompilerParams(vmem_limit_bytes=VMEM),
    )(index, own, got)


def turn(value, cosine, sine_up, sine_down, sign):
    up = pltpu.roll(value, value.shape[1] - ROT // 2, 1)
    down = pltpu.roll(value, ROT // 2, 1)
    return value * cosine + sign * (up * sine_up + down * sine_down)


def attend_kernel(
    ctx_ref, heads_ref, back_ref, cos_ref, up_ref, down_ref, heads_out, back_out,
    q_s, k_s, v_s, g_s, kt_s, vt_s, e_s, dp_s, dk_s, dv_s, dq_s, o_s, ot_s, dqt_s,
):
    step = pl.program_id(0)
    half = back_ref.shape[0] // 2
    lanes = back_ref.shape[1]
    ctx = ctx_ref[0]
    scale = HD ** (-0.5)

    @pl.when(step == 0)
    def _():
        dk_s[...] = jnp.zeros_like(dk_s)
        dv_s[...] = jnp.zeros_like(dv_s)
        for first, which in ((0, ctx), (half, 1 - ctx)):
            for at in range(0, half, BK):
                block = which * (half // BK) + at // BK
                rows = pl.ds(pl.multiple_of(block * BK, BK), BK)
                tables = (cos_ref[rows], up_ref[rows], down_ref[rows])
                here = slice(first + at, first + at + BK)
                query = turn(heads_ref[here, :lanes].astype(f32), *tables, 1.0).astype(bf16)
                q_s[rows] = (query.astype(f32) * scale).astype(bf16)
                key = turn(heads_ref[here, lanes : 2 * lanes].astype(f32), *tables, 1.0).astype(bf16)
                k_s[rows] = key
                kt_s[block] = key.astype(f32).T.astype(bf16)
                value = heads_ref[here, 2 * lanes :]
                v_s[rows] = value
                vt_s[block] = value.astype(f32).T.astype(bf16)
                g_s[rows] = back_ref[here]

    rows = pl.ds(pl.multiple_of(step * BQ, BQ), BQ)
    low_lanes = lax.broadcasted_iota(jnp.int32, (BQ, lanes), 1) < HD

    def both(value):
        value = value.astype(f32)
        return jnp.concatenate(
            [jnp.where(low_lanes, value, 0.0), jnp.where(low_lanes, 0.0, value)], axis=0
        ).astype(bf16)

    q_both = both(q_s[rows])
    g_both = both(g_s[rows])

    def keys_at(block):
        return pl.ds(pl.multiple_of(block * BK, BK), BK)

    def score(block):
        return dot(k_s[keys_at(block)], q_both, NT)

    key_row = lax.broadcasted_iota(jnp.int32, (BK, BQ), 0)
    query_col = lax.broadcasted_iota(jnp.int32, (BK, BQ), 1)
    keep = key_row <= query_col
    diagonal = score(step)
    diagonal = jnp.where(jnp.concatenate([keep, keep], axis=1), diagonal, masked_score)
    e_s[step] = diagonal
    top = jnp.max(diagonal, axis=0, keepdims=True)

    def first_pass(block, top):
        value = score(block)
        e_s[block] = value
        return jnp.maximum(top, jnp.max(value, axis=0, keepdims=True))

    top = lax.fori_loop(0, step, first_pass, top)

    def second_pass(block, carry):
        total, inner = carry
        exponent = jnp.exp(e_s[block] - top)
        d_shares = dot(v_s[keys_at(block)], g_both, NT)
        e_s[block] = exponent
        dp_s[block] = d_shares
        total = total + jnp.sum(exponent, axis=0, keepdims=True)
        inner = inner + jnp.sum(exponent * d_shares, axis=0, keepdims=True)
        return total, inner

    zero = jnp.zeros((1, 2 * BQ), f32)
    total, inner = lax.fori_loop(0, step + 1, second_pass, (zero, zero))
    inverse = 1.0 / total
    inner = inner * inverse
    ot_s[...] = jnp.zeros_like(ot_s)
    dqt_s[...] = jnp.zeros_like(dqt_s)

    def third_pass(block, carry):
        shares = e_s[block] * inverse
        low = shares.astype(bf16)
        d_scores = (shares * (dp_s[block] - inner)).astype(bf16)
        at = keys_at(block)
        dv_s[at] += dot(low, g_both, NN)
        dk_s[at] += dot(d_scores, q_both, NN)
        ot_s[...] += dot(vt_s[block], low, NN)
        dqt_s[...] += dot(kt_s[block], d_scores, NN)
        return carry

    lax.fori_loop(0, step + 1, third_pass, 0)

    def joined(ref):
        return jnp.concatenate([ref[:HD, :BQ], ref[HD:, BQ:]], axis=0).T

    o_s[rows] = joined(ot_s).astype(bf16)
    d_query = joined(dqt_s) * scale
    dq_s[rows] = turn(d_query, cos_ref[rows], up_ref[rows], down_ref[rows], -1.0).astype(bf16)

    @pl.when(step == pl.num_programs(0) - 1)
    def _():
        for first, which in ((0, ctx), (half, 1 - ctx)):
            for at in range(0, half, BK):
                here = slice(first + at, first + at + BK)
                rows = pl.ds(pl.multiple_of(which * half + at, BK), BK)
                tables = (cos_ref[rows], up_ref[rows], down_ref[rows])
                heads_out[here, :lanes] = dq_s[rows]
                heads_out[here, lanes : 2 * lanes] = turn(dk_s[rows], *tables, -1.0).astype(bf16)
                heads_out[here, 2 * lanes :] = dv_s[rows].astype(bf16)
                back_out[here] = o_s[rows]


def attend(ctx, heads, back, tables, pair):
    length = heads.shape[0]
    lanes = 2 * HD
    blocks = length // BK
    table = pl.BlockSpec((length, lanes), lambda i: (0, 0))
    return pl.pallas_call(
        attend_kernel,
        grid=(length // BQ,),
        in_specs=[
            pl.BlockSpec(memory_space=pltpu.SMEM),
            pl.BlockSpec((length, 3 * lanes), lambda i: (0, pair)),
            pl.BlockSpec((length, lanes), lambda i: (0, pair)),
            table,
            table,
            table,
        ],
        out_specs=[pl.BlockSpec((length, 3 * lanes), lambda i: (0, 0)), table],
        out_shape=[
            jax.ShapeDtypeStruct((length, 3 * lanes), bf16),
            jax.ShapeDtypeStruct((length, lanes), bf16),
        ],
        scratch_shapes=[pltpu.VMEM((length, lanes), bf16)] * 4
        + [pltpu.VMEM((blocks, lanes, BK), bf16)] * 2
        + [pltpu.VMEM((blocks, BK, 2 * BQ), f32)] * 2
        + [pltpu.VMEM((length, lanes), f32)] * 2
        + [pltpu.VMEM((length, lanes), bf16)] * 2
        + [pltpu.VMEM((lanes, 2 * BQ), f32)] * 2,
        cost_estimate=cost(6 * 4 * length * length * lanes * 2, 16 * length * lanes),
        compiler_params=pltpu.CompilerParams(vmem_limit_bytes=VMEM),
    )(ctx, heads, back, *tables)


def mlp_kernel(normed_ref, back_ref, up_ref, down_ref, bias_ref, act_ref, dh_ref, sum_ref):
    rows = normed_ref.shape[0]
    step = min(256, rows)
    total = jnp.zeros((1, up_ref.shape[1]), f32)
    for at in range(0, rows, step):
        here = slice(at, at + step)
        hidden = dot(normed_ref[here], up_ref[...], NN) + bias_ref[...]
        d_act = dot(back_ref[here], down_ref[...], NN)
        share = 0.5 * (1.0 + lax.erf(hidden * (0.5**0.5)))
        density = jnp.exp(-0.5 * hidden * hidden) * 0.3989422804014327
        act_ref[here] = (hidden * share).astype(bf16)
        d_hidden = (d_act * (share + hidden * density)).astype(bf16)
        dh_ref[here] = d_hidden
        total = total + jnp.sum(d_hidden.astype(f32), axis=0, keepdims=True)
    sum_ref[...] = total


def mlp(normed, back, up, down, bias):
    rows, width = normed.shape
    units = up.shape[1]
    whole = pl.BlockSpec((rows, width), lambda j: (0, 0))
    columns = pl.BlockSpec((width, UNIT_BLOCK), lambda j: (0, j))
    out = pl.BlockSpec((rows, UNIT_BLOCK), lambda j: (0, j))
    line = pl.BlockSpec((1, UNIT_BLOCK), lambda j: (0, j))
    return pl.pallas_call(
        mlp_kernel,
        grid=(units // UNIT_BLOCK,),
        in_specs=[whole, whole, columns, columns, line],
        out_specs=[out, out, line],
        out_shape=[
            jax.ShapeDtypeStruct((rows, units), bf16),
            jax.ShapeDtypeStruct((rows, units), bf16),
            jax.ShapeDtypeStruct((1, units), f32),
        ],
        cost_estimate=cost(12 * rows * width * units, 8 * rows * width),
        compiler_params=pltpu.CompilerParams(vmem_limit_bytes=VMEM),
    )(normed, back, up, down, bias)


def grads_kernel(column_ref, first_ref, second_ref, *refs):
    rights, (kept_ref, sent_ref) = refs[:-2], refs[-2:]
    parts = [dot((first_ref, second_ref)[at % 2][...], ref[...], TN) for at, ref in enumerate(rights)]
    value = jnp.concatenate(parts, axis=1)
    rows = value.shape[0] // 2
    top, bottom = value[:rows], value[rows:]
    here = column_ref[0] == 0
    kept_ref[0] = jnp.where(here, top, bottom)
    sent_ref[0] = jnp.where(here, bottom, top).astype(bf16)


def grads(column, first, second, rights):
    length, width = first.shape
    rows = width // 8
    cols = sum(right.shape[1] for right in rights)
    left = pl.BlockSpec((length, 2 * rows), lambda i: (0, i))
    out = pl.BlockSpec((1, rows, cols), lambda i: (i, 0, 0))
    return pl.pallas_call(
        grads_kernel,
        grid=(4,),
        in_specs=[pl.BlockSpec(memory_space=pltpu.SMEM), left, left]
        + [pl.BlockSpec(right.shape, lambda i: (0, 0)) for right in rights],
        out_specs=[out, out],
        out_shape=[
            jax.ShapeDtypeStruct((4, rows, cols), f32),
            jax.ShapeDtypeStruct((4, rows, cols), bf16),
        ],
        cost_estimate=cost(0, 6 * width * cols),
        compiler_params=pltpu.CompilerParams(vmem_limit_bytes=VMEM),
    )(column, first, second, *rights)


def combine(line, kept, crossed):
    def kernel(line_ref, kept_ref, crossed_ref, own_ref, *outs):
        for r, out in zip((0, 2, 3, 1), (own_ref,) + outs):
            at = line_ref[0] ^ r
            out[...] = (kept_ref[at] + crossed_ref[at].astype(f32)).astype(out.dtype)

    vmem = pl.BlockSpec(memory_space=pltpu.VMEM)
    shape = kept.shape[1:]
    return pl.pallas_call(
        kernel,
        in_specs=[pl.BlockSpec(memory_space=pltpu.SMEM), vmem, vmem],
        out_specs=[vmem] * 4,
        out_shape=[jax.ShapeDtypeStruct(shape, f32)] + [jax.ShapeDtypeStruct(shape, bf16)] * 3,
        cost_estimate=cost(0, 12 * math.prod(kept.shape)),
        compiler_params=pltpu.CompilerParams(vmem_limit_bytes=VMEM),
    )(line, kept, crossed)


def finish_kernel(
    tp_ref, dh_a, dh_b, o_a, o_b, act_a, act_b, du_a, du_b, tok_ref,
    wh, wd, f1_a, f1_b, f2_a, f2_b, gain_ref, out_ref, norm_ref, line_ref,
):
    cut = dh_a.shape[1]
    lanes = o_a.shape[1]

    @pl.when(pl.program_id(0) == 0)
    def _():
        norm_ref[...] = jnp.zeros_like(norm_ref)
        line_ref[...] = jnp.zeros_like(line_ref)

    out_ref[0] = (
        dot(act_a[...], f2_a[...], NT)
        + dot(act_b[...], f2_b[...], NT)
        + dot(o_a[...], wd[:, :lanes], NT)
        + dot(o_b[...], wd[:, lanes:], NT)
    ).astype(out_ref.dtype)
    one = dot(dh_a[...], wh[:, :cut], NT) + dot(dh_b[...], wh[:, cut:], NT)
    two = dot(du_a[...], f1_a[...], NT) + dot(du_b[...], f1_b[...], NT)
    out_ref[1] = (one * gain_ref[0:1] + two * gain_ref[1:2]).astype(out_ref.dtype)
    tokens = tok_ref[...].astype(f32)
    centre = tokens - jnp.mean(tokens, axis=-1, keepdims=True)
    unit = centre * lax.rsqrt(jnp.mean(centre * centre, axis=-1, keepdims=True) + norm_eps)
    for at, value in enumerate((one * unit, one, two * unit, two)):
        norm_ref[at : at + 1] += jnp.sum(value, axis=0, keepdims=True)
    line_ref[0:1, :cut] += jnp.sum(dh_a[...].astype(f32), axis=0, keepdims=True)
    line_ref[0:1, cut:] += jnp.sum(dh_b[...].astype(f32), axis=0, keepdims=True)


def finish(tp, rowwise, weights, gains, theirs, keep):
    length, width = rowwise[-1].shape
    block = min(256, length // 8)
    heads = weights[0].shape[1]
    steps = length // (4 * block)
    start = 2 * steps if theirs else 0
    kind = f32 if keep else bf16

    def row(i, tp_ref):
        side = tp_ref[0] if keep else 1 - tp_ref[0]
        return start + side * steps + i

    def by_rows(value):
        return pl.BlockSpec((block, value.shape[1]), lambda i, ref: (row(i, ref), 0))

    def fixed(shape):
        return pl.BlockSpec(shape, lambda i, ref: (0, 0))

    out = pl.BlockSpec((2, block, width), lambda i, ref: (0, i, 0))
    return pl.pallas_call(
        finish_kernel,
        grid_spec=pltpu.PrefetchScalarGridSpec(
            num_scalar_prefetch=1,
            grid=(steps,),
            in_specs=[by_rows(value) for value in rowwise]
            + [fixed(value.shape) for value in weights]
            + [fixed(gains.shape)],
            out_specs=[out, fixed((4, width)), fixed((1, heads))],
        ),
        out_shape=[
            jax.ShapeDtypeStruct((2, steps * block, width), kind),
            jax.ShapeDtypeStruct((4, width), f32),
            jax.ShapeDtypeStruct((1, heads), f32),
        ],
        cost_estimate=cost((6 if keep else 0) * length * width * sum(w.shape[1] for w in weights), 4 * length * width),
        compiler_params=pltpu.CompilerParams(vmem_limit_bytes=VMEM),
    )(tp, *rowwise, *weights, gains)


def share_kernel(tp_ref, own_a, other_a, own_b, other_b, out_a, out_b):
    half = own_a.shape[0]
    here = pl.ds(pl.multiple_of(tp_ref[0] * half, half), half)
    there = pl.ds(pl.multiple_of((1 - tp_ref[0]) * half, half), half)
    out_a[here] = own_a[...]
    out_a[there] = other_a[...]
    out_b[here] = own_b[...]
    out_b[there] = other_b[...]


def share(tp, own, other):
    half, width = own[0].shape
    vmem = pl.BlockSpec(memory_space=pltpu.VMEM)
    return pl.pallas_call(
        share_kernel,
        in_specs=[pl.BlockSpec(memory_space=pltpu.SMEM)] + [vmem] * 4,
        out_specs=[vmem] * 2,
        out_shape=[jax.ShapeDtypeStruct((2 * half, width), value.dtype) for value in own],
        cost_estimate=cost(0, 0),
        compiler_params=pltpu.CompilerParams(vmem_limit_bytes=VMEM),
    )(tp, own[0], other[0], own[1], other[1])


def after(value, *others):
    return lax.optimization_barrier((value,) + others)[0] if others else value


def gather_chunk(payload, index, widths):
    line = [swap(payload, "shard", r << 1) for r in (2, 3, 1)]

    def cross(*gates):
        own = jnp.stack([after(payload, *gates), line[2], line[0], line[1]])
        got = swap(own, "shard", 1)

        def build(*gates):
            full = assemble(after(own, *gates), got, index, widths)
            return [value.reshape(-1, value.shape[2]) for value in full]

        return own, build

    return cross


def adam(weight, first, second, gradient, rate, decay):
    first_new = beta_one * first + (1.0 - beta_one) * gradient
    second_new = beta_two * second + (1.0 - beta_two) * gradient * gradient
    scaled = (
        first_new
        / (1.0 - beta_one**STEP)
        / (jnp.sqrt(second_new / (1.0 - beta_two**STEP)) + adam_eps)
    )
    return (first_new, second_new, weight - rate * (scaled + decay * weight))


def adam_store(weight, first, second, gradient, outs, at):
    for ref, value in zip(outs, adam(weight[at], first[at], second[at], gradient, rate_matrix, weight_decay)):
        ref[at] = value


def adam_heads_kernel(ctx_ref, *refs):
    sums, (wq, mq, vq, wd, md, vd), outs = refs[:-12], refs[-12:-6], refs[-6:]
    mine, other = sums
    lanes = 2 * HD
    pairs = mine.shape[1] // (4 * lanes)
    first = ctx_ref[0] == 0
    for pair in range(pairs):
        for plane in range(4):
            cols = slice((4 * pair + plane) * lanes, (4 * pair + plane + 1) * lanes)
            left, right = mine[:, cols], other[:, cols]
            for group, total in enumerate((jnp.where(first, left, right), jnp.where(first, right, left))):
                start = (group * pairs + pair) * lanes
                place = slice(start, start + lanes)
                if plane < 3:
                    adam_store(wq, mq, vq, total, outs[:3], (plane, slice(None), place))
                else:
                    adam_store(wd, md, vd, total.T, outs[3:], (place, slice(None)))


def adam_fc_kernel(ctx_ref, *refs):
    sums, (w1, m1, v1, w2, m2, v2), outs = refs[:-12], refs[-12:-6], refs[-6:]
    chunks = len(sums) // 2
    cut = w1.shape[1] // (2 * chunks)
    tile = 128
    first = ctx_ref[0] == 0
    for chunk in range(chunks):
        mine, other = sums[2 * chunk : 2 * chunk + 2]
        for at in range(0, 2 * cut, tile):
            left, right = mine[:, at : at + tile], other[:, at : at + tile]
            for group, total in enumerate((jnp.where(first, left, right), jnp.where(first, right, left))):
                start = (group * chunks + chunk) * cut + at % cut
                place = slice(start, start + tile)
                if at < cut:
                    adam_store(w1, m1, v1, total, outs[:3], (slice(None), place))
                else:
                    adam_store(w2, m2, v2, total.T, outs[3:], (place, slice(None)))


def adam_matrices(kernel, ctx, sums, states):
    vmem = pl.BlockSpec(memory_space=pltpu.VMEM)
    return pl.pallas_call(
        kernel,
        in_specs=[pl.BlockSpec(memory_space=pltpu.SMEM)] + [vmem] * (len(sums) + 6),
        out_specs=[vmem] * 6,
        out_shape=[jax.ShapeDtypeStruct(value.shape, f32) for value in states],
        cost_estimate=cost(0, 0),
        compiler_params=pltpu.CompilerParams(vmem_limit_bytes=VMEM),
    )(ctx, *sums, *states)


def rope_tables(length, lanes):
    half = ROT // 2
    lane = jnp.arange(lanes, dtype=jnp.int32) % HD
    frequency = rope_base ** (-((lane % half).astype(f32) * 2.0) / ROT)
    angle = jnp.arange(length, dtype=f32)[:, None] * frequency[None, :]
    cosine, sine = jnp.cos(angle), jnp.sin(angle)
    return [
        jnp.where(lane < ROT, cosine, 1.0),
        jnp.where(lane < half, -sine, 0.0),
        jnp.where((lane >= half) & (lane < ROT), sine, 0.0),
    ]


def body(
    inputs, cotangent, w_qkv, m_qkv, v_qkv, w_dense, m_dense, v_dense,
    w_fc1, m_fc1, v_fc1, w_fc2, m_fc2, v_fc2, vectors, m_vectors, v_vectors,
):
    shard = lax.axis_index("shard")
    ctx = lax.axis_index("ctx")
    tp = lax.axis_index("tp")
    shards = lax.axis_size("shard")
    tok_count, width = inputs.shape
    rows = w_qkv.shape[1]
    head_cols = w_qkv.shape[2]
    units = w_fc1.shape[1]
    lanes = 2 * HD
    pairs, chunks = head_cols // (2 * lanes), 2
    own_heads, own_units = head_cols // 2, units // 2
    cut = own_units // chunks
    fc1_rows = FF // D
    count = vectors.shape[0]
    custom = shards == 8
    ctx_ref = ctx.reshape(1).astype(jnp.int32)
    shard_ref = shard.reshape(1).astype(jnp.int32)

    tp_ref = tp.reshape(1).astype(jnp.int32)
    column_ref, line_ref = shard_ref % 2, shard_ref // 2

    def gather(payload, widths):
        if custom:
            return gather_chunk(payload, shard_ref, widths)
        full = lax.all_gather(payload, "shard", axis=0, tiled=True)
        cuts = [sum(widths[:at]) for at in range(len(widths) + 1)]
        return lambda *gates: (full, lambda *gates: [full[:, a:b] for a, b in zip(cuts, cuts[1:])])

    def local_grads(first, rights):
        if custom:
            return grads(column_ref, first, all_back, rights)
        parts = [dot((first, all_back)[at % 2], right, TN) for at, right in enumerate(rights)]
        both = jnp.concatenate(parts, axis=1).astype(bf16)
        return both, both

    def step_across(kept, sent):
        if custom:
            crossed = swap(sent, "shard", 1)
            return combine(line_ref, kept, crossed)
        total = lax.psum_scatter(sent, "shard", scatter_dimension=0, tiled=True).astype(f32)
        return [total]

    def step_along(parts):
        total = parts[0]
        for r, part in zip((2, 3, 1), parts[1:]):
            total = total + swap(part, "shard", r << 1).astype(f32)
        return total

    def exchange_owned(totals, *gates):
        return [(value, swap(after(value, *gates), "ctx", 1)) for value in totals]

    with jax.named_scope("tokens"):
        part = tok_count // 2
        halves = [pick(value.reshape(2, part, width), tp, 0) for value in (inputs, cotangent)]

    with jax.named_scope("gather_params"):
        low_qkv = pick(w_qkv.reshape(3, rows, 2, pairs, lanes), ctx, 2).astype(bf16)
        low_qkv = jnp.transpose(low_qkv, (1, 2, 0, 3)).reshape(rows, pairs * 3 * lanes)
        low_dense = pick(w_dense.reshape(2, own_heads, rows), ctx, 0).astype(bf16).T
        low_fc1 = pick(w_fc1.reshape(rows, 2, own_units), ctx, 1).astype(bf16)
        low_fc2 = pick(w_fc2.reshape(2, own_units, rows), ctx, 0).astype(bf16).T
        low_vectors = jnp.pad(vectors.astype(bf16).T, ((0, 0), (0, 128 - count)))
        payload = jnp.concatenate([low_qkv, low_dense, low_vectors], axis=1)
        own, build = gather(payload, (pairs * 3 * lanes, pairs * lanes, 128))()
    with jax.named_scope("tokens"):
        direct = [swap(halves[0], "ctx", 1)]
        direct.append(swap(after(halves[1], own), "ctx", 1))
        shared_rows = [swap(value, "tp", 1) for value in direct]

        def whole_sequence(value, at):
            mine, other = direct[at], shared_rows[at]
            return jnp.concatenate(
                [value, jnp.where(tp == 0, mine, other), jnp.where(tp == 0, other, mine)], axis=0
            )

        all_tokens = whole_sequence(inputs, 0)
        all_back = whole_sequence(cotangent, 1)
    with jax.named_scope("gather_params"):
        full_qkv, full_dense, full_vectors = build()
        payloads = [
            jnp.concatenate([low_fc1[:, c * cut : (c + 1) * cut], low_fc2[:, c * cut : (c + 1) * cut]], axis=1)
            for c in range(chunks)
        ]
        cross_0 = gather(after(payloads[0], own, direct[1]), (cut, cut))

    vec_rows = full_vectors[:, :count].T.astype(f32)
    bias_qkv = lax.dynamic_slice_in_dim(vec_rows[0:3], tp * head_cols + ctx * own_heads, own_heads, 1)
    bias_qkv = jnp.swapaxes(bias_qkv.reshape(3, pairs, lanes), 0, 1).reshape(1, -1)
    bias_dense = vec_rows[3]
    bias_fc1 = lax.dynamic_slice_in_dim(
        vec_rows[4 : 4 + fc1_rows].reshape(1, -1), tp * units + ctx * own_units, own_units, 1
    )
    bias_fc2 = vec_rows[4 + fc1_rows]
    gain_one = vec_rows[5 + fc1_rows]
    shift_one = vec_rows[6 + fc1_rows]
    gain_two = vec_rows[7 + fc1_rows]
    shift_two = vec_rows[8 + fc1_rows]

    with jax.named_scope("norm"):
        tokens = all_tokens.astype(f32)
        centre = tokens - jnp.mean(tokens, axis=-1, keepdims=True)
        inverse = lax.rsqrt(jnp.mean(centre * centre, axis=-1, keepdims=True) + norm_eps)
        unit = centre * inverse
        normed_one = (unit * gain_one + shift_one).astype(bf16)
        normed_two = (unit * gain_two + shift_two).astype(bf16)

    tables = rope_tables(2 * tok_count, lanes)
    with jax.named_scope("project"):
        heads = (dot(normed_one, full_qkv, NN) + bias_qkv).astype(bf16)
        heads_back = dot(all_back, full_dense, NN).astype(bf16)

    def run_mlp(chunk, build, *gates):
        with jax.named_scope("mlp"):
            up, down = build(*gates)
            full_fc1.append(up)
            full_fc2.append(down)
            return mlp(
                normed_two, all_back, up, down,
                bias_fc1[:, chunk * cut : (chunk + 1) * cut],
            )

    def run_heads(pair, *gates):
        with jax.named_scope("attend"):
            return attend(ctx_ref, heads, after(heads_back, *gates), tables, pair)

    norm_sums, head_lines = [], []

    def run_finish(theirs, keep, *gates):
        with jax.named_scope("finish"):
            rowwise = [d_heads[0], d_heads[1], attended[0], attended[1]]
            rowwise += [act[0], act[1], d_hidden[0], d_hidden[1], all_tokens]
            weights = [full_qkv, full_dense] + full_fc1 + full_fc2
            gains = after(jnp.stack([gain_one, gain_two]), *gates)
            out, norm_sum, head_line = finish(tp_ref, rowwise, weights, gains, theirs, keep)
            norm_sums.append(norm_sum)
            head_lines.append(head_line)
            return out

    d_heads, attended, act, d_hidden, lines_fc1 = [], [], [], [], []
    full_fc1, full_fc2 = [], []

    def keep_heads(results):
        d_heads.append(results[0])
        attended.append(results[1])

    def keep_mlp(results):
        act.append(results[0])
        d_hidden.append(results[1])
        lines_fc1.append(results[2])

    keep_heads(run_heads(0))
    with jax.named_scope("gather_params"):
        own_0, build_0 = cross_0(attended[0])
        cross_1 = gather(after(payloads[1], own_0), (cut, cut))
    keep_heads(run_heads(1, own_0))
    with jax.named_scope("gather_params"):
        own_1, build_1 = cross_1(attended[1])
    keep_mlp(run_mlp(0, build_0, own_1))
    with jax.named_scope("grad_fc"):
        kept_0, sent_0 = local_grads(normed_two, [d_hidden[0], act[0]])
    with jax.named_scope("grad_heads"):
        kept_h, sent_h = local_grads(
            normed_one, [d_heads[0], attended[0], d_heads[1], after(attended[1], sent_0)]
        )
    keep_mlp(run_mlp(1, build_1, sent_h))
    with jax.named_scope("sum_fc"):
        parts_0 = step_across(after(kept_0, act[1]), sent_0)
    theirs_sent = run_finish(True, False, *parts_0)
    with jax.named_scope("finish"):
        theirs_got = swap(theirs_sent, "tp", 1)
    theirs_kept = run_finish(True, True, theirs_sent)
    with jax.named_scope("sum_fc"):
        total_0 = step_along([after(parts_0[0], theirs_kept)] + list(parts_0[1:]))
        (sums_0,) = exchange_owned([total_0])
    with jax.named_scope("sum_heads"):
        parts_h = step_across(after(kept_h, total_0), sent_h)
    with jax.named_scope("finish"):
        theirs_kept = after(theirs_kept, *parts_h)
        low_theirs = [(theirs_kept[at] + theirs_got[at].astype(f32)).astype(bf16) for at in range(2)]
        from_ctx = [swap(value, "ctx", 1) for value in low_theirs]
    with jax.named_scope("grad_fc"):
        kept_1, sent_1 = local_grads(normed_two, [d_hidden[1], after(act[1], *low_theirs)])
    with jax.named_scope("sum_heads"):
        mine_sent = run_finish(False, False, sent_1, sums_0[1])
        total_h = step_along([after(parts_h[0], mine_sent)] + list(parts_h[1:]))
    with jax.named_scope("finish"):
        mine_got = swap(mine_sent, "tp", 1)
    with jax.named_scope("sum_fc"):
        parts_1 = step_across(after(kept_1, mine_sent, from_ctx[0], total_h), sent_1)
    mine_kept = run_finish(False, True, mine_sent, *parts_1)
    with jax.named_scope("sum_fc"):
        (sums_h,) = exchange_owned([total_h], mine_kept)
        total_1 = step_along([after(parts_1[0], mine_kept)] + list(parts_1[1:]))
        (sums_1,) = exchange_owned([total_1])
    heads_states = (w_qkv, m_qkv, v_qkv, w_dense, m_dense, v_dense)
    fc_states = (w_fc1, m_fc1, v_fc1, w_fc2, m_fc2, v_fc2)

    with jax.named_scope("finish"):
        norm_rows = sum(norm_sums)
        head_line = sum(head_lines)
        out_sum, d_unit = [
            mine_kept[at] + mine_got[at].astype(f32) + after(from_ctx[at], total_1).astype(f32)
            for at in range(2)
        ]

        own_tokens, own_back = [after(half, attended[0]).astype(f32) for half in halves]
        outputs = (own_tokens + out_sum + bias_dense + bias_fc2).astype(bf16)
        centre = own_tokens - jnp.mean(own_tokens, axis=-1, keepdims=True)
        inverse = lax.rsqrt(jnp.mean(centre * centre, axis=-1, keepdims=True) + norm_eps)
        unit = centre * inverse
        mean_d = jnp.mean(d_unit, axis=-1, keepdims=True)
        mean_du = jnp.mean(d_unit * unit, axis=-1, keepdims=True)
        input_grad = own_back + inverse * (d_unit - mean_d - unit * mean_du)
        halves = [outputs, input_grad]
        outputs, input_grad = share(tp_ref, halves, [swap(value, "tp", 1) for value in halves])

    if custom:
        with jax.named_scope("adam"):
            heads_results = adam_matrices(adam_heads_kernel, ctx_ref, list(sums_h), heads_states)

    with jax.named_scope("vector_grads"):
        bias_back = jnp.sum(own_back, axis=0)[None]
        head_rows = jnp.swapaxes(head_line.reshape(pairs, 3, lanes), 0, 1).reshape(3, own_heads)
        placed_heads = lax.dynamic_update_slice_in_dim(
            jnp.zeros((3, width), f32), head_rows, tp * head_cols + ctx * own_heads, 1
        )
        placed_fc1 = lax.dynamic_update_slice_in_dim(
            jnp.zeros((1, FF), f32),
            jnp.concatenate(lines_fc1, axis=1),
            tp * units + ctx * own_units,
            1,
        ).reshape(fc1_rows, width)
        vector_grads = jnp.concatenate(
            [placed_heads, bias_back, placed_fc1, bias_back, norm_rows], axis=0
        )
        vector_grads = after(vector_grads, total_1)
        if custom:
            for axis, masks in (("tp", (1,)), ("shard", (1,)), ("shard", (4, 6, 2)), ("ctx", (1,))):
                if len(masks) > 1:
                    vector_grads = after(vector_grads, heads_results[0])
                vector_grads = vector_grads + sum(swap(vector_grads, axis, mask) for mask in masks)
        else:
            vector_grads = lax.psum(vector_grads, ("shard", "ctx", "tp"))
        owned_vectors = lax.dynamic_slice_in_dim(vector_grads, shard * rows, rows, 1)

    results = [outputs, input_grad]
    head_sums = list(sums_h)
    fc_sums = [*sums_0, *sums_1]
    with jax.named_scope("adam"):
        if custom:
            fc_results = adam_matrices(adam_fc_kernel, ctx_ref, fc_sums, fc_states)
            results += list(heads_results) + list(fc_results)
        else:

            def by_ctx(sums):
                mine, other = jnp.stack(sums[0::2]).astype(f32), jnp.stack(sums[1::2]).astype(f32)
                return jnp.stack([jnp.where(ctx == 0, mine, other), jnp.where(ctx == 0, other, mine)])

            owned = by_ctx(head_sums).reshape(2, rows, pairs, 4, lanes)
            owned = jnp.transpose(owned, (3, 1, 0, 2, 4)).reshape(4, rows, head_cols)
            owned_fc = by_ctx(fc_sums).reshape(2, chunks, rows, 2, cut)
            owned_fc = jnp.transpose(owned_fc, (3, 2, 0, 1, 4)).reshape(2, rows, units)
            for gradient, entry in (
                (owned[:3], heads_states[:3]),
                (owned[3].T, heads_states[3:]),
                (owned_fc[0], fc_states[:3]),
                (owned_fc[1].T, fc_states[3:]),
            ):
                results += adam(*entry, gradient, rate_matrix, weight_decay)
        results += adam(vectors, m_vectors, v_vectors, owned_vectors, rate_vector, 0.0)
    return tuple(results)


def solution(mesh):
    tokens = P(("shard", "ctx"), None)
    layouts = [P(None, "shard", "tp"), P("tp", "shard"), P("shard", "tp"), P("tp", "shard"), P(None, "shard")]
    params = tuple(layout for layout in layouts for _ in range(3))
    return jax.shard_map(
        body,
        mesh=mesh,
        in_specs=(tokens, tokens) + params,
        out_specs=(tokens, tokens) + params,
        check_vma=False,
    )
```

```python
import math

import jax
import jax.numpy as jnp
from jax import lax
from jax.experimental import pallas as pl
from jax.experimental.pallas import tpu as pltpu
from jax.sharding import PartitionSpec as P

D = 1024
HD = 64
ROT = 16
FF = 4096
STEP = 10

norm_eps = 1e-05
rope_base = 10000.0
masked_score = -1e30
beta_one = 0.9
beta_two = 0.95
adam_eps = 1e-08
rate_matrix = 0.05
rate_vector = 0.5
weight_decay = 0.01

BQ = 512
BK = 512
UNIT_BLOCK = 256
VMEM = 56 * 1024 * 1024

bf16 = jnp.bfloat16
f32 = jnp.float32


def dot(a, b, contract):
    return lax.dot_general(a, b, (contract, ((), ())), preferred_element_type=f32)


NN = ((1,), (0,))
NT = ((1,), (1,))
TN = ((0,), (0,))


def cost(flops, moved):
    return pl.CostEstimate(flops=int(flops), bytes_accessed=int(moved), transcendentals=0)


def swap(value, axis, mask):
    return lax.ppermute(value, axis, [(i, i ^ mask) for i in range(lax.axis_size(axis))])


def pick(value, index, axis):
    return lax.dynamic_index_in_dim(value, index, axis, keepdims=False)


def assemble(own, got, index, widths):
    _, rows, cols = own.shape

    def kernel(index_ref, own_ref, got_ref, *outs):
        for which, ref in enumerate((own_ref, got_ref)):
            for r in range(4):
                slot = index_ref[0] ^ ((r << 1) | which)
                start = 0
                for out, width in zip(outs, widths):
                    out[slot] = ref[r, :, start : start + width]
                    start += width

    vmem = pl.BlockSpec(memory_space=pltpu.VMEM)
    return pl.pallas_call(
        kernel,
        in_specs=[pl.BlockSpec(memory_space=pltpu.SMEM), vmem, vmem],
        out_specs=[vmem] * len(widths),
        out_shape=[jax.ShapeDtypeStruct((8, rows, width), bf16) for width in widths],
        cost_estimate=cost(0, 32 * rows * cols),
        compiler_params=pltpu.CompilerParams(vmem_limit_bytes=VMEM),
    )(index, own, got)


def turn(value, cosine, sine_up, sine_down, sign):
    up = pltpu.roll(value, value.shape[1] - ROT // 2, 1)
    down = pltpu.roll(value, ROT // 2, 1)
    return value * cosine + sign * (up * sine_up + down * sine_down)


def attend_kernel(
    ctx_ref, heads_ref, back_ref, cos_ref, up_ref, down_ref, heads_out, back_out,
    q_s, k_s, v_s, g_s, kt_s, vt_s, e_s, dp_s, dk_s, dv_s, dq_s, o_s, ot_s, dqt_s,
):
    step = pl.program_id(0)
    half = back_ref.shape[0] // 2
    lanes = back_ref.shape[1]
    ctx = ctx_ref[0]
    scale = HD ** (-0.5)

    @pl.when(step == 0)
    def _():
        dk_s[...] = jnp.zeros_like(dk_s)
        dv_s[...] = jnp.zeros_like(dv_s)
        for first, which in ((0, ctx), (half, 1 - ctx)):
            for at in range(0, half, BK):
                block = which * (half // BK) + at // BK
                rows = pl.ds(pl.multiple_of(block * BK, BK), BK)
                tables = (cos_ref[rows], up_ref[rows], down_ref[rows])
                here = slice(first + at, first + at + BK)
                query = turn(heads_ref[here, :lanes].astype(f32), *tables, 1.0).astype(bf16)
                q_s[rows] = (query.astype(f32) * scale).astype(bf16)
                key = turn(heads_ref[here, lanes : 2 * lanes].astype(f32), *tables, 1.0).astype(bf16)
                k_s[rows] = key
                kt_s[block] = key.astype(f32).T.astype(bf16)
                value = heads_ref[here, 2 * lanes :]
                v_s[rows] = value
                vt_s[block] = value.astype(f32).T.astype(bf16)
                g_s[rows] = back_ref[here]

    rows = pl.ds(pl.multiple_of(step * BQ, BQ), BQ)
    low_lanes = lax.broadcasted_iota(jnp.int32, (BQ, lanes), 1) < HD

    def both(value):
        value = value.astype(f32)
        return jnp.concatenate(
            [jnp.where(low_lanes, value, 0.0), jnp.where(low_lanes, 0.0, value)], axis=0
        ).astype(bf16)

    q_both = both(q_s[rows])
    g_both = both(g_s[rows])

    def keys_at(block):
        return pl.ds(pl.multiple_of(block * BK, BK), BK)

    def score(block):
        return dot(k_s[keys_at(block)], q_both, NT)

    key_row = lax.broadcasted_iota(jnp.int32, (BK, BQ), 0)
    query_col = lax.broadcasted_iota(jnp.int32, (BK, BQ), 1)
    keep = key_row <= query_col
    diagonal = score(step)
    diagonal = jnp.where(jnp.concatenate([keep, keep], axis=1), diagonal, masked_score)
    e_s[step] = diagonal
    top = jnp.max(diagonal, axis=0, keepdims=True)

    def first_pass(block, top):
        value = score(block)
        e_s[block] = value
        return jnp.maximum(top, jnp.max(value, axis=0, keepdims=True))

    top = lax.fori_loop(0, step, first_pass, top)

    def second_pass(block, carry):
        total, inner = carry
        exponent = jnp.exp(e_s[block] - top)
        d_shares = dot(v_s[keys_at(block)], g_both, NT)
        e_s[block] = exponent
        dp_s[block] = d_shares
        total = total + jnp.sum(exponent, axis=0, keepdims=True)
        inner = inner + jnp.sum(exponent * d_shares, axis=0, keepdims=True)
        return total, inner

    zero = jnp.zeros((1, 2 * BQ), f32)
    total, inner = lax.fori_loop(0, step + 1, second_pass, (zero, zero))
    inverse = 1.0 / total
    inner = inner * inverse
    ot_s[...] = jnp.zeros_like(ot_s)
    dqt_s[...] = jnp.zeros_like(dqt_s)

    def third_pass(block, carry):
        shares = e_s[block] * inverse
        low = shares.astype(bf16)
        d_scores = (shares * (dp_s[block] - inner)).astype(bf16)
        at = keys_at(block)
        dv_s[at] += dot(low, g_both, NN)
        dk_s[at] += dot(d_scores, q_both, NN)
        ot_s[...] += dot(vt_s[block], low, NN)
        dqt_s[...] += dot(kt_s[block], d_scores, NN)
        return carry

    lax.fori_loop(0, step + 1, third_pass, 0)

    def joined(ref):
        return jnp.concatenate([ref[:HD, :BQ], ref[HD:, BQ:]], axis=0).T

    o_s[rows] = joined(ot_s).astype(bf16)
    d_query = joined(dqt_s) * scale
    dq_s[rows] = turn(d_query, cos_ref[rows], up_ref[rows], down_ref[rows], -1.0).astype(bf16)

    @pl.when(step == pl.num_programs(0) - 1)
    def _():
        for first, which in ((0, ctx), (half, 1 - ctx)):
            for at in range(0, half, BK):
                here = slice(first + at, first + at + BK)
                rows = pl.ds(pl.multiple_of(which * half + at, BK), BK)
                tables = (cos_ref[rows], up_ref[rows], down_ref[rows])
                heads_out[here, :lanes] = dq_s[rows]
                heads_out[here, lanes : 2 * lanes] = turn(dk_s[rows], *tables, -1.0).astype(bf16)
                heads_out[here, 2 * lanes :] = dv_s[rows].astype(bf16)
                back_out[here] = o_s[rows]


def attend(ctx, heads, back, tables, pair):
    length = heads.shape[0]
    lanes = 2 * HD
    blocks = length // BK
    table = pl.BlockSpec((length, lanes), lambda i: (0, 0))
    return pl.pallas_call(
        attend_kernel,
        grid=(length // BQ,),
        in_specs=[
            pl.BlockSpec(memory_space=pltpu.SMEM),
            pl.BlockSpec((length, 3 * lanes), lambda i: (0, pair)),
            pl.BlockSpec((length, lanes), lambda i: (0, pair)),
            table,
            table,
            table,
        ],
        out_specs=[pl.BlockSpec((length, 3 * lanes), lambda i: (0, 0)), table],
        out_shape=[
            jax.ShapeDtypeStruct((length, 3 * lanes), bf16),
            jax.ShapeDtypeStruct((length, lanes), bf16),
        ],
        scratch_shapes=[pltpu.VMEM((length, lanes), bf16)] * 4
        + [pltpu.VMEM((blocks, lanes, BK), bf16)] * 2
        + [pltpu.VMEM((blocks, BK, 2 * BQ), f32)] * 2
        + [pltpu.VMEM((length, lanes), f32)] * 2
        + [pltpu.VMEM((length, lanes), bf16)] * 2
        + [pltpu.VMEM((lanes, 2 * BQ), f32)] * 2,
        cost_estimate=cost(6 * 4 * length * length * lanes * 2, 16 * length * lanes),
        compiler_params=pltpu.CompilerParams(vmem_limit_bytes=VMEM),
    )(ctx, heads, back, *tables)


def mlp_kernel(normed_ref, back_ref, up_ref, down_ref, bias_ref, act_ref, dh_ref, sum_ref):
    rows = normed_ref.shape[0]
    step = min(512, rows)
    total = jnp.zeros((1, up_ref.shape[1]), f32)
    for at in range(0, rows, step):
        here = slice(at, at + step)
        hidden = dot(normed_ref[here], up_ref[...], NN) + bias_ref[...]
        d_act = dot(back_ref[here], down_ref[...], NN)
        share = 0.5 * (1.0 + lax.erf(hidden * (0.5**0.5)))
        density = jnp.exp(-0.5 * hidden * hidden) * 0.3989422804014327
        act_ref[here] = (hidden * share).astype(bf16)
        d_hidden = (d_act * (share + hidden * density)).astype(bf16)
        dh_ref[here] = d_hidden
        total = total + jnp.sum(d_hidden.astype(f32), axis=0, keepdims=True)
    sum_ref[...] = total


def mlp(normed, back, up, down, bias):
    rows, width = normed.shape
    units = up.shape[1]
    whole = pl.BlockSpec((rows, width), lambda j: (0, 0))
    columns = pl.BlockSpec((width, UNIT_BLOCK), lambda j: (0, j))
    out = pl.BlockSpec((rows, UNIT_BLOCK), lambda j: (0, j))
    line = pl.BlockSpec((1, UNIT_BLOCK), lambda j: (0, j))
    return pl.pallas_call(
        mlp_kernel,
        grid=(units // UNIT_BLOCK,),
        in_specs=[whole, whole, columns, columns, line],
        out_specs=[out, out, line],
        out_shape=[
            jax.ShapeDtypeStruct((rows, units), bf16),
            jax.ShapeDtypeStruct((rows, units), bf16),
            jax.ShapeDtypeStruct((1, units), f32),
        ],
        cost_estimate=cost(12 * rows * width * units, 8 * rows * width),
        compiler_params=pltpu.CompilerParams(vmem_limit_bytes=VMEM),
    )(normed, back, up, down, bias)


def grads_kernel(column_ref, first_ref, second_ref, *refs):
    rights, (kept_ref, sent_ref) = refs[:-2], refs[-2:]
    parts = [dot((first_ref, second_ref)[at % 2][...], ref[...], TN) for at, ref in enumerate(rights)]
    value = jnp.concatenate(parts, axis=1)
    lines, rows, _ = kept_ref.shape
    here = column_ref[0] == 0
    for at in range(lines):
        top, bottom = [value[(2 * at + which) * rows : (2 * at + which + 1) * rows] for which in range(2)]
        kept_ref[at] = jnp.where(here, top, bottom)
        sent_ref[at] = jnp.where(here, bottom, top).astype(bf16)


def grads(column, first, second, rights):
    length, width = first.shape
    rows = width // 8
    cols = sum(right.shape[1] for right in rights)
    left = pl.BlockSpec((length, 4 * rows), lambda i: (0, i))
    out = pl.BlockSpec((2, rows, cols), lambda i: (i, 0, 0))
    return pl.pallas_call(
        grads_kernel,
        grid=(2,),
        in_specs=[pl.BlockSpec(memory_space=pltpu.SMEM), left, left]
        + [pl.BlockSpec(right.shape, lambda i: (0, 0)) for right in rights],
        out_specs=[out, out],
        out_shape=[
            jax.ShapeDtypeStruct((4, rows, cols), f32),
            jax.ShapeDtypeStruct((4, rows, cols), bf16),
        ],
        cost_estimate=cost(0, 6 * width * cols),
        compiler_params=pltpu.CompilerParams(vmem_limit_bytes=VMEM),
    )(column, first, second, *rights)


def combine(line, kept, crossed):
    def kernel(line_ref, kept_ref, crossed_ref, own_ref, *outs):
        for r, out in zip((0, 2, 3, 1), (own_ref,) + outs):
            at = line_ref[0] ^ r
            out[...] = (kept_ref[at] + crossed_ref[at].astype(f32)).astype(out.dtype)

    vmem = pl.BlockSpec(memory_space=pltpu.VMEM)
    shape = kept.shape[1:]
    return pl.pallas_call(
        kernel,
        in_specs=[pl.BlockSpec(memory_space=pltpu.SMEM), vmem, vmem],
        out_specs=[vmem] * 4,
        out_shape=[jax.ShapeDtypeStruct(shape, f32)] + [jax.ShapeDtypeStruct(shape, bf16)] * 3,
        cost_estimate=cost(0, 12 * math.prod(kept.shape)),
        compiler_params=pltpu.CompilerParams(vmem_limit_bytes=VMEM),
    )(line, kept, crossed)


def finish_kernel(
    tp_ref, dh_a, dh_b, o_a, o_b, act_a, act_b, du_a, du_b, tok_ref,
    wh, wd, f1_a, f1_b, f2_a, f2_b, gain_ref, out_ref, norm_ref, line_ref,
):
    cut = dh_a.shape[1]
    lanes = o_a.shape[1]

    @pl.when(pl.program_id(0) == 0)
    def _():
        norm_ref[...] = jnp.zeros_like(norm_ref)
        line_ref[...] = jnp.zeros_like(line_ref)

    out_ref[0] = (
        dot(act_a[...], f2_a[...], NT)
        + dot(act_b[...], f2_b[...], NT)
        + dot(o_a[...], wd[:, :lanes], NT)
        + dot(o_b[...], wd[:, lanes:], NT)
    ).astype(out_ref.dtype)
    one = dot(dh_a[...], wh[:, :cut], NT) + dot(dh_b[...], wh[:, cut:], NT)
    two = dot(du_a[...], f1_a[...], NT) + dot(du_b[...], f1_b[...], NT)
    out_ref[1] = (one * gain_ref[0:1] + two * gain_ref[1:2]).astype(out_ref.dtype)
    tokens = tok_ref[...].astype(f32)
    centre = tokens - jnp.mean(tokens, axis=-1, keepdims=True)
    unit = centre * lax.rsqrt(jnp.mean(centre * centre, axis=-1, keepdims=True) + norm_eps)
    for at, value in enumerate((one * unit, one, two * unit, two)):
        norm_ref[at : at + 1] += jnp.sum(value, axis=0, keepdims=True)
    line_ref[0:1, :cut] += jnp.sum(dh_a[...].astype(f32), axis=0, keepdims=True)
    line_ref[0:1, cut:] += jnp.sum(dh_b[...].astype(f32), axis=0, keepdims=True)


def finish(tp, rowwise, weights, gains, theirs, keep):
    length, width = rowwise[-1].shape
    block = min(512, length // 4)
    heads = weights[0].shape[1]
    steps = length // (4 * block)
    start = 2 * steps if theirs else 0
    kind = f32 if keep else bf16

    def row(i, tp_ref):
        side = tp_ref[0] if keep else 1 - tp_ref[0]
        return start + side * steps + i

    def by_rows(value):
        return pl.BlockSpec((block, value.shape[1]), lambda i, ref: (row(i, ref), 0))

    def fixed(shape):
        return pl.BlockSpec(shape, lambda i, ref: (0, 0))

    out = pl.BlockSpec((2, block, width), lambda i, ref: (0, i, 0))
    return pl.pallas_call(
        finish_kernel,
        grid_spec=pltpu.PrefetchScalarGridSpec(
            num_scalar_prefetch=1,
            grid=(steps,),
            in_specs=[by_rows(value) for value in rowwise]
            + [fixed(value.shape) for value in weights]
            + [fixed(gains.shape)],
            out_specs=[out, fixed((4, width)), fixed((1, heads))],
        ),
        out_shape=[
            jax.ShapeDtypeStruct((2, steps * block, width), kind),
            jax.ShapeDtypeStruct((4, width), f32),
            jax.ShapeDtypeStruct((1, heads), f32),
        ],
        cost_estimate=cost((6 if keep else 0) * length * width * sum(w.shape[1] for w in weights), 4 * length * width),
        compiler_params=pltpu.CompilerParams(vmem_limit_bytes=VMEM),
    )(tp, *rowwise, *weights, gains)


def share_kernel(tp_ref, own_a, other_a, own_b, other_b, out_a, out_b):
    half = own_a.shape[0]
    here = pl.ds(pl.multiple_of(tp_ref[0] * half, half), half)
    there = pl.ds(pl.multiple_of((1 - tp_ref[0]) * half, half), half)
    out_a[here] = own_a[...]
    out_a[there] = other_a[...]
    out_b[here] = own_b[...]
    out_b[there] = other_b[...]


def share(tp, own, other):
    half, width = own[0].shape
    vmem = pl.BlockSpec(memory_space=pltpu.VMEM)
    return pl.pallas_call(
        share_kernel,
        in_specs=[pl.BlockSpec(memory_space=pltpu.SMEM)] + [vmem] * 4,
        out_specs=[vmem] * 2,
        out_shape=[jax.ShapeDtypeStruct((2 * half, width), value.dtype) for value in own],
        cost_estimate=cost(0, 0),
        compiler_params=pltpu.CompilerParams(vmem_limit_bytes=VMEM),
    )(tp, own[0], other[0], own[1], other[1])


def after(value, *others):
    return lax.optimization_barrier((value,) + others)[0] if others else value


def gather_chunk(payload, index, widths):
    line = [swap(payload, "shard", r << 1) for r in (2, 3, 1)]

    def cross(*gates):
        own = jnp.stack([after(payload, *gates), line[2], line[0], line[1]])
        got = swap(own, "shard", 1)

        def build(*gates):
            full = assemble(after(own, *gates), got, index, widths)
            return [value.reshape(-1, value.shape[2]) for value in full]

        return own, build

    return cross


def adam(weight, first, second, gradient, rate, decay):
    first_new = beta_one * first + (1.0 - beta_one) * gradient
    second_new = beta_two * second + (1.0 - beta_two) * gradient * gradient
    scaled = (
        first_new
        / (1.0 - beta_one**STEP)
        / (jnp.sqrt(second_new / (1.0 - beta_two**STEP)) + adam_eps)
    )
    return (first_new, second_new, weight - rate * (scaled + decay * weight))


def adam_store(weight, first, second, gradient, outs, at):
    for ref, value in zip(outs, adam(weight[at], first[at], second[at], gradient, rate_matrix, weight_decay)):
        ref[at] = value


def adam_heads_kernel(ctx_ref, *refs):
    sums, (wq, mq, vq, wd, md, vd), outs = refs[:-12], refs[-12:-6], refs[-6:]
    mine, other = sums
    lanes = 2 * HD
    pairs = mine.shape[1] // (4 * lanes)
    first = ctx_ref[0] == 0
    for pair in range(pairs):
        for plane in range(4):
            cols = slice((4 * pair + plane) * lanes, (4 * pair + plane + 1) * lanes)
            left, right = mine[:, cols], other[:, cols]
            for group, total in enumerate((jnp.where(first, left, right), jnp.where(first, right, left))):
                start = (group * pairs + pair) * lanes
                place = slice(start, start + lanes)
                if plane < 3:
                    adam_store(wq, mq, vq, total, outs[:3], (plane, slice(None), place))
                else:
                    adam_store(wd, md, vd, total.T, outs[3:], (place, slice(None)))


def adam_fc_kernel(ctx_ref, *refs):
    sums, (w1, m1, v1, w2, m2, v2), outs = refs[:-12], refs[-12:-6], refs[-6:]
    chunks = len(sums) // 2
    cut = w1.shape[1] // (2 * chunks)
    tile = 128
    first = ctx_ref[0] == 0
    for chunk in range(chunks):
        mine, other = sums[2 * chunk : 2 * chunk + 2]
        for at in range(0, 2 * cut, tile):
            left, right = mine[:, at : at + tile], other[:, at : at + tile]
            for group, total in enumerate((jnp.where(first, left, right), jnp.where(first, right, left))):
                start = (group * chunks + chunk) * cut + at % cut
                place = slice(start, start + tile)
                if at < cut:
                    adam_store(w1, m1, v1, total, outs[:3], (slice(None), place))
                else:
                    adam_store(w2, m2, v2, total.T, outs[3:], (place, slice(None)))


def adam_matrices(kernel, ctx, sums, states):
    vmem = pl.BlockSpec(memory_space=pltpu.VMEM)
    return pl.pallas_call(
        kernel,
        in_specs=[pl.BlockSpec(memory_space=pltpu.SMEM)] + [vmem] * (len(sums) + 6),
        out_specs=[vmem] * 6,
        out_shape=[jax.ShapeDtypeStruct(value.shape, f32) for value in states],
        cost_estimate=cost(0, 0),
        compiler_params=pltpu.CompilerParams(vmem_limit_bytes=VMEM),
    )(ctx, *sums, *states)


def rope_tables(length, lanes):
    half = ROT // 2
    lane = jnp.arange(lanes, dtype=jnp.int32) % HD
    frequency = rope_base ** (-((lane % half).astype(f32) * 2.0) / ROT)
    angle = jnp.arange(length, dtype=f32)[:, None] * frequency[None, :]
    cosine, sine = jnp.cos(angle), jnp.sin(angle)
    return [
        jnp.where(lane < ROT, cosine, 1.0),
        jnp.where(lane < half, -sine, 0.0),
        jnp.where((lane >= half) & (lane < ROT), sine, 0.0),
    ]


def body(
    inputs, cotangent, w_qkv, m_qkv, v_qkv, w_dense, m_dense, v_dense,
    w_fc1, m_fc1, v_fc1, w_fc2, m_fc2, v_fc2, vectors, m_vectors, v_vectors,
):
    shard = lax.axis_index("shard")
    ctx = lax.axis_index("ctx")
    tp = lax.axis_index("tp")
    shards = lax.axis_size("shard")
    tok_count, width = inputs.shape
    rows = w_qkv.shape[1]
    head_cols = w_qkv.shape[2]
    units = w_fc1.shape[1]
    lanes = 2 * HD
    pairs, chunks = head_cols // (2 * lanes), 2
    own_heads, own_units = head_cols // 2, units // 2
    cut = own_units // chunks
    fc1_rows = FF // D
    count = vectors.shape[0]
    custom = shards == 8
    ctx_ref = ctx.reshape(1).astype(jnp.int32)
    shard_ref = shard.reshape(1).astype(jnp.int32)

    tp_ref = tp.reshape(1).astype(jnp.int32)
    column_ref, line_ref = shard_ref % 2, shard_ref // 2

    def gather(payload, widths):
        if custom:
            return gather_chunk(payload, shard_ref, widths)
        full = lax.all_gather(payload, "shard", axis=0, tiled=True)
        cuts = [sum(widths[:at]) for at in range(len(widths) + 1)]
        return lambda *gates: (full, lambda *gates: [full[:, a:b] for a, b in zip(cuts, cuts[1:])])

    def local_grads(first, rights):
        if custom:
            return grads(column_ref, first, all_back, rights)
        parts = [dot((first, all_back)[at % 2], right, TN) for at, right in enumerate(rights)]
        both = jnp.concatenate(parts, axis=1).astype(bf16)
        return both, both

    def step_across(kept, sent):
        if custom:
            crossed = swap(sent, "shard", 1)
            return combine(line_ref, kept, crossed)
        total = lax.psum_scatter(sent, "shard", scatter_dimension=0, tiled=True).astype(f32)
        return [total]

    def step_along(parts):
        total = parts[0]
        for r, part in zip((2, 3, 1), parts[1:]):
            total = total + swap(part, "shard", r << 1).astype(f32)
        return total

    def exchange_owned(totals, *gates):
        return [(value, swap(after(value, *gates), "ctx", 1)) for value in totals]

    with jax.named_scope("tokens"):
        part = tok_count // 2
        halves = [pick(value.reshape(2, part, width), tp, 0) for value in (inputs, cotangent)]

    with jax.named_scope("gather_params"):
        low_qkv = pick(w_qkv.reshape(3, rows, 2, pairs, lanes), ctx, 2).astype(bf16)
        low_qkv = jnp.transpose(low_qkv, (1, 2, 0, 3)).reshape(rows, pairs * 3 * lanes)
        low_dense = pick(w_dense.reshape(2, own_heads, rows), ctx, 0).astype(bf16).T
        low_fc1 = pick(w_fc1.reshape(rows, 2, own_units), ctx, 1).astype(bf16)
        low_fc2 = pick(w_fc2.reshape(2, own_units, rows), ctx, 0).astype(bf16).T
        low_vectors = jnp.pad(vectors.astype(bf16).T, ((0, 0), (0, 128 - count)))
        payload = jnp.concatenate([low_qkv, low_dense, low_vectors], axis=1)
        own, build = gather(payload, (pairs * 3 * lanes, pairs * lanes, 128))()
    with jax.named_scope("tokens"):
        direct = [swap(halves[0], "ctx", 1)]
        direct.append(swap(after(halves[1], own), "ctx", 1))
        shared_rows = [swap(direct[0], "tp", 1)]

        def whole_sequence(value, at):
            mine, other = direct[at], shared_rows[at]
            return jnp.concatenate(
                [value, jnp.where(tp == 0, mine, other), jnp.where(tp == 0, other, mine)], axis=0
            )

        all_tokens = whole_sequence(inputs, 0)
        tokens = all_tokens.astype(f32)
        centre = tokens - jnp.mean(tokens, axis=-1, keepdims=True)
        inverse = lax.rsqrt(jnp.mean(centre * centre, axis=-1, keepdims=True) + norm_eps)
        shared_rows.append(swap(after(direct[1], inverse), "tp", 1))
        all_back = whole_sequence(cotangent, 1)

    with jax.named_scope("gather_params"):
        full_qkv, full_dense, full_vectors = build()
        payloads = [
            jnp.concatenate([low_fc1[:, c * cut : (c + 1) * cut], low_fc2[:, c * cut : (c + 1) * cut]], axis=1)
            for c in range(chunks)
        ]

    vec_rows = full_vectors[:, :count].T.astype(f32)
    bias_qkv = lax.dynamic_slice_in_dim(vec_rows[0:3], tp * head_cols + ctx * own_heads, own_heads, 1)
    bias_qkv = jnp.swapaxes(bias_qkv.reshape(3, pairs, lanes), 0, 1).reshape(1, -1)
    bias_dense = vec_rows[3]
    bias_fc1 = lax.dynamic_slice_in_dim(
        vec_rows[4 : 4 + fc1_rows].reshape(1, -1), tp * units + ctx * own_units, own_units, 1
    )
    bias_fc2 = vec_rows[4 + fc1_rows]
    gain_one = vec_rows[5 + fc1_rows]
    shift_one = vec_rows[6 + fc1_rows]
    gain_two = vec_rows[7 + fc1_rows]
    shift_two = vec_rows[8 + fc1_rows]

    with jax.named_scope("norm"):
        unit = centre * inverse
        normed_one = (unit * gain_one + shift_one).astype(bf16)
        normed_two = (unit * gain_two + shift_two).astype(bf16)

    tables = rope_tables(2 * tok_count, lanes)
    with jax.named_scope("project"):
        heads = (dot(normed_one, full_qkv, NN) + bias_qkv).astype(bf16)
        heads_back = dot(all_back, full_dense, NN).astype(bf16)

    with jax.named_scope("gather_params"):
        cross_0 = gather(after(payloads[0], own, heads_back), (cut, cut))

    def run_mlp(chunk, build, *gates):
        with jax.named_scope("mlp"):
            up, down = build(*gates)
            full_fc1.append(up)
            full_fc2.append(down)
            return mlp(
                normed_two, all_back, up, down,
                bias_fc1[:, chunk * cut : (chunk + 1) * cut],
            )

    def run_heads(pair, *gates):
        with jax.named_scope("attend"):
            return attend(ctx_ref, heads, after(heads_back, *gates), tables, pair)

    norm_sums, head_lines = [], []

    def run_finish(theirs, keep, *gates):
        with jax.named_scope("finish"):
            rowwise = [d_heads[0], d_heads[1], attended[0], attended[1]]
            rowwise += [act[0], act[1], d_hidden[0], d_hidden[1], all_tokens]
            weights = [full_qkv, full_dense] + full_fc1 + full_fc2
            gains = after(jnp.stack([gain_one, gain_two]), *gates)
            out, norm_sum, head_line = finish(tp_ref, rowwise, weights, gains, theirs, keep)
            norm_sums.append(norm_sum)
            head_lines.append(head_line)
            return out

    d_heads, attended, act, d_hidden, lines_fc1 = [], [], [], [], []
    full_fc1, full_fc2 = [], []

    def keep_heads(results):
        d_heads.append(results[0])
        attended.append(results[1])

    def keep_mlp(results):
        act.append(results[0])
        d_hidden.append(results[1])
        lines_fc1.append(results[2])

    keep_heads(run_heads(0))
    with jax.named_scope("gather_params"):
        own_0, build_0 = cross_0(attended[0])
        cross_1 = gather(after(payloads[1], own_0), (cut, cut))
    keep_heads(run_heads(1, own_0))
    with jax.named_scope("gather_params"):
        own_1, build_1 = cross_1(attended[1])
    keep_mlp(run_mlp(0, build_0, own_1))
    with jax.named_scope("grad_fc"):
        kept_0, sent_0 = local_grads(normed_two, [d_hidden[0], act[0]])
    with jax.named_scope("grad_heads"):
        kept_h, sent_h = local_grads(
            normed_one, [d_heads[0], attended[0], d_heads[1], after(attended[1], sent_0)]
        )
    keep_mlp(run_mlp(1, build_1, sent_h))
    with jax.named_scope("sum_fc"):
        parts_0 = step_across(after(kept_0, act[1]), sent_0)
    theirs_sent = run_finish(True, False, *parts_0)
    with jax.named_scope("finish"):
        theirs_got = swap(theirs_sent, "tp", 1)
    theirs_kept = run_finish(True, True, theirs_sent)
    with jax.named_scope("sum_fc"):
        total_0 = step_along([after(parts_0[0], theirs_kept)] + list(parts_0[1:]))
        (sums_0,) = exchange_owned([total_0])
    with jax.named_scope("sum_heads"):
        parts_h = step_across(after(kept_h, total_0), sent_h)
    with jax.named_scope("finish"):
        theirs_kept = after(theirs_kept, *parts_h)
        low_theirs = [(theirs_kept[at] + theirs_got[at].astype(f32)).astype(bf16) for at in range(2)]
        from_ctx = [swap(value, "ctx", 1) for value in low_theirs]
    with jax.named_scope("grad_fc"):
        kept_1, sent_1 = local_grads(normed_two, [d_hidden[1], after(act[1], *low_theirs)])
    with jax.named_scope("sum_heads"):
        mine_sent = run_finish(False, False, sent_1, sums_0[1])
        total_h = step_along([after(parts_h[0], mine_sent)] + list(parts_h[1:]))
    with jax.named_scope("finish"):
        mine_got = swap(mine_sent, "tp", 1)
    with jax.named_scope("sum_fc"):
        parts_1 = step_across(after(kept_1, mine_sent, from_ctx[0], total_h), sent_1)
    mine_kept = run_finish(False, True, mine_sent, *parts_1)
    with jax.named_scope("sum_fc"):
        (sums_h,) = exchange_owned([total_h], mine_kept)
        total_1 = step_along([after(parts_1[0], mine_kept)] + list(parts_1[1:]))
        (sums_1,) = exchange_owned([total_1])
    heads_states = (w_qkv, m_qkv, v_qkv, w_dense, m_dense, v_dense)
    fc_states = (w_fc1, m_fc1, v_fc1, w_fc2, m_fc2, v_fc2)

    with jax.named_scope("finish"):
        norm_rows = sum(norm_sums)
        head_line = sum(head_lines)
        out_sum, d_unit = [
            mine_kept[at] + mine_got[at].astype(f32) + after(from_ctx[at], total_1).astype(f32)
            for at in range(2)
        ]

        own_tokens, own_back = [after(half, attended[0]).astype(f32) for half in halves]
        outputs = (own_tokens + out_sum + bias_dense + bias_fc2).astype(bf16)
        centre = own_tokens - jnp.mean(own_tokens, axis=-1, keepdims=True)
        inverse = lax.rsqrt(jnp.mean(centre * centre, axis=-1, keepdims=True) + norm_eps)
        unit = centre * inverse
        mean_d = jnp.mean(d_unit, axis=-1, keepdims=True)
        mean_du = jnp.mean(d_unit * unit, axis=-1, keepdims=True)
        input_grad = own_back + inverse * (d_unit - mean_d - unit * mean_du)
        halves = [outputs, input_grad]
        outputs, input_grad = share(tp_ref, halves, [swap(value, "tp", 1) for value in halves])

    if custom:
        with jax.named_scope("adam"):
            heads_results = adam_matrices(adam_heads_kernel, ctx_ref, list(sums_h), heads_states)

    with jax.named_scope("vector_grads"):
        bias_back = jnp.sum(own_back, axis=0)[None]
        head_rows = jnp.swapaxes(head_line.reshape(pairs, 3, lanes), 0, 1).reshape(3, own_heads)
        placed_heads = lax.dynamic_update_slice_in_dim(
            jnp.zeros((3, width), f32), head_rows, tp * head_cols + ctx * own_heads, 1
        )
        placed_fc1 = lax.dynamic_update_slice_in_dim(
            jnp.zeros((1, FF), f32),
            jnp.concatenate(lines_fc1, axis=1),
            tp * units + ctx * own_units,
            1,
        ).reshape(fc1_rows, width)
        vector_grads = jnp.concatenate(
            [placed_heads, bias_back, placed_fc1, bias_back, norm_rows], axis=0
        )
        vector_grads = after(vector_grads, total_1)
        if custom:
            for axis, mask in (("tp", 1), ("shard", 1), ("shard", 2), ("shard", 4), ("ctx", 1)):
                if mask == 2:
                    vector_grads = after(vector_grads, heads_results[0])
                vector_grads = vector_grads + swap(vector_grads, axis, mask)
        else:
            vector_grads = lax.psum(vector_grads, ("shard", "ctx", "tp"))
        owned_vectors = lax.dynamic_slice_in_dim(vector_grads, shard * rows, rows, 1)

    results = [outputs, input_grad]
    head_sums = list(sums_h)
    fc_sums = [*sums_0, *sums_1]
    with jax.named_scope("adam"):
        if custom:
            fc_results = adam_matrices(adam_fc_kernel, ctx_ref, fc_sums, fc_states)
            results += list(heads_results) + list(fc_results)
        else:

            def by_ctx(sums):
                mine, other = jnp.stack(sums[0::2]).astype(f32), jnp.stack(sums[1::2]).astype(f32)
                return jnp.stack([jnp.where(ctx == 0, mine, other), jnp.where(ctx == 0, other, mine)])

            owned = by_ctx(head_sums).reshape(2, rows, pairs, 4, lanes)
            owned = jnp.transpose(owned, (3, 1, 0, 2, 4)).reshape(4, rows, head_cols)
            owned_fc = by_ctx(fc_sums).reshape(2, chunks, rows, 2, cut)
            owned_fc = jnp.transpose(owned_fc, (3, 2, 0, 1, 4)).reshape(2, rows, units)
            for gradient, entry in (
                (owned[:3], heads_states[:3]),
                (owned[3].T, heads_states[3:]),
                (owned_fc[0], fc_states[:3]),
                (owned_fc[1].T, fc_states[3:]),
            ):
                results += adam(*entry, gradient, rate_matrix, weight_decay)
        results += adam(vectors, m_vectors, v_vectors, owned_vectors, rate_vector, 0.0)
    return tuple(results)


def solution(mesh):
    tokens = P(("shard", "ctx"), None)
    layouts = [P(None, "shard", "tp"), P("tp", "shard"), P("shard", "tp"), P("tp", "shard"), P(None, "shard")]
    params = tuple(layout for layout in layouts for _ in range(3))
    return jax.shard_map(
        body,
        mesh=mesh,
        in_specs=(tokens, tokens) + params,
        out_specs=(tokens, tokens) + params,
        check_vma=False,
    )
```

```python
import math

import jax
import jax.numpy as jnp
from jax import lax
from jax.experimental import pallas as pl
from jax.experimental.pallas import tpu as pltpu
from jax.sharding import PartitionSpec as P

D = 1024
HD = 64
ROT = 16
FF = 4096
STEP = 10

norm_eps = 1e-05
rope_base = 10000.0
masked_score = -1e30
beta_one = 0.9
beta_two = 0.95
adam_eps = 1e-08
rate_matrix = 0.05
rate_vector = 0.5
weight_decay = 0.01

BQ = 512
BK = 512
UNIT_BLOCK = 256
VMEM = 56 * 1024 * 1024

bf16 = jnp.bfloat16
f32 = jnp.float32


def dot(a, b, contract):
    return lax.dot_general(a, b, (contract, ((), ())), preferred_element_type=f32)


NN = ((1,), (0,))
NT = ((1,), (1,))
TN = ((0,), (0,))


def cost(flops, moved):
    return pl.CostEstimate(flops=int(flops), bytes_accessed=int(moved), transcendentals=0)


def swap(value, axis, mask):
    return lax.ppermute(value, axis, [(i, i ^ mask) for i in range(lax.axis_size(axis))])


def pick(value, index, axis):
    return lax.dynamic_index_in_dim(value, index, axis, keepdims=False)


def assemble(own, got, index, widths):
    _, rows, cols = own.shape

    def kernel(index_ref, own_ref, got_ref, *outs):
        for which, ref in enumerate((own_ref, got_ref)):
            for r in range(4):
                slot = index_ref[0] ^ ((r << 1) | which)
                start = 0
                for out, width in zip(outs, widths):
                    out[slot] = ref[r, :, start : start + width]
                    start += width

    vmem = pl.BlockSpec(memory_space=pltpu.VMEM)
    return pl.pallas_call(
        kernel,
        in_specs=[pl.BlockSpec(memory_space=pltpu.SMEM), vmem, vmem],
        out_specs=[vmem] * len(widths),
        out_shape=[jax.ShapeDtypeStruct((8, rows, width), bf16) for width in widths],
        cost_estimate=cost(0, 32 * rows * cols),
        compiler_params=pltpu.CompilerParams(vmem_limit_bytes=VMEM),
    )(index, own, got)


def turn(value, cosine, sine_up, sine_down, sign):
    up = pltpu.roll(value, value.shape[1] - ROT // 2, 1)
    down = pltpu.roll(value, ROT // 2, 1)
    return value * cosine + sign * (up * sine_up + down * sine_down)


def attend_kernel(
    ctx_ref, heads_ref, back_ref, cos_ref, up_ref, down_ref, heads_out, back_out,
    q_s, k_s, v_s, g_s, kt_s, vt_s, e_s, dp_s, dk_s, dv_s, dq_s, o_s, ot_s, dqt_s,
):
    step = pl.program_id(0)
    half = back_ref.shape[0] // 2
    lanes = back_ref.shape[1]
    ctx = ctx_ref[0]
    scale = HD ** (-0.5)

    @pl.when(step == 0)
    def _():
        dk_s[...] = jnp.zeros_like(dk_s)
        dv_s[...] = jnp.zeros_like(dv_s)
        for first, which in ((0, ctx), (half, 1 - ctx)):
            for at in range(0, half, BK):
                block = which * (half // BK) + at // BK
                rows = pl.ds(pl.multiple_of(block * BK, BK), BK)
                tables = (cos_ref[rows], up_ref[rows], down_ref[rows])
                here = slice(first + at, first + at + BK)
                query = turn(heads_ref[here, :lanes].astype(f32), *tables, 1.0).astype(bf16)
                q_s[rows] = (query.astype(f32) * scale).astype(bf16)
                key = turn(heads_ref[here, lanes : 2 * lanes].astype(f32), *tables, 1.0).astype(bf16)
                k_s[rows] = key
                kt_s[block] = key.astype(f32).T.astype(bf16)
                value = heads_ref[here, 2 * lanes :]
                v_s[rows] = value
                vt_s[block] = value.astype(f32).T.astype(bf16)
                g_s[rows] = back_ref[here]

    rows = pl.ds(pl.multiple_of(step * BQ, BQ), BQ)
    low_lanes = lax.broadcasted_iota(jnp.int32, (BQ, lanes), 1) < HD

    def both(value):
        value = value.astype(f32)
        return jnp.concatenate(
            [jnp.where(low_lanes, value, 0.0), jnp.where(low_lanes, 0.0, value)], axis=0
        ).astype(bf16)

    q_both = both(q_s[rows])
    g_both = both(g_s[rows])

    def keys_at(block):
        return pl.ds(pl.multiple_of(block * BK, BK), BK)

    def score(block):
        return dot(k_s[keys_at(block)], q_both, NT)

    key_row = lax.broadcasted_iota(jnp.int32, (BK, BQ), 0)
    query_col = lax.broadcasted_iota(jnp.int32, (BK, BQ), 1)
    keep = key_row <= query_col
    diagonal = score(step)
    diagonal = jnp.where(jnp.concatenate([keep, keep], axis=1), diagonal, masked_score)
    e_s[step] = diagonal
    top = jnp.max(diagonal, axis=0, keepdims=True)

    def first_pass(block, top):
        value = score(block)
        e_s[block] = value
        return jnp.maximum(top, jnp.max(value, axis=0, keepdims=True))

    top = lax.fori_loop(0, step, first_pass, top)

    def second_pass(block, carry):
        total, inner = carry
        exponent = jnp.exp(e_s[block] - top)
        d_shares = dot(v_s[keys_at(block)], g_both, NT)
        e_s[block] = exponent
        dp_s[block] = d_shares
        total = total + jnp.sum(exponent, axis=0, keepdims=True)
        inner = inner + jnp.sum(exponent * d_shares, axis=0, keepdims=True)
        return total, inner

    zero = jnp.zeros((1, 2 * BQ), f32)
    total, inner = lax.fori_loop(0, step + 1, second_pass, (zero, zero))
    inverse = 1.0 / total
    inner = inner * inverse
    ot_s[...] = jnp.zeros_like(ot_s)
    dqt_s[...] = jnp.zeros_like(dqt_s)

    def third_pass(block, carry):
        shares = e_s[block] * inverse
        low = shares.astype(bf16)
        d_scores = (shares * (dp_s[block] - inner)).astype(bf16)
        at = keys_at(block)
        dv_s[at] += dot(low, g_both, NN)
        dk_s[at] += dot(d_scores, q_both, NN)
        ot_s[...] += dot(vt_s[block], low, NN)
        dqt_s[...] += dot(kt_s[block], d_scores, NN)
        return carry

    lax.fori_loop(0, step + 1, third_pass, 0)

    def joined(ref):
        return jnp.concatenate([ref[:HD, :BQ], ref[HD:, BQ:]], axis=0).T

    o_s[rows] = joined(ot_s).astype(bf16)
    d_query = joined(dqt_s) * scale
    dq_s[rows] = turn(d_query, cos_ref[rows], up_ref[rows], down_ref[rows], -1.0).astype(bf16)

    @pl.when(step == pl.num_programs(0) - 1)
    def _():
        for first, which in ((0, ctx), (half, 1 - ctx)):
            for at in range(0, half, BK):
                here = slice(first + at, first + at + BK)
                rows = pl.ds(pl.multiple_of(which * half + at, BK), BK)
                tables = (cos_ref[rows], up_ref[rows], down_ref[rows])
                heads_out[here, :lanes] = dq_s[rows]
                heads_out[here, lanes : 2 * lanes] = turn(dk_s[rows], *tables, -1.0).astype(bf16)
                heads_out[here, 2 * lanes :] = dv_s[rows].astype(bf16)
                back_out[here] = o_s[rows]


def attend(ctx, heads, back, tables, pair):
    length = heads.shape[0]
    lanes = 2 * HD
    blocks = length // BK
    table = pl.BlockSpec((length, lanes), lambda i: (0, 0))
    return pl.pallas_call(
        attend_kernel,
        grid=(length // BQ,),
        in_specs=[
            pl.BlockSpec(memory_space=pltpu.SMEM),
            pl.BlockSpec((length, 3 * lanes), lambda i: (0, pair)),
            pl.BlockSpec((length, lanes), lambda i: (0, pair)),
            table,
            table,
            table,
        ],
        out_specs=[pl.BlockSpec((length, 3 * lanes), lambda i: (0, 0)), table],
        out_shape=[
            jax.ShapeDtypeStruct((length, 3 * lanes), bf16),
            jax.ShapeDtypeStruct((length, lanes), bf16),
        ],
        scratch_shapes=[pltpu.VMEM((length, lanes), bf16)] * 4
        + [pltpu.VMEM((blocks, lanes, BK), bf16)] * 2
        + [pltpu.VMEM((blocks, BK, 2 * BQ), f32)] * 2
        + [pltpu.VMEM((length, lanes), f32)] * 2
        + [pltpu.VMEM((length, lanes), bf16)] * 2
        + [pltpu.VMEM((lanes, 2 * BQ), f32)] * 2,
        cost_estimate=cost(6 * 4 * length * length * lanes * 2, 16 * length * lanes),
        compiler_params=pltpu.CompilerParams(vmem_limit_bytes=VMEM),
    )(ctx, heads, back, *tables)


def mlp_kernel(normed_ref, back_ref, up_ref, down_ref, bias_ref, act_ref, dh_ref, sum_ref):
    units = up_ref.shape[1]

    @pl.when(pl.program_id(0) == 0)
    def _():
        sum_ref[...] = jnp.zeros_like(sum_ref)

    for at in range(0, units, UNIT_BLOCK):
        here = slice(at, at + UNIT_BLOCK)
        hidden = dot(normed_ref[...], up_ref[:, here], NN) + bias_ref[:, here]
        d_act = dot(back_ref[...], down_ref[:, here], NN)
        share = 0.5 * (1.0 + lax.erf(hidden * (0.5**0.5)))
        density = jnp.exp(-0.5 * hidden * hidden) * 0.3989422804014327
        act_ref[:, here] = (hidden * share).astype(bf16)
        d_hidden = (d_act * (share + hidden * density)).astype(bf16)
        dh_ref[:, here] = d_hidden
        sum_ref[:, here] += jnp.sum(d_hidden.astype(f32), axis=0, keepdims=True)


def mlp(normed, back, up, down, bias):
    rows, width = normed.shape
    units = up.shape[1]
    block = min(256, rows)
    by_rows = pl.BlockSpec((block, width), lambda i: (i, 0))
    whole = pl.BlockSpec((width, units), lambda i: (0, 0))
    line = pl.BlockSpec((1, units), lambda i: (0, 0))
    out = pl.BlockSpec((block, units), lambda i: (i, 0))
    return pl.pallas_call(
        mlp_kernel,
        grid=(rows // block,),
        in_specs=[by_rows, by_rows, whole, whole, line],
        out_specs=[out, out, line],
        out_shape=[
            jax.ShapeDtypeStruct((rows, units), bf16),
            jax.ShapeDtypeStruct((rows, units), bf16),
            jax.ShapeDtypeStruct((1, units), f32),
        ],
        cost_estimate=cost(12 * rows * width * units, 8 * rows * width),
        compiler_params=pltpu.CompilerParams(vmem_limit_bytes=VMEM),
    )(normed, back, up, down, bias)


def grads_kernel(column_ref, first_ref, second_ref, *refs):
    rights, (kept_ref, sent_ref) = refs[:-2], refs[-2:]
    parts = [dot((first_ref, second_ref)[at % 2][...], ref[...], TN) for at, ref in enumerate(rights)]
    value = jnp.concatenate(parts, axis=1)
    lines, rows, _ = kept_ref.shape
    here = column_ref[0] == 0
    for at in range(lines):
        top, bottom = [value[(2 * at + which) * rows : (2 * at + which + 1) * rows] for which in range(2)]
        kept_ref[at] = jnp.where(here, top, bottom)
        sent_ref[at] = jnp.where(here, bottom, top).astype(bf16)


def grads(column, first, second, rights):
    length, width = first.shape
    rows = width // 8
    cols = sum(right.shape[1] for right in rights)
    left = pl.BlockSpec((length, 4 * rows), lambda i: (0, i))
    out = pl.BlockSpec((2, rows, cols), lambda i: (i, 0, 0))
    return pl.pallas_call(
        grads_kernel,
        grid=(2,),
        in_specs=[pl.BlockSpec(memory_space=pltpu.SMEM), left, left]
        + [pl.BlockSpec(right.shape, lambda i: (0, 0)) for right in rights],
        out_specs=[out, out],
        out_shape=[
            jax.ShapeDtypeStruct((4, rows, cols), f32),
            jax.ShapeDtypeStruct((4, rows, cols), bf16),
        ],
        cost_estimate=cost(0, 6 * width * cols),
        compiler_params=pltpu.CompilerParams(vmem_limit_bytes=VMEM),
    )(column, first, second, *rights)


def combine(line, kept, crossed):
    def kernel(line_ref, kept_ref, crossed_ref, own_ref, *outs):
        for r, out in zip((0, 2, 3, 1), (own_ref,) + outs):
            at = line_ref[0] ^ r
            out[...] = (kept_ref[at] + crossed_ref[at].astype(f32)).astype(out.dtype)

    vmem = pl.BlockSpec(memory_space=pltpu.VMEM)
    shape = kept.shape[1:]
    return pl.pallas_call(
        kernel,
        in_specs=[pl.BlockSpec(memory_space=pltpu.SMEM), vmem, vmem],
        out_specs=[vmem] * 4,
        out_shape=[jax.ShapeDtypeStruct(shape, f32)] + [jax.ShapeDtypeStruct(shape, bf16)] * 3,
        cost_estimate=cost(0, 12 * math.prod(kept.shape)),
        compiler_params=pltpu.CompilerParams(vmem_limit_bytes=VMEM),
    )(line, kept, crossed)


def finish_kernel(
    tp_ref, dh_a, dh_b, o_a, o_b, act_a, act_b, du_a, du_b, tok_ref,
    wh, wd, f1_a, f1_b, f2_a, f2_b, gain_ref, out_ref, norm_ref, line_ref,
):
    cut = dh_a.shape[1]
    lanes = o_a.shape[1]

    @pl.when(pl.program_id(0) == 0)
    def _():
        norm_ref[...] = jnp.zeros_like(norm_ref)
        line_ref[...] = jnp.zeros_like(line_ref)

    out_ref[0] = (
        dot(act_a[...], f2_a[...], NT)
        + dot(act_b[...], f2_b[...], NT)
        + dot(o_a[...], wd[:, :lanes], NT)
        + dot(o_b[...], wd[:, lanes:], NT)
    ).astype(out_ref.dtype)
    one = dot(dh_a[...], wh[:, :cut], NT) + dot(dh_b[...], wh[:, cut:], NT)
    two = dot(du_a[...], f1_a[...], NT) + dot(du_b[...], f1_b[...], NT)
    out_ref[1] = (one * gain_ref[0:1] + two * gain_ref[1:2]).astype(out_ref.dtype)
    tokens = tok_ref[...].astype(f32)
    centre = tokens - jnp.mean(tokens, axis=-1, keepdims=True)
    unit = centre * lax.rsqrt(jnp.mean(centre * centre, axis=-1, keepdims=True) + norm_eps)
    for at, value in enumerate((one * unit, one, two * unit, two)):
        norm_ref[at : at + 1] += jnp.sum(value, axis=0, keepdims=True)
    line_ref[0:1, :cut] += jnp.sum(dh_a[...].astype(f32), axis=0, keepdims=True)
    line_ref[0:1, cut:] += jnp.sum(dh_b[...].astype(f32), axis=0, keepdims=True)


def finish(tp, rowwise, weights, gains, theirs, keep):
    length, width = rowwise[-1].shape
    block = min(256, length // 8)
    heads = weights[0].shape[1]
    steps = length // (4 * block)
    start = 2 * steps if theirs else 0
    kind = f32 if keep else bf16

    def row(i, tp_ref):
        side = tp_ref[0] if keep else 1 - tp_ref[0]
        return start + side * steps + i

    def by_rows(value):
        return pl.BlockSpec((block, value.shape[1]), lambda i, ref: (row(i, ref), 0))

    def fixed(shape):
        return pl.BlockSpec(shape, lambda i, ref: (0, 0))

    out = pl.BlockSpec((2, block, width), lambda i, ref: (0, i, 0))
    return pl.pallas_call(
        finish_kernel,
        grid_spec=pltpu.PrefetchScalarGridSpec(
            num_scalar_prefetch=1,
            grid=(steps,),
            in_specs=[by_rows(value) for value in rowwise]
            + [fixed(value.shape) for value in weights]
            + [fixed(gains.shape)],
            out_specs=[out, fixed((4, width)), fixed((1, heads))],
        ),
        out_shape=[
            jax.ShapeDtypeStruct((2, steps * block, width), kind),
            jax.ShapeDtypeStruct((4, width), f32),
            jax.ShapeDtypeStruct((1, heads), f32),
        ],
        cost_estimate=cost((6 if keep else 0) * length * width * sum(w.shape[1] for w in weights), 4 * length * width),
        compiler_params=pltpu.CompilerParams(vmem_limit_bytes=VMEM),
    )(tp, *rowwise, *weights, gains)


def share_kernel(tp_ref, own_a, other_a, own_b, other_b, out_a, out_b):
    half = own_a.shape[0]
    here = pl.ds(pl.multiple_of(tp_ref[0] * half, half), half)
    there = pl.ds(pl.multiple_of((1 - tp_ref[0]) * half, half), half)
    out_a[here] = own_a[...]
    out_a[there] = other_a[...]
    out_b[here] = own_b[...]
    out_b[there] = other_b[...]


def share(tp, own, other):
    half, width = own[0].shape
    vmem = pl.BlockSpec(memory_space=pltpu.VMEM)
    return pl.pallas_call(
        share_kernel,
        in_specs=[pl.BlockSpec(memory_space=pltpu.SMEM)] + [vmem] * 4,
        out_specs=[vmem] * 2,
        out_shape=[jax.ShapeDtypeStruct((2 * half, width), value.dtype) for value in own],
        cost_estimate=cost(0, 0),
        compiler_params=pltpu.CompilerParams(vmem_limit_bytes=VMEM),
    )(tp, own[0], other[0], own[1], other[1])


def after(value, *others):
    return lax.optimization_barrier((value,) + others)[0] if others else value


def gather_chunk(payload, index, widths):
    line = [swap(payload, "shard", r << 1) for r in (2, 3, 1)]

    def cross(*gates):
        own = jnp.stack([after(payload, *gates), line[2], line[0], line[1]])
        got = swap(own, "shard", 1)

        def build(*gates):
            full = assemble(after(own, *gates), got, index, widths)
            return [value.reshape(-1, value.shape[2]) for value in full]

        return own, build

    return cross


def adam(weight, first, second, gradient, rate, decay):
    first_new = beta_one * first + (1.0 - beta_one) * gradient
    second_new = beta_two * second + (1.0 - beta_two) * gradient * gradient
    scaled = (
        first_new
        / (1.0 - beta_one**STEP)
        / (jnp.sqrt(second_new / (1.0 - beta_two**STEP)) + adam_eps)
    )
    return (first_new, second_new, weight - rate * (scaled + decay * weight))


def adam_store(weight, first, second, gradient, outs, at):
    for ref, value in zip(outs, adam(weight[at], first[at], second[at], gradient, rate_matrix, weight_decay)):
        ref[at] = value


def adam_heads_kernel(ctx_ref, *refs):
    sums, (wq, mq, vq, wd, md, vd), outs = refs[:-12], refs[-12:-6], refs[-6:]
    mine, other = sums
    lanes = 2 * HD
    pairs = mine.shape[1] // (4 * lanes)
    first = ctx_ref[0] == 0
    for pair in range(pairs):
        for plane in range(4):
            cols = slice((4 * pair + plane) * lanes, (4 * pair + plane + 1) * lanes)
            left, right = mine[:, cols], other[:, cols]
            for group, total in enumerate((jnp.where(first, left, right), jnp.where(first, right, left))):
                start = (group * pairs + pair) * lanes
                place = slice(start, start + lanes)
                if plane < 3:
                    adam_store(wq, mq, vq, total, outs[:3], (plane, slice(None), place))
                else:
                    adam_store(wd, md, vd, total.T, outs[3:], (place, slice(None)))


def adam_fc_kernel(ctx_ref, *refs):
    sums, (w1, m1, v1, w2, m2, v2), outs = refs[:-12], refs[-12:-6], refs[-6:]
    chunks = len(sums) // 2
    cut = w1.shape[1] // (2 * chunks)
    tile = 128
    first = ctx_ref[0] == 0
    for chunk in range(chunks):
        mine, other = sums[2 * chunk : 2 * chunk + 2]
        for at in range(0, 2 * cut, tile):
            left, right = mine[:, at : at + tile], other[:, at : at + tile]
            for group, total in enumerate((jnp.where(first, left, right), jnp.where(first, right, left))):
                start = (group * chunks + chunk) * cut + at % cut
                place = slice(start, start + tile)
                if at < cut:
                    adam_store(w1, m1, v1, total, outs[:3], (slice(None), place))
                else:
                    adam_store(w2, m2, v2, total.T, outs[3:], (place, slice(None)))


def adam_matrices(kernel, ctx, sums, states):
    vmem = pl.BlockSpec(memory_space=pltpu.VMEM)
    return pl.pallas_call(
        kernel,
        in_specs=[pl.BlockSpec(memory_space=pltpu.SMEM)] + [vmem] * (len(sums) + 6),
        out_specs=[vmem] * 6,
        out_shape=[jax.ShapeDtypeStruct(value.shape, f32) for value in states],
        cost_estimate=cost(0, 0),
        compiler_params=pltpu.CompilerParams(vmem_limit_bytes=VMEM),
    )(ctx, *sums, *states)


def rope_tables(length, lanes):
    half = ROT // 2
    lane = jnp.arange(lanes, dtype=jnp.int32) % HD
    frequency = rope_base ** (-((lane % half).astype(f32) * 2.0) / ROT)
    angle = jnp.arange(length, dtype=f32)[:, None] * frequency[None, :]
    cosine, sine = jnp.cos(angle), jnp.sin(angle)
    return [
        jnp.where(lane < ROT, cosine, 1.0),
        jnp.where(lane < half, -sine, 0.0),
        jnp.where((lane >= half) & (lane < ROT), sine, 0.0),
    ]


def body(
    inputs, cotangent, w_qkv, m_qkv, v_qkv, w_dense, m_dense, v_dense,
    w_fc1, m_fc1, v_fc1, w_fc2, m_fc2, v_fc2, vectors, m_vectors, v_vectors,
):
    shard = lax.axis_index("shard")
    ctx = lax.axis_index("ctx")
    tp = lax.axis_index("tp")
    shards = lax.axis_size("shard")
    tok_count, width = inputs.shape
    rows = w_qkv.shape[1]
    head_cols = w_qkv.shape[2]
    units = w_fc1.shape[1]
    lanes = 2 * HD
    pairs, chunks = head_cols // (2 * lanes), 2
    own_heads, own_units = head_cols // 2, units // 2
    cut = own_units // chunks
    fc1_rows = FF // D
    count = vectors.shape[0]
    custom = shards == 8
    ctx_ref = ctx.reshape(1).astype(jnp.int32)
    shard_ref = shard.reshape(1).astype(jnp.int32)

    tp_ref = tp.reshape(1).astype(jnp.int32)
    column_ref, line_ref = shard_ref % 2, shard_ref // 2

    def gather(payload, widths):
        if custom:
            return gather_chunk(payload, shard_ref, widths)
        full = lax.all_gather(payload, "shard", axis=0, tiled=True)
        cuts = [sum(widths[:at]) for at in range(len(widths) + 1)]
        return lambda *gates: (full, lambda *gates: [full[:, a:b] for a, b in zip(cuts, cuts[1:])])

    def local_grads(first, rights):
        if custom:
            return grads(column_ref, first, all_back, rights)
        parts = [dot((first, all_back)[at % 2], right, TN) for at, right in enumerate(rights)]
        both = jnp.concatenate(parts, axis=1).astype(bf16)
        return both, both

    def step_across(kept, sent):
        if custom:
            crossed = swap(sent, "shard", 1)
            return combine(line_ref, kept, crossed)
        total = lax.psum_scatter(sent, "shard", scatter_dimension=0, tiled=True).astype(f32)
        return [total]

    def step_along(parts):
        total = parts[0]
        for r, part in zip((2, 3, 1), parts[1:]):
            total = total + swap(part, "shard", r << 1).astype(f32)
        return total

    def exchange_owned(totals, *gates):
        return [(value, swap(after(value, *gates), "ctx", 1)) for value in totals]

    with jax.named_scope("tokens"):
        part = tok_count // 2
        halves = [pick(value.reshape(2, part, width), tp, 0) for value in (inputs, cotangent)]

    with jax.named_scope("gather_params"):
        low_qkv = pick(w_qkv.reshape(3, rows, 2, pairs, lanes), ctx, 2).astype(bf16)
        low_qkv = jnp.transpose(low_qkv, (1, 2, 0, 3)).reshape(rows, pairs * 3 * lanes)
        low_dense = pick(w_dense.reshape(2, own_heads, rows), ctx, 0).astype(bf16).T
        low_fc1 = pick(w_fc1.reshape(rows, 2, own_units), ctx, 1).astype(bf16)
        low_fc2 = pick(w_fc2.reshape(2, own_units, rows), ctx, 0).astype(bf16).T
        low_vectors = jnp.pad(vectors.astype(bf16).T, ((0, 0), (0, 128 - count)))
        payload = jnp.concatenate([low_qkv, low_dense, low_vectors], axis=1)
        own, build = gather(payload, (pairs * 3 * lanes, pairs * lanes, 128))()
    with jax.named_scope("tokens"):
        direct = [swap(halves[0], "ctx", 1)]
        direct.append(swap(after(halves[1], own), "ctx", 1))
        shared_rows = [swap(direct[0], "tp", 1)]

        def whole_sequence(value, at):
            mine, other = direct[at], shared_rows[at]
            return jnp.concatenate(
                [value, jnp.where(tp == 0, mine, other), jnp.where(tp == 0, other, mine)], axis=0
            )

        all_tokens = whole_sequence(inputs, 0)
        tokens = all_tokens.astype(f32)
        centre = tokens - jnp.mean(tokens, axis=-1, keepdims=True)
        inverse = lax.rsqrt(jnp.mean(centre * centre, axis=-1, keepdims=True) + norm_eps)
        shared_rows.append(swap(after(direct[1], inverse), "tp", 1))
        all_back = whole_sequence(cotangent, 1)

    with jax.named_scope("gather_params"):
        full_qkv, full_dense, full_vectors = build()
        payloads = [
            jnp.concatenate([low_fc1[:, c * cut : (c + 1) * cut], low_fc2[:, c * cut : (c + 1) * cut]], axis=1)
            for c in range(chunks)
        ]

    vec_rows = full_vectors[:, :count].T.astype(f32)
    bias_qkv = lax.dynamic_slice_in_dim(vec_rows[0:3], tp * head_cols + ctx * own_heads, own_heads, 1)
    bias_qkv = jnp.swapaxes(bias_qkv.reshape(3, pairs, lanes), 0, 1).reshape(1, -1)
    bias_dense = vec_rows[3]
    bias_fc1 = lax.dynamic_slice_in_dim(
        vec_rows[4 : 4 + fc1_rows].reshape(1, -1), tp * units + ctx * own_units, own_units, 1
    )
    bias_fc2 = vec_rows[4 + fc1_rows]
    gain_one = vec_rows[5 + fc1_rows]
    shift_one = vec_rows[6 + fc1_rows]
    gain_two = vec_rows[7 + fc1_rows]
    shift_two = vec_rows[8 + fc1_rows]

    with jax.named_scope("norm"):
        unit = centre * inverse
        normed_one = (unit * gain_one + shift_one).astype(bf16)
        normed_two = (unit * gain_two + shift_two).astype(bf16)

    tables = rope_tables(2 * tok_count, lanes)
    with jax.named_scope("project"):
        heads = (dot(normed_one, full_qkv, NN) + bias_qkv).astype(bf16)
        heads_back = dot(all_back, full_dense, NN).astype(bf16)

    with jax.named_scope("gather_params"):
        cross_0 = gather(after(payloads[0], own, heads_back), (cut, cut))

    def run_mlp(chunk, build, *gates):
        with jax.named_scope("mlp"):
            up, down = build(*gates)
            full_fc1.append(up)
            full_fc2.append(down)
            return mlp(
                normed_two, all_back, up, down,
                bias_fc1[:, chunk * cut : (chunk + 1) * cut],
            )

    def run_heads(pair, *gates):
        with jax.named_scope("attend"):
            return attend(ctx_ref, heads, after(heads_back, *gates), tables, pair)

    norm_sums, head_lines = [], []

    def run_finish(theirs, keep, *gates):
        with jax.named_scope("finish"):
            rowwise = [d_heads[0], d_heads[1], attended[0], attended[1]]
            rowwise += [act[0], act[1], d_hidden[0], d_hidden[1], all_tokens]
            weights = [full_qkv, full_dense] + full_fc1 + full_fc2
            gains = after(jnp.stack([gain_one, gain_two]), *gates)
            out, norm_sum, head_line = finish(tp_ref, rowwise, weights, gains, theirs, keep)
            norm_sums.append(norm_sum)
            head_lines.append(head_line)
            return out

    d_heads, attended, act, d_hidden, lines_fc1 = [], [], [], [], []
    full_fc1, full_fc2 = [], []

    def keep_heads(results):
        d_heads.append(results[0])
        attended.append(results[1])

    def keep_mlp(results):
        act.append(results[0])
        d_hidden.append(results[1])
        lines_fc1.append(results[2])

    keep_heads(run_heads(0))
    with jax.named_scope("gather_params"):
        own_0, build_0 = cross_0(attended[0])
        cross_1 = gather(after(payloads[1], own_0), (cut, cut))
    keep_heads(run_heads(1, own_0))
    with jax.named_scope("gather_params"):
        own_1, build_1 = cross_1(attended[1])
    keep_mlp(run_mlp(0, build_0, own_1))
    with jax.named_scope("grad_fc"):
        kept_0, sent_0 = local_grads(normed_two, [d_hidden[0], act[0]])
    with jax.named_scope("grad_heads"):
        kept_h, sent_h = local_grads(
            normed_one, [d_heads[0], attended[0], d_heads[1], after(attended[1], sent_0)]
        )
    keep_mlp(run_mlp(1, build_1, sent_h))
    with jax.named_scope("sum_fc"):
        parts_0 = step_across(after(kept_0, act[1]), sent_0)
    theirs_sent = run_finish(True, False, *parts_0)
    with jax.named_scope("finish"):
        theirs_got = swap(theirs_sent, "tp", 1)
    theirs_kept = run_finish(True, True, theirs_sent)
    with jax.named_scope("sum_fc"):
        total_0 = step_along([after(parts_0[0], theirs_kept)] + list(parts_0[1:]))
        (sums_0,) = exchange_owned([total_0])
    with jax.named_scope("sum_heads"):
        parts_h = step_across(after(kept_h, total_0), sent_h)
    with jax.named_scope("finish"):
        theirs_kept = after(theirs_kept, *parts_h)
        low_theirs = [(theirs_kept[at] + theirs_got[at].astype(f32)).astype(bf16) for at in range(2)]
        from_ctx = [swap(value, "ctx", 1) for value in low_theirs]
    with jax.named_scope("grad_fc"):
        kept_1, sent_1 = local_grads(normed_two, [d_hidden[1], after(act[1], *low_theirs)])
    with jax.named_scope("sum_heads"):
        mine_sent = run_finish(False, False, sent_1, sums_0[1])
        total_h = step_along([after(parts_h[0], mine_sent)] + list(parts_h[1:]))
    with jax.named_scope("finish"):
        mine_got = swap(mine_sent, "tp", 1)
    with jax.named_scope("sum_fc"):
        parts_1 = step_across(after(kept_1, mine_sent, from_ctx[0], total_h), sent_1)
    mine_kept = run_finish(False, True, mine_sent, *parts_1)
    with jax.named_scope("sum_fc"):
        (sums_h,) = exchange_owned([total_h], mine_kept)
        total_1 = step_along([after(parts_1[0], mine_kept)] + list(parts_1[1:]))
        (sums_1,) = exchange_owned([total_1])
    heads_states = (w_qkv, m_qkv, v_qkv, w_dense, m_dense, v_dense)
    fc_states = (w_fc1, m_fc1, v_fc1, w_fc2, m_fc2, v_fc2)

    with jax.named_scope("finish"):
        norm_rows = sum(norm_sums)
        head_line = sum(head_lines)
        out_sum, d_unit = [
            mine_kept[at] + mine_got[at].astype(f32) + after(from_ctx[at], *gates).astype(f32)
            for at, gates in ((0, ()), (1, (total_1,)))
        ]

        own_tokens, own_back = [after(half, attended[0]).astype(f32) for half in halves]
        outputs = (own_tokens + out_sum + bias_dense + bias_fc2).astype(bf16)
        centre = own_tokens - jnp.mean(own_tokens, axis=-1, keepdims=True)
        inverse = lax.rsqrt(jnp.mean(centre * centre, axis=-1, keepdims=True) + norm_eps)
        unit = centre * inverse
        mean_d = jnp.mean(d_unit, axis=-1, keepdims=True)
        mean_du = jnp.mean(d_unit * unit, axis=-1, keepdims=True)
        input_grad = own_back + inverse * (d_unit - mean_d - unit * mean_du)
        halves = [outputs, input_grad]
        outputs, input_grad = share(tp_ref, halves, [swap(value, "tp", 1) for value in halves])

    if custom:
        with jax.named_scope("adam"):
            heads_results = adam_matrices(adam_heads_kernel, ctx_ref, list(sums_h), heads_states)

    with jax.named_scope("vector_grads"):
        bias_back = jnp.sum(own_back, axis=0)[None]
        head_rows = jnp.swapaxes(head_line.reshape(pairs, 3, lanes), 0, 1).reshape(3, own_heads)
        placed_heads = lax.dynamic_update_slice_in_dim(
            jnp.zeros((3, width), f32), head_rows, tp * head_cols + ctx * own_heads, 1
        )
        placed_fc1 = lax.dynamic_update_slice_in_dim(
            jnp.zeros((1, FF), f32),
            jnp.concatenate(lines_fc1, axis=1),
            tp * units + ctx * own_units,
            1,
        ).reshape(fc1_rows, width)
        vector_grads = jnp.concatenate(
            [placed_heads, bias_back, placed_fc1, bias_back, norm_rows], axis=0
        )
        vector_grads = after(vector_grads, total_1)
        if custom:
            for axis, mask in (("tp", 1), ("shard", 1), ("shard", 2), ("shard", 4), ("ctx", 1)):
                vector_grads = vector_grads + swap(vector_grads, axis, mask)
        else:
            vector_grads = lax.psum(vector_grads, ("shard", "ctx", "tp"))
        owned_vectors = lax.dynamic_slice_in_dim(vector_grads, shard * rows, rows, 1)

    results = [outputs, input_grad]
    head_sums = list(sums_h)
    fc_sums = [*sums_0, *sums_1]
    with jax.named_scope("adam"):
        if custom:
            fc_results = adam_matrices(adam_fc_kernel, ctx_ref, fc_sums, fc_states)
            results += list(heads_results) + list(fc_results)
        else:

            def by_ctx(sums):
                mine, other = jnp.stack(sums[0::2]).astype(f32), jnp.stack(sums[1::2]).astype(f32)
                return jnp.stack([jnp.where(ctx == 0, mine, other), jnp.where(ctx == 0, other, mine)])

            owned = by_ctx(head_sums).reshape(2, rows, pairs, 4, lanes)
            owned = jnp.transpose(owned, (3, 1, 0, 2, 4)).reshape(4, rows, head_cols)
            owned_fc = by_ctx(fc_sums).reshape(2, chunks, rows, 2, cut)
            owned_fc = jnp.transpose(owned_fc, (3, 2, 0, 1, 4)).reshape(2, rows, units)
            for gradient, entry in (
                (owned[:3], heads_states[:3]),
                (owned[3].T, heads_states[3:]),
                (owned_fc[0], fc_states[:3]),
                (owned_fc[1].T, fc_states[3:]),
            ):
                results += adam(*entry, gradient, rate_matrix, weight_decay)
        results += adam(vectors, m_vectors, v_vectors, owned_vectors, rate_vector, 0.0)
    return tuple(results)


def solution(mesh):
    tokens = P(("shard", "ctx"), None)
    layouts = [P(None, "shard", "tp"), P("tp", "shard"), P("shard", "tp"), P("tp", "shard"), P(None, "shard")]
    params = tuple(layout for layout in layouts for _ in range(3))
    return jax.shard_map(
        body,
        mesh=mesh,
        in_specs=(tokens, tokens) + params,
        out_specs=(tokens, tokens) + params,
        check_vma=False,
    )
```

```python
import math

import jax
import jax.numpy as jnp
from jax import lax
from jax.experimental import pallas as pl
from jax.experimental.pallas import tpu as pltpu
from jax.sharding import PartitionSpec as P

D = 1024
HD = 64
ROT = 16
FF = 4096
STEP = 10

norm_eps = 1e-05
rope_base = 10000.0
masked_score = -1e30
beta_one = 0.9
beta_two = 0.95
adam_eps = 1e-08
rate_matrix = 0.05
rate_vector = 0.5
weight_decay = 0.01

BQ = 512
BK = 512
UNIT_BLOCK = 256
VMEM = 56 * 1024 * 1024

bf16 = jnp.bfloat16
f32 = jnp.float32


def dot(a, b, contract):
    return lax.dot_general(a, b, (contract, ((), ())), preferred_element_type=f32)


NN = ((1,), (0,))
NT = ((1,), (1,))
TN = ((0,), (0,))


def cost(flops, moved):
    return pl.CostEstimate(flops=int(flops), bytes_accessed=int(moved), transcendentals=0)


def swap(value, axis, mask):
    return lax.ppermute(value, axis, [(i, i ^ mask) for i in range(lax.axis_size(axis))])


def pick(value, index, axis):
    return lax.dynamic_index_in_dim(value, index, axis, keepdims=False)


def assemble(own, got, index, widths):
    _, rows, cols = own.shape

    def kernel(index_ref, own_ref, got_ref, *outs):
        for which, ref in enumerate((own_ref, got_ref)):
            for r in range(4):
                slot = index_ref[0] ^ ((r << 1) | which)
                start = 0
                for out, width in zip(outs, widths):
                    out[slot] = ref[r, :, start : start + width]
                    start += width

    vmem = pl.BlockSpec(memory_space=pltpu.VMEM)
    return pl.pallas_call(
        kernel,
        in_specs=[pl.BlockSpec(memory_space=pltpu.SMEM), vmem, vmem],
        out_specs=[vmem] * len(widths),
        out_shape=[jax.ShapeDtypeStruct((8, rows, width), bf16) for width in widths],
        cost_estimate=cost(0, 32 * rows * cols),
        compiler_params=pltpu.CompilerParams(vmem_limit_bytes=VMEM),
    )(index, own, got)


def turn(value, cosine, sine_up, sine_down, sign):
    up = pltpu.roll(value, value.shape[1] - ROT // 2, 1)
    down = pltpu.roll(value, ROT // 2, 1)
    return value * cosine + sign * (up * sine_up + down * sine_down)


def attend_kernel(
    ctx_ref, heads_ref, back_ref, cos_ref, up_ref, down_ref, heads_out, back_out,
    q_s, k_s, v_s, g_s, kt_s, vt_s, e_s, dp_s, dk_s, dv_s, dq_s, o_s, ot_s, dqt_s,
):
    step = pl.program_id(0)
    half = back_ref.shape[0] // 2
    lanes = back_ref.shape[1]
    ctx = ctx_ref[0]
    scale = HD ** (-0.5)

    @pl.when(step == 0)
    def _():
        dk_s[...] = jnp.zeros_like(dk_s)
        dv_s[...] = jnp.zeros_like(dv_s)
        for first, which in ((0, ctx), (half, 1 - ctx)):
            for at in range(0, half, BK):
                block = which * (half // BK) + at // BK
                rows = pl.ds(pl.multiple_of(block * BK, BK), BK)
                tables = (cos_ref[rows], up_ref[rows], down_ref[rows])
                here = slice(first + at, first + at + BK)
                query = turn(heads_ref[here, :lanes].astype(f32), *tables, 1.0).astype(bf16)
                q_s[rows] = (query.astype(f32) * scale).astype(bf16)
                key = turn(heads_ref[here, lanes : 2 * lanes].astype(f32), *tables, 1.0).astype(bf16)
                k_s[rows] = key
                kt_s[block] = key.astype(f32).T.astype(bf16)
                value = heads_ref[here, 2 * lanes :]
                v_s[rows] = value
                vt_s[block] = value.astype(f32).T.astype(bf16)
                g_s[rows] = back_ref[here]

    rows = pl.ds(pl.multiple_of(step * BQ, BQ), BQ)
    low_lanes = lax.broadcasted_iota(jnp.int32, (BQ, lanes), 1) < HD

    def both(value):
        value = value.astype(f32)
        return jnp.concatenate(
            [jnp.where(low_lanes, value, 0.0), jnp.where(low_lanes, 0.0, value)], axis=0
        ).astype(bf16)

    q_both = both(q_s[rows])
    g_both = both(g_s[rows])

    def keys_at(block):
        return pl.ds(pl.multiple_of(block * BK, BK), BK)

    def score(block):
        return dot(k_s[keys_at(block)], q_both, NT)

    key_row = lax.broadcasted_iota(jnp.int32, (BK, BQ), 0)
    query_col = lax.broadcasted_iota(jnp.int32, (BK, BQ), 1)
    keep = key_row <= query_col
    diagonal = score(step)
    diagonal = jnp.where(jnp.concatenate([keep, keep], axis=1), diagonal, masked_score)
    e_s[step] = diagonal
    top = jnp.max(diagonal, axis=0, keepdims=True)

    def first_pass(block, top):
        value = score(block)
        e_s[block] = value
        return jnp.maximum(top, jnp.max(value, axis=0, keepdims=True))

    top = lax.fori_loop(0, step, first_pass, top)

    def second_pass(block, carry):
        total, inner = carry
        exponent = jnp.exp(e_s[block] - top)
        d_shares = dot(v_s[keys_at(block)], g_both, NT)
        e_s[block] = exponent
        dp_s[block] = d_shares
        total = total + jnp.sum(exponent, axis=0, keepdims=True)
        inner = inner + jnp.sum(exponent * d_shares, axis=0, keepdims=True)
        return total, inner

    zero = jnp.zeros((1, 2 * BQ), f32)
    total, inner = lax.fori_loop(0, step + 1, second_pass, (zero, zero))
    inverse = 1.0 / total
    inner = inner * inverse
    ot_s[...] = jnp.zeros_like(ot_s)
    dqt_s[...] = jnp.zeros_like(dqt_s)

    def third_pass(block, carry):
        shares = e_s[block] * inverse
        low = shares.astype(bf16)
        d_scores = (shares * (dp_s[block] - inner)).astype(bf16)
        at = keys_at(block)
        dv_s[at] += dot(low, g_both, NN)
        dk_s[at] += dot(d_scores, q_both, NN)
        ot_s[...] += dot(vt_s[block], low, NN)
        dqt_s[...] += dot(kt_s[block], d_scores, NN)
        return carry

    lax.fori_loop(0, step + 1, third_pass, 0)

    def joined(ref):
        return jnp.concatenate([ref[:HD, :BQ], ref[HD:, BQ:]], axis=0).T

    o_s[rows] = joined(ot_s).astype(bf16)
    d_query = joined(dqt_s) * scale
    dq_s[rows] = turn(d_query, cos_ref[rows], up_ref[rows], down_ref[rows], -1.0).astype(bf16)

    @pl.when(step == pl.num_programs(0) - 1)
    def _():
        for first, which in ((0, ctx), (half, 1 - ctx)):
            for at in range(0, half, BK):
                here = slice(first + at, first + at + BK)
                rows = pl.ds(pl.multiple_of(which * half + at, BK), BK)
                tables = (cos_ref[rows], up_ref[rows], down_ref[rows])
                heads_out[here, :lanes] = dq_s[rows]
                heads_out[here, lanes : 2 * lanes] = turn(dk_s[rows], *tables, -1.0).astype(bf16)
                heads_out[here, 2 * lanes :] = dv_s[rows].astype(bf16)
                back_out[here] = o_s[rows]


def attend(ctx, heads, back, tables, pair):
    length = heads.shape[0]
    lanes = 2 * HD
    blocks = length // BK
    table = pl.BlockSpec((length, lanes), lambda i: (0, 0))
    return pl.pallas_call(
        attend_kernel,
        grid=(length // BQ,),
        in_specs=[
            pl.BlockSpec(memory_space=pltpu.SMEM),
            pl.BlockSpec((length, 3 * lanes), lambda i: (0, pair)),
            pl.BlockSpec((length, lanes), lambda i: (0, pair)),
            table,
            table,
            table,
        ],
        out_specs=[pl.BlockSpec((length, 3 * lanes), lambda i: (0, 0)), table],
        out_shape=[
            jax.ShapeDtypeStruct((length, 3 * lanes), bf16),
            jax.ShapeDtypeStruct((length, lanes), bf16),
        ],
        scratch_shapes=[pltpu.VMEM((length, lanes), bf16)] * 4
        + [pltpu.VMEM((blocks, lanes, BK), bf16)] * 2
        + [pltpu.VMEM((blocks, BK, 2 * BQ), f32)] * 2
        + [pltpu.VMEM((length, lanes), f32)] * 2
        + [pltpu.VMEM((length, lanes), bf16)] * 2
        + [pltpu.VMEM((lanes, 2 * BQ), f32)] * 2,
        cost_estimate=cost(6 * 4 * length * length * lanes * 2, 16 * length * lanes),
        compiler_params=pltpu.CompilerParams(vmem_limit_bytes=VMEM),
    )(ctx, heads, back, *tables)


def mlp_kernel(normed_ref, back_ref, up_ref, down_ref, bias_ref, act_ref, dh_ref, sum_ref):
    units = up_ref.shape[1]

    @pl.when(pl.program_id(0) == 0)
    def _():
        sum_ref[...] = jnp.zeros_like(sum_ref)

    for at in range(0, units, UNIT_BLOCK):
        here = slice(at, at + UNIT_BLOCK)
        hidden = dot(normed_ref[...], up_ref[:, here], NN) + bias_ref[:, here]
        d_act = dot(back_ref[...], down_ref[:, here], NN)
        share = 0.5 * (1.0 + lax.erf(hidden * (0.5**0.5)))
        density = jnp.exp(-0.5 * hidden * hidden) * 0.3989422804014327
        act_ref[:, here] = (hidden * share).astype(bf16)
        d_hidden = (d_act * (share + hidden * density)).astype(bf16)
        dh_ref[:, here] = d_hidden
        sum_ref[:, here] += jnp.sum(d_hidden.astype(f32), axis=0, keepdims=True)


def mlp(normed, back, up, down, bias):
    rows, width = normed.shape
    units = up.shape[1]
    block = min(256, rows)
    by_rows = pl.BlockSpec((block, width), lambda i: (i, 0))
    whole = pl.BlockSpec((width, units), lambda i: (0, 0))
    line = pl.BlockSpec((1, units), lambda i: (0, 0))
    out = pl.BlockSpec((block, units), lambda i: (i, 0))
    return pl.pallas_call(
        mlp_kernel,
        grid=(rows // block,),
        in_specs=[by_rows, by_rows, whole, whole, line],
        out_specs=[out, out, line],
        out_shape=[
            jax.ShapeDtypeStruct((rows, units), bf16),
            jax.ShapeDtypeStruct((rows, units), bf16),
            jax.ShapeDtypeStruct((1, units), f32),
        ],
        cost_estimate=cost(12 * rows * width * units, 8 * rows * width),
        compiler_params=pltpu.CompilerParams(vmem_limit_bytes=VMEM),
    )(normed, back, up, down, bias)


def grads_kernel(column_ref, first_ref, second_ref, *refs):
    rights, (kept_ref, sent_ref) = refs[:-2], refs[-2:]
    parts = [dot((first_ref, second_ref)[at % 2][...], ref[...], TN) for at, ref in enumerate(rights)]
    value = jnp.concatenate(parts, axis=1)
    lines, rows, _ = kept_ref.shape
    here = column_ref[0] == 0
    for at in range(lines):
        top, bottom = [value[(2 * at + which) * rows : (2 * at + which + 1) * rows] for which in range(2)]
        kept_ref[at] = jnp.where(here, top, bottom)
        sent_ref[at] = jnp.where(here, bottom, top).astype(bf16)


def grads(column, first, second, rights):
    length, width = first.shape
    rows = width // 8
    cols = sum(right.shape[1] for right in rights)
    left = pl.BlockSpec((length, 4 * rows), lambda i: (0, i))
    out = pl.BlockSpec((2, rows, cols), lambda i: (i, 0, 0))
    return pl.pallas_call(
        grads_kernel,
        grid=(2,),
        in_specs=[pl.BlockSpec(memory_space=pltpu.SMEM), left, left]
        + [pl.BlockSpec(right.shape, lambda i: (0, 0)) for right in rights],
        out_specs=[out, out],
        out_shape=[
            jax.ShapeDtypeStruct((4, rows, cols), f32),
            jax.ShapeDtypeStruct((4, rows, cols), bf16),
        ],
        cost_estimate=cost(0, 6 * width * cols),
        compiler_params=pltpu.CompilerParams(vmem_limit_bytes=VMEM),
    )(column, first, second, *rights)


def combine(line, kept, crossed):
    def kernel(line_ref, kept_ref, crossed_ref, own_ref, *outs):
        for r, out in zip((0, 2, 3, 1), (own_ref,) + outs):
            at = line_ref[0] ^ r
            out[...] = (kept_ref[at] + crossed_ref[at].astype(f32)).astype(out.dtype)

    vmem = pl.BlockSpec(memory_space=pltpu.VMEM)
    shape = kept.shape[1:]
    return pl.pallas_call(
        kernel,
        in_specs=[pl.BlockSpec(memory_space=pltpu.SMEM), vmem, vmem],
        out_specs=[vmem] * 4,
        out_shape=[jax.ShapeDtypeStruct(shape, f32)] + [jax.ShapeDtypeStruct(shape, bf16)] * 3,
        cost_estimate=cost(0, 12 * math.prod(kept.shape)),
        compiler_params=pltpu.CompilerParams(vmem_limit_bytes=VMEM),
    )(line, kept, crossed)


def finish_kernel(
    tp_ref, dh_a, dh_b, o_a, o_b, act_a, act_b, du_a, du_b, tok_ref,
    wh, wd, f1_a, f1_b, f2_a, f2_b, gain_ref, out_ref, norm_ref, line_ref,
):
    cut = dh_a.shape[1]
    lanes = o_a.shape[1]

    @pl.when(pl.program_id(0) == 0)
    def _():
        norm_ref[...] = jnp.zeros_like(norm_ref)
        line_ref[...] = jnp.zeros_like(line_ref)

    out_ref[0] = (
        dot(act_a[...], f2_a[...], NT)
        + dot(act_b[...], f2_b[...], NT)
        + dot(o_a[...], wd[:, :lanes], NT)
        + dot(o_b[...], wd[:, lanes:], NT)
    ).astype(out_ref.dtype)
    one = dot(dh_a[...], wh[:, :cut], NT) + dot(dh_b[...], wh[:, cut:], NT)
    two = dot(du_a[...], f1_a[...], NT) + dot(du_b[...], f1_b[...], NT)
    out_ref[1] = (one * gain_ref[0:1] + two * gain_ref[1:2]).astype(out_ref.dtype)
    tokens = tok_ref[...].astype(f32)
    centre = tokens - jnp.mean(tokens, axis=-1, keepdims=True)
    unit = centre * lax.rsqrt(jnp.mean(centre * centre, axis=-1, keepdims=True) + norm_eps)
    for at, value in enumerate((one * unit, one, two * unit, two)):
        norm_ref[at : at + 1] += jnp.sum(value, axis=0, keepdims=True)
    line_ref[0:1, :cut] += jnp.sum(dh_a[...].astype(f32), axis=0, keepdims=True)
    line_ref[0:1, cut:] += jnp.sum(dh_b[...].astype(f32), axis=0, keepdims=True)


def finish(tp, rowwise, weights, gains, theirs, keep):
    length, width = rowwise[-1].shape
    block = min(256, length // 8)
    heads = weights[0].shape[1]
    steps = length // (4 * block)
    start = 2 * steps if theirs else 0
    kind = f32 if keep else bf16

    def row(i, tp_ref):
        side = tp_ref[0] if keep else 1 - tp_ref[0]
        return start + side * steps + i

    def by_rows(value):
        return pl.BlockSpec((block, value.shape[1]), lambda i, ref: (row(i, ref), 0))

    def fixed(shape):
        return pl.BlockSpec(shape, lambda i, ref: (0, 0))

    out = pl.BlockSpec((2, block, width), lambda i, ref: (0, i, 0))
    return pl.pallas_call(
        finish_kernel,
        grid_spec=pltpu.PrefetchScalarGridSpec(
            num_scalar_prefetch=1,
            grid=(steps,),
            in_specs=[by_rows(value) for value in rowwise]
            + [fixed(value.shape) for value in weights]
            + [fixed(gains.shape)],
            out_specs=[out, fixed((4, width)), fixed((1, heads))],
        ),
        out_shape=[
            jax.ShapeDtypeStruct((2, steps * block, width), kind),
            jax.ShapeDtypeStruct((4, width), f32),
            jax.ShapeDtypeStruct((1, heads), f32),
        ],
        cost_estimate=cost((6 if keep else 0) * length * width * sum(w.shape[1] for w in weights), 4 * length * width),
        compiler_params=pltpu.CompilerParams(vmem_limit_bytes=VMEM),
    )(tp, *rowwise, *weights, gains)


def share_kernel(tp_ref, own_a, other_a, own_b, other_b, out_a, out_b):
    half = own_a.shape[0]
    here = pl.ds(pl.multiple_of(tp_ref[0] * half, half), half)
    there = pl.ds(pl.multiple_of((1 - tp_ref[0]) * half, half), half)
    out_a[here] = own_a[...]
    out_a[there] = other_a[...]
    out_b[here] = own_b[...]
    out_b[there] = other_b[...]


def share(tp, own, other):
    half, width = own[0].shape
    vmem = pl.BlockSpec(memory_space=pltpu.VMEM)
    return pl.pallas_call(
        share_kernel,
        in_specs=[pl.BlockSpec(memory_space=pltpu.SMEM)] + [vmem] * 4,
        out_specs=[vmem] * 2,
        out_shape=[jax.ShapeDtypeStruct((2 * half, width), value.dtype) for value in own],
        cost_estimate=cost(0, 0),
        compiler_params=pltpu.CompilerParams(vmem_limit_bytes=VMEM),
    )(tp, own[0], other[0], own[1], other[1])


def after(value, *others):
    return lax.optimization_barrier((value,) + others)[0] if others else value


def gather_chunk(payload, index, widths):
    line = [swap(payload, "shard", r << 1) for r in (2, 3, 1)]

    def cross(*gates):
        own = jnp.stack([after(payload, *gates), line[2], line[0], line[1]])
        got = swap(own, "shard", 1)

        def build(*gates):
            full = assemble(after(own, *gates), got, index, widths)
            return [value.reshape(-1, value.shape[2]) for value in full]

        return own, build

    return cross


def adam(weight, first, second, gradient, rate, decay):
    first_new = beta_one * first + (1.0 - beta_one) * gradient
    second_new = beta_two * second + (1.0 - beta_two) * gradient * gradient
    scaled = (
        first_new
        / (1.0 - beta_one**STEP)
        / (jnp.sqrt(second_new / (1.0 - beta_two**STEP)) + adam_eps)
    )
    return (first_new, second_new, weight - rate * (scaled + decay * weight))


def adam_store(weight, first, second, gradient, outs, at):
    for ref, value in zip(outs, adam(weight[at], first[at], second[at], gradient, rate_matrix, weight_decay)):
        ref[at] = value


def adam_heads_kernel(ctx_ref, *refs):
    sums, (wq, mq, vq, wd, md, vd), outs = refs[:-12], refs[-12:-6], refs[-6:]
    mine, other = sums
    lanes = 2 * HD
    pairs = mine.shape[1] // (4 * lanes)
    first = ctx_ref[0] == 0
    for pair in range(pairs):
        for plane in range(4):
            cols = slice((4 * pair + plane) * lanes, (4 * pair + plane + 1) * lanes)
            left, right = mine[:, cols], other[:, cols]
            for group, total in enumerate((jnp.where(first, left, right), jnp.where(first, right, left))):
                start = (group * pairs + pair) * lanes
                place = slice(start, start + lanes)
                if plane < 3:
                    adam_store(wq, mq, vq, total, outs[:3], (plane, slice(None), place))
                else:
                    adam_store(wd, md, vd, total.T, outs[3:], (place, slice(None)))


def adam_fc_kernel(ctx_ref, *refs):
    sums, (w1, m1, v1, w2, m2, v2), outs = refs[:-12], refs[-12:-6], refs[-6:]
    chunks = len(sums) // 2
    cut = w1.shape[1] // (2 * chunks)
    tile = 128
    first = ctx_ref[0] == 0
    for chunk in range(chunks):
        mine, other = sums[2 * chunk : 2 * chunk + 2]
        for at in range(0, 2 * cut, tile):
            left, right = mine[:, at : at + tile], other[:, at : at + tile]
            for group, total in enumerate((jnp.where(first, left, right), jnp.where(first, right, left))):
                start = (group * chunks + chunk) * cut + at % cut
                place = slice(start, start + tile)
                if at < cut:
                    adam_store(w1, m1, v1, total, outs[:3], (slice(None), place))
                else:
                    adam_store(w2, m2, v2, total.T, outs[3:], (place, slice(None)))


def adam_matrices(kernel, ctx, sums, states):
    vmem = pl.BlockSpec(memory_space=pltpu.VMEM)
    return pl.pallas_call(
        kernel,
        in_specs=[pl.BlockSpec(memory_space=pltpu.SMEM)] + [vmem] * (len(sums) + 6),
        out_specs=[vmem] * 6,
        out_shape=[jax.ShapeDtypeStruct(value.shape, f32) for value in states],
        cost_estimate=cost(0, 0),
        compiler_params=pltpu.CompilerParams(vmem_limit_bytes=VMEM),
    )(ctx, *sums, *states)


def rope_tables(length, lanes):
    half = ROT // 2
    lane = jnp.arange(lanes, dtype=jnp.int32) % HD
    frequency = rope_base ** (-((lane % half).astype(f32) * 2.0) / ROT)
    angle = jnp.arange(length, dtype=f32)[:, None] * frequency[None, :]
    cosine, sine = jnp.cos(angle), jnp.sin(angle)
    return [
        jnp.where(lane < ROT, cosine, 1.0),
        jnp.where(lane < half, -sine, 0.0),
        jnp.where((lane >= half) & (lane < ROT), sine, 0.0),
    ]


def body(
    inputs, cotangent, w_qkv, m_qkv, v_qkv, w_dense, m_dense, v_dense,
    w_fc1, m_fc1, v_fc1, w_fc2, m_fc2, v_fc2, vectors, m_vectors, v_vectors,
):
    shard = lax.axis_index("shard")
    ctx = lax.axis_index("ctx")
    tp = lax.axis_index("tp")
    shards = lax.axis_size("shard")
    tok_count, width = inputs.shape
    rows = w_qkv.shape[1]
    head_cols = w_qkv.shape[2]
    units = w_fc1.shape[1]
    lanes = 2 * HD
    pairs, chunks = head_cols // (2 * lanes), 2
    own_heads, own_units = head_cols // 2, units // 2
    cut = own_units // chunks
    fc1_rows = FF // D
    count = vectors.shape[0]
    custom = shards == 8
    ctx_ref = ctx.reshape(1).astype(jnp.int32)
    shard_ref = shard.reshape(1).astype(jnp.int32)

    tp_ref = tp.reshape(1).astype(jnp.int32)
    column_ref, line_ref = shard_ref % 2, shard_ref // 2

    def gather(payload, widths):
        if custom:
            return gather_chunk(payload, shard_ref, widths)
        full = lax.all_gather(payload, "shard", axis=0, tiled=True)
        cuts = [sum(widths[:at]) for at in range(len(widths) + 1)]
        return lambda *gates: (full, lambda *gates: [full[:, a:b] for a, b in zip(cuts, cuts[1:])])

    def local_grads(first, rights):
        if custom:
            return grads(column_ref, first, all_back, rights)
        parts = [dot((first, all_back)[at % 2], right, TN) for at, right in enumerate(rights)]
        both = jnp.concatenate(parts, axis=1).astype(bf16)
        return both, both

    def step_across(kept, sent):
        if custom:
            crossed = swap(sent, "shard", 1)
            return combine(line_ref, kept, crossed)
        total = lax.psum_scatter(sent, "shard", scatter_dimension=0, tiled=True).astype(f32)
        return [total]

    def step_along(parts):
        total = parts[0]
        for r, part in zip((2, 3, 1), parts[1:]):
            total = total + swap(part, "shard", r << 1).astype(f32)
        return total

    def exchange_owned(totals, *gates):
        return [(value, swap(after(value, *gates), "ctx", 1)) for value in totals]

    with jax.named_scope("tokens"):
        part = tok_count // 2
        halves = [pick(value.reshape(2, part, width), tp, 0) for value in (inputs, cotangent)]

    with jax.named_scope("gather_params"):
        low_qkv = pick(w_qkv.reshape(3, rows, 2, pairs, lanes), ctx, 2).astype(bf16)
        low_qkv = jnp.transpose(low_qkv, (1, 2, 0, 3)).reshape(rows, pairs * 3 * lanes)
        low_dense = pick(w_dense.reshape(2, own_heads, rows), ctx, 0).astype(bf16).T
        low_fc1 = pick(w_fc1.reshape(rows, 2, own_units), ctx, 1).astype(bf16)
        low_fc2 = pick(w_fc2.reshape(2, own_units, rows), ctx, 0).astype(bf16).T
        low_vectors = jnp.pad(vectors.astype(bf16).T, ((0, 0), (0, 128 - count)))
        payload = jnp.concatenate([low_qkv, low_dense, low_vectors], axis=1)
        own, build = gather(payload, (pairs * 3 * lanes, pairs * lanes, 128))()
    with jax.named_scope("tokens"):
        direct = [swap(halves[0], "ctx", 1)]
        direct.append(swap(after(halves[1], own), "ctx", 1))
        shared_rows = [swap(direct[0], "tp", 1)]

        def whole_sequence(value, at):
            mine, other = direct[at], shared_rows[at]
            return jnp.concatenate(
                [value, jnp.where(tp == 0, mine, other), jnp.where(tp == 0, other, mine)], axis=0
            )

        all_tokens = whole_sequence(inputs, 0)
        tokens = all_tokens.astype(f32)
        centre = tokens - jnp.mean(tokens, axis=-1, keepdims=True)
        inverse = lax.rsqrt(jnp.mean(centre * centre, axis=-1, keepdims=True) + norm_eps)
        shared_rows.append(swap(after(direct[1], inverse), "tp", 1))
        all_back = whole_sequence(cotangent, 1)

    with jax.named_scope("gather_params"):
        full_qkv, full_dense, full_vectors = build()
        payloads = [
            jnp.concatenate([low_fc1[:, c * cut : (c + 1) * cut], low_fc2[:, c * cut : (c + 1) * cut]], axis=1)
            for c in range(chunks)
        ]

    vec_rows = full_vectors[:, :count].T.astype(f32)
    bias_qkv = lax.dynamic_slice_in_dim(vec_rows[0:3], tp * head_cols + ctx * own_heads, own_heads, 1)
    bias_qkv = jnp.swapaxes(bias_qkv.reshape(3, pairs, lanes), 0, 1).reshape(1, -1)
    bias_dense = vec_rows[3]
    bias_fc1 = lax.dynamic_slice_in_dim(
        vec_rows[4 : 4 + fc1_rows].reshape(1, -1), tp * units + ctx * own_units, own_units, 1
    )
    bias_fc2 = vec_rows[4 + fc1_rows]
    gain_one = vec_rows[5 + fc1_rows]
    shift_one = vec_rows[6 + fc1_rows]
    gain_two = vec_rows[7 + fc1_rows]
    shift_two = vec_rows[8 + fc1_rows]

    with jax.named_scope("norm"):
        unit = centre * inverse
        normed_one = (unit * gain_one + shift_one).astype(bf16)
        normed_two = (unit * gain_two + shift_two).astype(bf16)

    tables = rope_tables(2 * tok_count, lanes)
    with jax.named_scope("project"):
        heads = (dot(normed_one, full_qkv, NN) + bias_qkv).astype(bf16)
        heads_back = dot(all_back, full_dense, NN).astype(bf16)

    with jax.named_scope("gather_params"):
        cross_0 = gather(after(payloads[0], own, heads_back), (cut, cut))

    def run_mlp(chunk, build, *gates):
        with jax.named_scope("mlp"):
            up, down = build(*gates)
            full_fc1.append(up)
            full_fc2.append(down)
            return mlp(
                normed_two, all_back, up, down,
                bias_fc1[:, chunk * cut : (chunk + 1) * cut],
            )

    def run_heads(pair, *gates):
        with jax.named_scope("attend"):
            return attend(ctx_ref, heads, after(heads_back, *gates), tables, pair)

    norm_sums, head_lines = [], []

    def run_finish(theirs, keep, *gates):
        with jax.named_scope("finish"):
            rowwise = [d_heads[0], d_heads[1], attended[0], attended[1]]
            rowwise += [act[0], act[1], d_hidden[0], d_hidden[1], all_tokens]
            weights = [full_qkv, full_dense] + full_fc1 + full_fc2
            gains = after(jnp.stack([gain_one, gain_two]), *gates)
            out, norm_sum, head_line = finish(tp_ref, rowwise, weights, gains, theirs, keep)
            norm_sums.append(norm_sum)
            head_lines.append(head_line)
            return out

    d_heads, attended, act, d_hidden, lines_fc1 = [], [], [], [], []
    full_fc1, full_fc2 = [], []

    def keep_heads(results):
        d_heads.append(results[0])
        attended.append(results[1])

    def keep_mlp(results):
        act.append(results[0])
        d_hidden.append(results[1])
        lines_fc1.append(results[2])

    keep_heads(run_heads(0))
    with jax.named_scope("gather_params"):
        own_0, build_0 = cross_0(attended[0])
        cross_1 = gather(after(payloads[1], own_0), (cut, cut))
    keep_heads(run_heads(1, own_0))
    with jax.named_scope("gather_params"):
        own_1, build_1 = cross_1(attended[1])
    keep_mlp(run_mlp(0, build_0, own_1))
    with jax.named_scope("grad_fc"):
        kept_0, sent_0 = local_grads(normed_two, [d_hidden[0], act[0]])
    with jax.named_scope("grad_heads"):
        kept_h, sent_h = local_grads(
            normed_one, [d_heads[0], attended[0], d_heads[1], after(attended[1], sent_0)]
        )
    keep_mlp(run_mlp(1, build_1, sent_h))
    with jax.named_scope("sum_fc"):
        parts_0 = step_across(after(kept_0, act[1]), sent_0)
    theirs_sent = run_finish(True, False, *parts_0)
    with jax.named_scope("finish"):
        theirs_got = swap(theirs_sent, "tp", 1)
    theirs_kept = run_finish(True, True, theirs_sent)
    with jax.named_scope("sum_fc"):
        total_0 = step_along([after(parts_0[0], theirs_kept)] + list(parts_0[1:]))
        (sums_0,) = exchange_owned([total_0])
    with jax.named_scope("sum_heads"):
        parts_h = step_across(after(kept_h, total_0), sent_h)
    with jax.named_scope("finish"):
        theirs_kept = after(theirs_kept, *parts_h)
        low_theirs = [(theirs_kept[at] + theirs_got[at].astype(f32)).astype(bf16) for at in range(2)]
        from_ctx = [swap(value, "ctx", 1) for value in low_theirs]
    with jax.named_scope("grad_fc"):
        kept_1, sent_1 = local_grads(normed_two, [d_hidden[1], after(act[1], *low_theirs)])
    with jax.named_scope("sum_heads"):
        mine_sent = run_finish(False, False, sent_1, sums_0[1])
        total_h = step_along([after(parts_h[0], mine_sent)] + list(parts_h[1:]))
    with jax.named_scope("finish"):
        mine_got = swap(mine_sent, "tp", 1)
    with jax.named_scope("sum_fc"):
        parts_1 = step_across(after(kept_1, mine_sent, from_ctx[0], total_h), sent_1)
    mine_kept = run_finish(False, True, mine_sent, *parts_1)
    with jax.named_scope("sum_fc"):
        (sums_h,) = exchange_owned([total_h], mine_kept)
        total_1 = step_along([after(parts_1[0], mine_kept)] + list(parts_1[1:]))
        (sums_1,) = exchange_owned([total_1])
    heads_states = (w_qkv, m_qkv, v_qkv, w_dense, m_dense, v_dense)
    fc_states = (w_fc1, m_fc1, v_fc1, w_fc2, m_fc2, v_fc2)

    with jax.named_scope("finish"):
        norm_rows = sum(norm_sums)
        head_line = sum(head_lines)
        out_sum, d_unit = [
            mine_kept[at] + mine_got[at].astype(f32) + after(from_ctx[at], *gates).astype(f32)
            for at, gates in ((0, ()), (1, (total_1,)))
        ]

        own_tokens, own_back = [after(half, attended[0]).astype(f32) for half in halves]
        outputs = (own_tokens + out_sum + bias_dense + bias_fc2).astype(bf16)
        centre = own_tokens - jnp.mean(own_tokens, axis=-1, keepdims=True)
        inverse = lax.rsqrt(jnp.mean(centre * centre, axis=-1, keepdims=True) + norm_eps)
        unit = centre * inverse
        mean_d = jnp.mean(d_unit, axis=-1, keepdims=True)
        mean_du = jnp.mean(d_unit * unit, axis=-1, keepdims=True)
        input_grad = own_back + inverse * (d_unit - mean_d - unit * mean_du)
        halves = [outputs, input_grad]
        outputs, input_grad = share(tp_ref, halves, [swap(value, "tp", 1) for value in halves])

    if custom:
        with jax.named_scope("adam"):
            heads_results = adam_matrices(adam_heads_kernel, ctx_ref, list(sums_h), heads_states)

    with jax.named_scope("vector_grads"):
        bias_back = jnp.sum(own_back, axis=0)[None]
        head_rows = jnp.swapaxes(head_line.reshape(pairs, 3, lanes), 0, 1).reshape(3, own_heads)
        placed_heads = lax.dynamic_update_slice_in_dim(
            jnp.zeros((3, width), f32), head_rows, tp * head_cols + ctx * own_heads, 1
        )
        placed_fc1 = lax.dynamic_update_slice_in_dim(
            jnp.zeros((1, FF), f32),
            jnp.concatenate(lines_fc1, axis=1),
            tp * units + ctx * own_units,
            1,
        ).reshape(fc1_rows, width)
        vector_grads = jnp.concatenate(
            [placed_heads, bias_back, placed_fc1, bias_back, norm_rows], axis=0
        )
        vector_grads = after(vector_grads, total_1)
        if custom:
            for axis, mask in (("tp", 1), ("shard", 1), ("shard", 2), ("shard", 4), ("ctx", 1)):
                got = swap(vector_grads, axis, mask)
                if mask == 2:
                    got = after(got, outputs)
                if mask == 4:
                    got = after(got, heads_results[0])
                vector_grads = vector_grads + got
        else:
            vector_grads = lax.psum(vector_grads, ("shard", "ctx", "tp"))
        owned_vectors = lax.dynamic_slice_in_dim(vector_grads, shard * rows, rows, 1)

    results = [outputs, input_grad]
    head_sums = list(sums_h)
    fc_sums = [*sums_0, *sums_1]
    with jax.named_scope("adam"):
        if custom:
            fc_results = adam_matrices(adam_fc_kernel, ctx_ref, fc_sums, fc_states)
            results += list(heads_results) + list(fc_results)
        else:

            def by_ctx(sums):
                mine, other = jnp.stack(sums[0::2]).astype(f32), jnp.stack(sums[1::2]).astype(f32)
                return jnp.stack([jnp.where(ctx == 0, mine, other), jnp.where(ctx == 0, other, mine)])

            owned = by_ctx(head_sums).reshape(2, rows, pairs, 4, lanes)
            owned = jnp.transpose(owned, (3, 1, 0, 2, 4)).reshape(4, rows, head_cols)
            owned_fc = by_ctx(fc_sums).reshape(2, chunks, rows, 2, cut)
            owned_fc = jnp.transpose(owned_fc, (3, 2, 0, 1, 4)).reshape(2, rows, units)
            for gradient, entry in (
                (owned[:3], heads_states[:3]),
                (owned[3].T, heads_states[3:]),
                (owned_fc[0], fc_states[:3]),
                (owned_fc[1].T, fc_states[3:]),
            ):
                results += adam(*entry, gradient, rate_matrix, weight_decay)
        results += adam(vectors, m_vectors, v_vectors, owned_vectors, rate_vector, 0.0)
    return tuple(results)


def solution(mesh):
    tokens = P(("shard", "ctx"), None)
    layouts = [P(None, "shard", "tp"), P("tp", "shard"), P("shard", "tp"), P("tp", "shard"), P(None, "shard")]
    params = tuple(layout for layout in layouts for _ in range(3))
    return jax.shard_map(
        body,
        mesh=mesh,
        in_specs=(tokens, tokens) + params,
        out_specs=(tokens, tokens) + params,
        check_vma=False,
    )
```
